32 devices in a mesh: row: 8 (over z, y), col: 4 (over x, core).
Axes of the slice: x: 2, y: 2, z: 4, core: 2. Of those that a mesh axis runs over, the one named last changes fastest.
Arguments:
- pairs: float32 [6400, 6400], P('row', 'col'), may hold values from -6 to 6
- one_body: float32 [80, 80], replicated, may hold values from -0.625 to 0.625
- aux: float32 [80, 80, 512], P('row', 'col'), may hold values from -1 to 1, as said below
- weights: float32 [512], replicated, may hold values from 0.3 to 3
Outputs:
- propagated: float32 [6400, 6400], P('row', 'col')
The draws below stay inside these ranges and needn't reach their ends.
Inputs may be any that keep to these rules, and one draw needn't show every extreme that they name: aux[p, q, a] equals aux[q, p, a].
All inputs are finite; a program needn't handle non-finite values.
Results may differ from the reference program's by a relative error of at most 0.0001.
Values sent between devices are 32-bit elements; how exact they have to be, the bound alone decides.
No kernel may reach another device: no remote copies, remote signals or barrier semaphores. Data moves between devices by JAX's collectives and lax.ppermute only.
A program may use at most 192 MiB of HBM per device.

```python
import math
import jax
import jax.numpy as jnp
from jax import lax

N = 80
NAUX = 512
ITERS = 1
PAIRS = 6400


def draw_aux(key, part):
    scale = (NAUX * N * N) ** (-0.25)
    first = jax.random.fold_in(jax.random.fold_in(key, 7), 0)
    values = jnp.clip(jax.random.normal(first, (N, N, NAUX), jnp.float32), -4.0, 4.0)
    values = (values + jnp.transpose(values, (1, 0, 2))) * (scale / 1.4142135)
    values = jnp.clip(values, -1.0, 1.0)
    return values.astype(jnp.float32)


def block_levels(stream_key, shape, pieces, smallest, high):
    gain, own = 1.0, jax.random.fold_in(stream_key, 6)
    for dim, parts in pieces:
        heights = jnp.exp(jax.random.uniform(jax.random.fold_in(own, dim), (parts,), jnp.float32, smallest / len(pieces), high / len(pieces)))
        gain = gain * jnp.repeat(heights, shape[dim] // parts).reshape([-1 if axis == dim else 1 for axis in range(len(shape))])
    return gain


def gaussian(stream_key, shape, width, most, pieces=(), held_as=jnp.bfloat16):
    level = block_levels(stream_key, shape, pieces, -0.22, 0.18) if pieces else 1.0
    array = jax.random.normal(stream_key, shape, jnp.float32) * width * level
    return jnp.minimum(jnp.maximum(array, -most), most).astype(held_as)


def setup_inputs(seed: int = 0) -> dict:
    key_of = jax.random.split(jax.random.key(seed), 5)
    pairs = gaussian(key_of[0], (PAIRS, PAIRS), 1.0, 6.0, ((0, 8), (1, 4)), jnp.float32)
    one_body = gaussian(key_of[1], (N, N), N ** -0.5, 0.625, (), jnp.float32)
    aux = draw_aux(jax.random.fold_in(key_of[4], 71), 0)
    weights = jnp.clip(jnp.exp(jax.random.uniform(key_of[3], (NAUX,), jnp.float32, math.log(0.3), math.log(3.0))), 0.3, 3.0)
    return dict(pairs=pairs, one_body=one_body, aux=aux, weights=weights)


time_step = 0.15
highest = lax.Precision.HIGHEST


def derivative(field, one_body, aux, weights):
    result = jnp.einsum('im,mjkl->ijkl', one_body, field, precision=highest)
    result = result + jnp.einsum('jm,imkl->ijkl', one_body, field, precision=highest)
    result = result - jnp.einsum('ijml,mk->ijkl', field, one_body, precision=highest)
    result = result - jnp.einsum('ijkm,ml->ijkl', field, one_body, precision=highest)
    first_proj = jnp.einsum('ila,ijkl->jka', aux, field, precision=highest) * weights
    second_proj = jnp.einsum('ijkl,jka->ila', field, aux, precision=highest) * weights
    result = result + jnp.einsum('ila,jka->ijkl', aux, first_proj, precision=highest)
    result = result - jnp.einsum('ila,jka->ijkl', second_proj, aux, precision=highest)
    return result


def reference(pairs, one_body, aux, weights):
    field = pairs.reshape(N, N, N, N)
    for step in range(ITERS):
        first = derivative(field, one_body, aux, weights)
        trial = field + time_step * first
        second = derivative(trial, one_body, aux, weights)
        field = field + (time_step / 2.0) * (first + second)
    return field.reshape(N * N, N * N)
```

```python
import functools

import jax
import jax.numpy as jnp
from jax import lax
from jax.experimental import pallas as pl
from jax.experimental.pallas import tpu as pltpu
from jax.sharding import PartitionSpec as P

time_step = 0.15
vmem_limit = 60 * 1024 * 1024
f32, bf16 = jnp.float32, jnp.bfloat16


def halves(x):
    high = x.astype(bf16)
    return high, (x - high.astype(f32)).astype(bf16)


def dot(a, b):
    return lax.dot_general(a, b, (((1,), (0,)), ((), ())), preferred_element_type=f32)


def dot3(a, b):
    return dot(a[0], b[0]) + dot(a[0], b[1]) + dot(a[1], b[0])


def stacked(x):
    high, low = halves(x)
    return jnp.concatenate([high, high, low], axis=0)


def call(body, out_shape, scratch=(), flops=0, moved=0):
    return pl.pallas_call(
        body,
        out_shape=out_shape,
        scratch_shapes=list(scratch),
        compiler_params=pltpu.CompilerParams(vmem_limit_bytes=vmem_limit),
        cost_estimate=pl.CostEstimate(flops=flops, bytes_accessed=moved, transcendentals=0),
    )


def regroup_body(n, x_ref, crossed_ref, turned_ref):
    for i in range(x_ref.shape[0] // n):
        for k in range(x_ref.shape[1] // n):
            a, b = slice(i * n, (i + 1) * n), slice(k * n, (k + 1) * n)
            block = x_ref[a, b]
            crossed_ref[b, a] = block
            turned_ref[a, b] = block.T


def turn_body(x_ref, out_ref):
    rows = x_ref.shape[0]
    for start in range(0, rows, 128):
        stop = min(start + 128, rows)
        out_ref[:, start:stop] = x_ref[start:stop, :].T


def finish_body(n, x_ref, crossed_ref, turned_ref, out_ref):
    for i in range(x_ref.shape[0] // n):
        for k in range(x_ref.shape[1] // n):
            a, b = slice(i * n, (i + 1) * n), slice(k * n, (k + 1) * n)
            out_ref[a, b] = x_ref[a, b] + crossed_ref[b, a] + turned_ref[a, b].T


def split_body(x_ref, high_ref, low_ref):
    high_ref[...], low_ref[...] = halves(x_ref[...])


def take(ref, rows, batch):
    tiles = [ref[t, rows, : min(128, batch - 128 * t)] for t in range(ref.shape[0])]
    return jnp.concatenate(tiles, axis=1) if len(tiles) > 1 else tiles[0]


def put(ref, rows, value):
    for t in range(ref.shape[0]):
        part = value[:, 128 * t : 128 * (t + 1)]
        ref[t, rows, : part.shape[1]] = part


def project(source_ref, high_ref, low_ref, weights_ref):
    blocks, batch, width = source_ref.shape

    def step(r, total):
        rows = pl.ds(pl.multiple_of(r * width, 16), width)
        return total + dot3(halves(source_ref[r]), (high_ref[rows, :], low_ref[rows, :]))

    total = lax.fori_loop(0, blocks, step, jnp.zeros((batch, high_ref.shape[1]), f32))
    return halves((total * weights_ref[...]).T)


def major_term(n, source_ref, major_ref, out_ref):
    def step(q, carry):
        for tile in range(source_ref.shape[0]):
            at = (tile, pl.ds(q, n, stride=n), slice(None))
            out_ref[at] = dot(major_ref[...], stacked(source_ref[at]))
        return carry

    lax.fori_loop(0, n, step, 0)


def block_result(n, r, width, source_ref, term_ref, high_ref, low_ref, minor_ref, proj):
    batch = proj[0].shape[1]
    rows = pl.ds(pl.multiple_of(r * width, 16), width)
    cycle = dot3((high_ref[rows, :], low_ref[rows, :]), proj)
    minor = []
    for p in range(width // n):
        at = pl.ds(pl.multiple_of(r * width + p * n, 16), n)
        minor.append(dot(minor_ref[...], stacked(take(source_ref, at, batch))))
    return cycle + jnp.concatenate(minor, axis=0) + take(term_ref, rows, batch)


def spread(source_ref, out_ref):
    blocks, batch, width = source_ref.shape

    def step(r, carry):
        rows = pl.ds(pl.multiple_of(r * width, 16), width)
        put(out_ref, rows, source_ref[r].T)
        return carry

    lax.fori_loop(0, blocks, step, 0)


def twice_body(n, x_ref, high_ref, low_ref, weights_ref, major_ref, minor_ref, z_ref, s_ref, xp, zp):
    blocks, batch, width = x_ref.shape
    spread(x_ref, xp)
    proj = project(x_ref, high_ref, low_ref, weights_ref)
    major_term(n, xp, major_ref, zp)

    def first(r, carry):
        rows = pl.ds(pl.multiple_of(r * width, 16), width)
        result = block_result(n, r, width, xp, zp, high_ref, low_ref, minor_ref, proj)
        put(zp, rows, result)
        z_ref[r] = result.T
        return carry

    lax.fori_loop(0, blocks, first, 0)
    proj2 = project(z_ref, high_ref, low_ref, weights_ref)
    major_term(n, zp, major_ref, xp)

    def second(r, carry):
        result = block_result(n, r, width, zp, xp, high_ref, low_ref, minor_ref, proj2)
        s_ref[r] = time_step * z_ref[r] + (time_step * time_step / 2.0) * result.T
        return carry

    lax.fori_loop(0, blocks, second, 0)


def once_body(n, keep, scale, x_ref, high_ref, low_ref, weights_ref, major_ref, minor_ref, out_ref, xp, zp):
    blocks, batch, width = x_ref.shape
    spread(x_ref, xp)
    proj = project(x_ref, high_ref, low_ref, weights_ref)
    major_term(n, xp, major_ref, zp)

    def step(r, carry):
        result = block_result(n, r, width, xp, zp, high_ref, low_ref, minor_ref, proj)
        out_ref[r] = scale * result.T + (keep * x_ref[r] if keep else 0.0)
        return carry

    lax.fori_loop(0, blocks, step, 0)


def added_body(n, x_ref, z_ref, *refs):
    blocks = x_ref.shape[0]
    *rest, total = refs

    def step(r, carry):
        total[r] = x_ref[r] + (time_step * time_step) * z_ref[r]
        return carry

    lax.fori_loop(0, blocks, step, 0)
    once_body(n, 0.0, 1.0, total, *rest)


def tripled(matrix):
    high = lax.reduce_precision(matrix, 8, 7)
    low = matrix - high
    return jnp.concatenate([high, low, high], axis=1).astype(bf16)


def exchange(x, axis):
    return lax.all_to_all(x, axis, split_axis=0, concat_axis=0, tiled=True)


def shards(rows, cols, pairs, one_body, aux, weights):
    n = one_body.shape[0]
    naux = aux.shape[2]
    local_rows, local_cols = pairs.shape
    size = local_rows * local_cols

    whole = lax.all_gather(aux, "row", axis=0, tiled=True)
    whole = lax.all_gather(whole, "col", axis=1, tiled=True).reshape(n * n, naux)
    steps = n // 10 if n % 10 == 0 else 1
    tile = n * n // steps
    shape = jax.ShapeDtypeStruct((n * n, naux), bf16)
    high, low = pl.pallas_call(
        split_body,
        grid=(steps,),
        in_specs=[pl.BlockSpec((tile, naux), lambda s: (s, 0))],
        out_specs=[pl.BlockSpec((tile, naux), lambda s: (s, 0))] * 2,
        out_shape=[shape, shape],
        compiler_params=pltpu.CompilerParams(vmem_limit_bytes=vmem_limit),
        cost_estimate=pl.CostEstimate(
            flops=2 * n * n * naux, bytes_accessed=8 * n * n * naux, transcendentals=0
        ),
    )(whole)

    left = tripled(one_body)
    right = tripled(-one_body.T)
    gain = weights.reshape(1, naux)

    crossed, turned = call(
        functools.partial(regroup_body, n),
        [
            jax.ShapeDtypeStruct((local_cols, local_rows), f32),
            jax.ShapeDtypeStruct((local_rows, local_cols), f32),
        ],
        moved=12 * size,
    )(pairs)

    def operator(body, arrays, plus, major, minor, outs, extra=()):
        blocks, batch, width = arrays[0].shape
        shape = jax.ShapeDtypeStruct((blocks, batch, width), f32)
        work = pltpu.VMEM((-(-batch // 128), n * n, 128), f32)
        return call(
            functools.partial(body, n),
            [shape] * outs if outs > 1 else shape,
            [work, work, *extra],
            flops=outs * (12 * n * n * naux * batch + 12 * n * n * n * batch),
            moved=4 * n * n * naux + 4 * size * (len(arrays) + outs),
        )(*arrays, high, low, plus, major, minor)

    mine = exchange(crossed.reshape(rows, local_cols // rows, local_rows), "row")
    first, double = operator(twice_body, [mine], gain, left, right, 2)
    first = exchange(first, "row").reshape(local_cols, local_rows)
    double = exchange(double, "row").reshape(local_cols, local_rows)

    theirs = exchange(turned.reshape(cols, local_rows // cols, local_cols), "col")
    base = operator(
        lambda n, *refs: once_body(n, time_step, time_step * time_step / 2.0, *refs),
        [theirs], -gain, right, left, 1,
    )
    first = call(
        turn_body, jax.ShapeDtypeStruct((local_rows, local_cols), f32), moved=8 * size
    )(first)
    first = exchange(first.reshape(cols, local_rows // cols, local_cols), "col")
    last = operator(
        added_body, [base, first], -gain, right, left, 1, [pltpu.VMEM(base.shape, f32)]
    )
    last = exchange(last, "col").reshape(local_rows, local_cols)

    return call(
        functools.partial(finish_body, n),
        jax.ShapeDtypeStruct(pairs.shape, f32),
        moved=16 * size,
    )(pairs, double, last)


def solution(mesh):
    body = functools.partial(shards, mesh.shape["row"], mesh.shape["col"])
    in_specs = (P("row", "col"), P(), P("row", "col", None), P())
    return jax.shard_map(
        body, mesh=mesh, in_specs=in_specs, out_specs=P("row", "col"), check_vma=False
    )
```

```python
import functools

import jax
import jax.numpy as jnp
from jax import lax
from jax.experimental import pallas as pl
from jax.experimental.pallas import tpu as pltpu
from jax.sharding import PartitionSpec as P

time_step = 0.15
vmem_limit = 60 * 1024 * 1024
f32, bf16 = jnp.float32, jnp.bfloat16


def halves(x):
    high = x.astype(bf16)
    return high, (x - high.astype(f32)).astype(bf16)


def dot(a, b):
    return lax.dot_general(a, b, (((1,), (0,)), ((), ())), preferred_element_type=f32)


def dot3(a, b):
    return dot(a[0], b[0]) + dot(a[0], b[1]) + dot(a[1], b[0])


def stacked(x):
    high, low = halves(x)
    return jnp.concatenate([high, high, low], axis=0)


def call(body, out_shape, operands, scratch=(), flops=0, moved=0):
    vmem, smem = pl.BlockSpec(memory_space=pltpu.VMEM), pl.BlockSpec(memory_space=pltpu.SMEM)
    return pl.pallas_call(
        body,
        in_specs=[smem if x.dtype == jnp.int32 else vmem for x in operands],
        out_specs=jax.tree.map(lambda _: vmem, out_shape),
        out_shape=out_shape,
        scratch_shapes=list(scratch),
        compiler_params=pltpu.CompilerParams(vmem_limit_bytes=vmem_limit),
        cost_estimate=pl.CostEstimate(flops=flops, bytes_accessed=moved, transcendentals=0),
    )(*operands)


def tiles(total, size=128):
    return [slice(start, min(start + size, total)) for start in range(0, total, size)]


def cross_body(n, x_ref, crossed_ref):
    rows = tiles(x_ref.shape[0], n)
    for k in tiles(x_ref.shape[1], n):
        crossed_ref[k, :] = jnp.concatenate([x_ref[i, k] for i in rows], axis=1)


def turn_body(me_ref, x_ref, *refs):
    *outs, stage = refs
    count, batch, _ = stage.shape
    for strip in tiles(x_ref.shape[0]):
        turned = x_ref[strip, :].T
        for b in range(count):
            stage[b, :, strip] = turned[b * batch : (b + 1) * batch]
    hand_out(me_ref, stage, outs)


def hand_out(me_ref, stage, outs):
    for s, out_ref in enumerate(outs):
        out_ref[...] = stage[lax.rem(me_ref[0] + s, len(outs))]


def take_in(me_ref, ins, stage):
    for s, in_ref in enumerate(ins):
        stage[lax.rem(me_ref[0] + len(ins) - s, len(ins))] = in_ref[...]


def finish_body(n, me_ref, x_ref, crossed_ref, *refs):
    *ins, out_ref, stage, total = refs
    take_in(me_ref, ins, stage)
    for strip in tiles(total.shape[0]):
        turned = jnp.concatenate([stage[b, :, strip] for b in range(len(ins))], axis=0)
        total[strip, :] = crossed_ref[strip, :] + turned.T
    cols = tiles(x_ref.shape[1], n)
    for i in tiles(x_ref.shape[0], n):
        out_ref[i, :] = x_ref[i, :] + jnp.concatenate([total[k, i] for k in cols], axis=1)


def split_body(n, x_ref, high_ref, low_ref):
    wide = x_ref.shape[1] * x_ref.shape[0] // n
    each = n // x_ref.shape[0]
    for p in range(wide):
        parts = [x_ref[c, p * each : (p + 1) * each, :] for c in range(x_ref.shape[0])]
        rows = slice(p * n, (p + 1) * n)
        high_ref[rows, :], low_ref[rows, :] = halves(jnp.concatenate(parts, axis=0))


def take(ref, rows, batch):
    parts = [ref[t, rows, : min(128, batch - 128 * t)] for t in range(ref.shape[0])]
    return jnp.concatenate(parts, axis=1) if len(parts) > 1 else parts[0]


def put(ref, rows, value):
    for t in range(ref.shape[0]):
        part = value[:, 128 * t : 128 * (t + 1)]
        ref[t, rows, : part.shape[1]] = part


def apply_operator(
    n, keep, scale, field, target, high_ref, low_ref, weights_ref, major_ref, minor_ref, xp, zp
):
    blocks, batch, width = field.shape

    def span(r):
        return pl.ds(pl.multiple_of(r * width, 16), width)

    def project(r, total):
        x = field[r]
        put(xp, span(r), x.T)
        return total + dot3(halves(x), (high_ref[span(r), :], low_ref[span(r), :]))

    total = jnp.zeros((batch, high_ref.shape[1]), f32)
    total = lax.fori_loop(0, blocks, project, total)
    proj = halves((total * weights_ref[...]).T)

    group = 8 if n % 8 == 0 else 1

    def major(step, carry):
        for g in range(group):
            at = (pl.ds(step * group + g, n, stride=n), slice(None))
            parts = [xp[(t, *at)] for t in range(xp.shape[0])]
            x = jnp.concatenate(parts, axis=1) if len(parts) > 1 else parts[0]
            term = dot(major_ref[...], stacked(x))
            for t in range(xp.shape[0]):
                zp[(t, *at)] = term[:, 128 * t : 128 * (t + 1)]
        return carry

    lax.fori_loop(0, n // group, major, 0)

    def result(r, carry):
        total = dot3((high_ref[span(r), :], low_ref[span(r), :]), proj)
        minor = []
        for p in range(width // n):
            at = pl.ds(pl.multiple_of(r * width + p * n, 16), n)
            minor.append(dot(minor_ref[...], stacked(take(xp, at, batch))))
        total = total + jnp.concatenate(minor, axis=0) + take(zp, span(r), batch)
        if keep:
            target[r] = scale * total.T + keep * field[r]
        else:
            target[r] = scale * total.T
        return carry

    lax.fori_loop(0, blocks, result, 0)


def direct_body(n, keep, scale, x_ref, *refs):
    *consts, out_ref, xp, zp = refs
    apply_operator(n, keep, scale, x_ref, out_ref, *consts, xp, zp)


def arriving_body(n, keep, scale, count, me_ref, *refs):
    ins, (*consts, out_ref, stage, xp, zp) = refs[:count], refs[count:]
    take_in(me_ref, ins, stage)
    apply_operator(n, keep, scale, stage, out_ref, *consts, xp, zp)


def added_body(n, count, me_ref, base_ref, *refs):
    ins, rest = refs[:count], refs[count:]
    consts, outs, (stage, xp, zp) = rest[:-3 - count], rest[-3 - count : -3], rest[-3:]
    for s in range(count):
        b = lax.rem(me_ref[0] + count - s, count)
        stage[b] = base_ref[b] + (time_step * time_step) * ins[s][...]
    apply_operator(n, 0.0, 1.0, stage, stage, *consts, xp, zp)
    hand_out(me_ref, stage, outs)


def tripled(matrix):
    high = lax.reduce_precision(matrix, 8, 7)
    low = matrix - high
    return jnp.concatenate([high, low, high], axis=1).astype(bf16)


def exchange(x, axis):
    return lax.all_to_all(x, axis, split_axis=0, concat_axis=0, tiled=True)


def shift(parts, axis):
    n = len(parts)
    return [parts[0]] + [
        lax.ppermute(parts[s], axis, [(d, (d + s) % n) for d in range(n)]) for s in range(1, n)
    ]


def shards(rows, cols, pairs, one_body, aux, weights):
    n = one_body.shape[0]
    naux = aux.shape[2]
    local_rows, local_cols = pairs.shape
    size = local_rows * local_cols
    me = lax.axis_index("col").astype(jnp.int32).reshape(1)

    crossed = call(
        functools.partial(cross_body, n),
        jax.ShapeDtypeStruct((local_cols, local_rows), f32), [pairs], moved=8 * size,
    )

    whole = lax.all_gather(aux.reshape(-1, naux), "row", axis=0, tiled=True)
    whole = lax.all_gather(whole, "col", axis=0, tiled=False)
    group = 8 if n % 8 == 0 else n
    shape = jax.ShapeDtypeStruct((n * n, naux), bf16)
    high, low = pl.pallas_call(
        functools.partial(split_body, n),
        grid=(n // group,),
        in_specs=[pl.BlockSpec((cols, group * n // cols, naux), lambda s: (0, s, 0))],
        out_specs=[pl.BlockSpec((group * n, naux), lambda s: (s, 0))] * 2,
        out_shape=[shape, shape],
        compiler_params=pltpu.CompilerParams(vmem_limit_bytes=vmem_limit),
        cost_estimate=pl.CostEstimate(
            flops=2 * n * n * naux, bytes_accessed=8 * n * n * naux, transcendentals=0
        ),
    )(whole)

    left = tripled(one_body)
    right = tripled(-one_body.T)
    gain = weights.reshape(1, naux)
    half_square = time_step * time_step / 2.0

    def operator(body, arrays, consts, outs, block, staged):
        blocks, batch, width = block
        work = pltpu.VMEM((-(-batch // 128), n * n, 128), f32)
        return call(
            functools.partial(body, n),
            outs,
            [*arrays, high, low, *consts],
            [pltpu.VMEM(block, f32)] * staged + [work, work],
            flops=12 * n * n * (naux + n) * batch,
            moved=4 * n * n * naux + 12 * size,
        )

    block = (rows, local_cols // rows, local_rows)
    shape = jax.ShapeDtypeStruct(block, f32)
    consts = [gain, left, right]
    mine = exchange(crossed.reshape(block), "row")
    first = operator(
        lambda n, *refs: direct_body(n, 0.0, 1.0, *refs), [mine], consts, shape, block, 0
    )
    double = operator(
        lambda n, *refs: direct_body(n, time_step, half_square, *refs),
        [first], consts, shape, block, 0,
    )
    first = exchange(first, "row").reshape(local_cols, local_rows)
    double = exchange(double, "row").reshape(local_cols, local_rows)

    block = (cols, local_rows // cols, local_cols)
    shape = jax.ShapeDtypeStruct(block, f32)
    parts = [jax.ShapeDtypeStruct(block[1:], f32)] * cols
    consts = [-gain, right, left]
    stage = pltpu.VMEM(block, f32)

    def turn(x):
        return call(turn_body, parts, [me, x], [stage], moved=8 * size)

    theirs = shift(turn(crossed), "col")
    base = operator(
        lambda n, *refs: arriving_body(n, time_step, half_square, cols, *refs),
        [me, *theirs], consts, shape, block, 1,
    )
    first = shift(turn(first), "col")
    last = operator(
        lambda n, *refs: added_body(n, cols, *refs), [me, base, *first], consts, parts, block, 1
    )
    last = shift(last, "col")

    return call(
        functools.partial(finish_body, n),
        jax.ShapeDtypeStruct(pairs.shape, f32),
        [me, pairs, double, *last],
        [stage, pltpu.VMEM((local_cols, local_rows), f32)],
        moved=16 * size,
    )


def solution(mesh):
    body = functools.partial(shards, mesh.shape["row"], mesh.shape["col"])
    in_specs = (P("row", "col"), P(), P("row", "col", None), P())
    return jax.shard_map(
        body, mesh=mesh, in_specs=in_specs, out_specs=P("row", "col"), check_vma=False
    )
```

```python
import functools

import jax
import jax.numpy as jnp
from jax import lax
from jax.experimental import pallas as pl
from jax.experimental.pallas import tpu as pltpu
from jax.sharding import PartitionSpec as P

time_step = 0.15
vmem_limit = 60 * 1024 * 1024
f32, bf16 = jnp.float32, jnp.bfloat16


def halves(x):
    high = x.astype(bf16)
    return high, (x - high.astype(f32)).astype(bf16)


def dot(a, b):
    return lax.dot_general(a, b, (((1,), (0,)), ((), ())), preferred_element_type=f32)


def dot3(a, b):
    return dot(a[0], b[0]) + dot(a[0], b[1]) + dot(a[1], b[0])


def stacked(x):
    high, low = halves(x)
    return jnp.concatenate([high, high, low], axis=0)


def call(body, out_shape, operands, scratch=(), flops=0, moved=0):
    vmem, smem = pl.BlockSpec(memory_space=pltpu.VMEM), pl.BlockSpec(memory_space=pltpu.SMEM)
    return pl.pallas_call(
        body,
        in_specs=[smem if x.dtype == jnp.int32 else vmem for x in operands],
        out_specs=jax.tree.map(lambda _: vmem, out_shape),
        out_shape=out_shape,
        scratch_shapes=list(scratch),
        compiler_params=pltpu.CompilerParams(vmem_limit_bytes=vmem_limit),
        cost_estimate=pl.CostEstimate(flops=flops, bytes_accessed=moved, transcendentals=0),
    )(*operands)


def tiles(total, size=128):
    return [slice(start, min(start + size, total)) for start in range(0, total, size)]


def cross_body(n, x_ref, crossed_ref):
    rows = tiles(x_ref.shape[0], n)
    for k in tiles(x_ref.shape[1], n):
        crossed_ref[k, :] = jnp.concatenate([x_ref[i, k] for i in rows], axis=1)


def turn_body(me_ref, x_ref, *refs):
    *outs, stage = refs
    count, batch, _ = stage.shape
    for strip in tiles(x_ref.shape[0]):
        turned = x_ref[strip, :].T
        for b in range(count):
            stage[b, :, strip] = turned[b * batch : (b + 1) * batch]
    hand_out(me_ref, stage, outs)


def hand_out(me_ref, stage, outs):
    for s, out_ref in enumerate(outs):
        out_ref[...] = stage[lax.rem(me_ref[0] + s, len(outs))]


def take_in(me_ref, ins, stage):
    for s, in_ref in enumerate(ins):
        stage[lax.rem(me_ref[0] + len(ins) - s, len(ins))] = in_ref[...]


def finish_body(n, me_ref, x_ref, crossed_ref, *refs):
    *ins, out_ref, stage, total = refs
    take_in(me_ref, ins, stage)
    for strip in tiles(total.shape[0]):
        turned = jnp.concatenate([stage[b, :, strip] for b in range(len(ins))], axis=0)
        total[strip, :] = crossed_ref[strip, :] + turned.T
    cols = tiles(x_ref.shape[1], n)
    for i in tiles(x_ref.shape[0], n):
        out_ref[i, :] = x_ref[i, :] + jnp.concatenate([total[k, i] for k in cols], axis=1)


def split_body(n, x_ref, high_ref, low_ref):
    wide = x_ref.shape[1] * x_ref.shape[0] // n
    each = n // x_ref.shape[0]
    for p in range(wide):
        parts = [x_ref[c, p * each : (p + 1) * each, :] for c in range(x_ref.shape[0])]
        rows = slice(p * n, (p + 1) * n)
        high_ref[rows, :], low_ref[rows, :] = halves(jnp.concatenate(parts, axis=0))


def take(ref, rows, batch):
    parts = [ref[t, rows, : min(128, batch - 128 * t)] for t in range(ref.shape[0])]
    return jnp.concatenate(parts, axis=1) if len(parts) > 1 else parts[0]


def put(ref, rows, value):
    for t in range(ref.shape[0]):
        part = value[:, 128 * t : 128 * (t + 1)]
        ref[t, rows, : part.shape[1]] = part


def apply_operator(
    n, keep, scale, field, target, high_ref, low_ref, weights_ref, major_ref, minor_ref, xp, zp
):
    blocks, batch, width = field.shape

    def span(r):
        return pl.ds(pl.multiple_of(r * width, 16), width)

    def project(r, total):
        x = field[r]
        put(xp, span(r), x.T)
        return total + dot3(halves(x), (high_ref[span(r), :], low_ref[span(r), :]))

    total = jnp.zeros((batch, high_ref.shape[1]), f32)
    total = lax.fori_loop(0, blocks, project, total)
    proj = halves((total * weights_ref[...]).T)

    group = 8 if n % 8 == 0 else 1

    def major(step, carry):
        for g in range(group):
            at = (pl.ds(step * group + g, n, stride=n), slice(None))
            parts = [xp[(t, *at)] for t in range(xp.shape[0])]
            x = jnp.concatenate(parts, axis=1) if len(parts) > 1 else parts[0]
            term = dot(major_ref[...], stacked(x))
            for t in range(xp.shape[0]):
                zp[(t, *at)] = term[:, 128 * t : 128 * (t + 1)]
        return carry

    lax.fori_loop(0, n // group, major, 0)

    def result(r, carry):
        total = dot3((high_ref[span(r), :], low_ref[span(r), :]), proj)
        minor = []
        for p in range(width // n):
            at = pl.ds(pl.multiple_of(r * width + p * n, 16), n)
            minor.append(dot(minor_ref[...], stacked(take(xp, at, batch))))
        total = total + jnp.concatenate(minor, axis=0) + take(zp, span(r), batch)
        if keep:
            target[r] = scale * total.T + keep * field[r]
        else:
            target[r] = scale * total.T
        return carry

    lax.fori_loop(0, blocks, result, 0)


def direct_body(n, keep, scale, x_ref, *refs):
    *consts, out_ref, xp, zp = refs
    apply_operator(n, keep, scale, x_ref, out_ref, *consts, xp, zp)


def arriving_body(n, keep, scale, count, me_ref, *refs):
    ins, (*consts, out_ref, stage, xp, zp) = refs[:count], refs[count:]
    take_in(me_ref, ins, stage)
    apply_operator(n, keep, scale, stage, out_ref, *consts, xp, zp)


def added_body(n, count, me_ref, base_ref, *refs):
    ins, rest = refs[:count], refs[count:]
    consts, outs, (stage, xp, zp) = rest[:-3 - count], rest[-3 - count : -3], rest[-3:]
    for s in range(count):
        b = lax.rem(me_ref[0] + count - s, count)
        stage[b] = base_ref[b] + (time_step * time_step) * ins[s][...]
    apply_operator(n, 0.0, 1.0, stage, stage, *consts, xp, zp)
    hand_out(me_ref, stage, outs)


def tripled(matrix):
    high = lax.reduce_precision(matrix, 8, 7)
    low = matrix - high
    return jnp.concatenate([high, low, high], axis=1).astype(bf16)


def exchange(x, axis):
    return lax.all_to_all(x, axis, split_axis=0, concat_axis=0, tiled=True)


def shift(parts, axis):
    n = len(parts)
    return [parts[0]] + [
        lax.ppermute(parts[s], axis, [(d, (d + s) % n) for d in range(n)]) for s in range(1, n)
    ]


def shards(rows, cols, pairs, one_body, aux, weights):
    n = one_body.shape[0]
    naux = aux.shape[2]
    local_rows, local_cols = pairs.shape
    size = local_rows * local_cols
    me = lax.axis_index("col").astype(jnp.int32).reshape(1)

    crossed = call(
        functools.partial(cross_body, n),
        jax.ShapeDtypeStruct((local_cols, local_rows), f32), [pairs], moved=8 * size,
    )

    crossed, aux = lax.optimization_barrier((crossed, aux))
    whole = lax.all_gather(aux.reshape(-1, naux), "row", axis=0, tiled=True)
    whole = lax.all_gather(whole, "col", axis=0, tiled=False)
    group = 8 if n % 8 == 0 else n
    shape = jax.ShapeDtypeStruct((n * n, naux), bf16)
    high, low = pl.pallas_call(
        functools.partial(split_body, n),
        grid=(n // group,),
        in_specs=[pl.BlockSpec((cols, group * n // cols, naux), lambda s: (0, s, 0))],
        out_specs=[pl.BlockSpec((group * n, naux), lambda s: (s, 0))] * 2,
        out_shape=[shape, shape],
        compiler_params=pltpu.CompilerParams(vmem_limit_bytes=vmem_limit),
        cost_estimate=pl.CostEstimate(
            flops=2 * n * n * naux, bytes_accessed=8 * n * n * naux, transcendentals=0
        ),
    )(whole)

    left = tripled(one_body)
    right = tripled(-one_body.T)
    gain = weights.reshape(1, naux)
    half_square = time_step * time_step / 2.0

    def operator(body, arrays, consts, outs, block, staged):
        blocks, batch, width = block
        work = pltpu.VMEM((-(-batch // 128), n * n, 128), f32)
        return call(
            functools.partial(body, n),
            outs,
            [*arrays, high, low, *consts],
            [pltpu.VMEM(block, f32)] * staged + [work, work],
            flops=12 * n * n * (naux + n) * batch,
            moved=4 * n * n * naux + 12 * size,
        )

    row_block = (rows, local_cols // rows, local_rows)
    col_block = (cols, local_rows // cols, local_cols)
    row_shape = jax.ShapeDtypeStruct(row_block, f32)
    col_shape = jax.ShapeDtypeStruct(col_block, f32)
    parts = [jax.ShapeDtypeStruct(col_block[1:], f32)] * cols
    row_consts = [gain, left, right]
    col_consts = [-gain, right, left]
    stage = pltpu.VMEM(col_block, f32)

    def turn(x):
        return call(turn_body, parts, [me, x], [stage], moved=8 * size)

    mine = exchange(crossed.reshape(row_block), "row")
    theirs = shift(turn(crossed), "col")
    mine, theirs = lax.optimization_barrier((mine, theirs))
    first = operator(
        lambda n, *refs: direct_body(n, 0.0, 1.0, *refs),
        [mine], row_consts, row_shape, row_block, 0,
    )
    first, theirs = lax.optimization_barrier((first, theirs))
    arriving = exchange(first, "row").reshape(local_cols, local_rows)
    double = operator(
        lambda n, *refs: direct_body(n, time_step, half_square, *refs),
        [first], row_consts, row_shape, row_block, 0,
    )
    base = operator(
        lambda n, *refs: arriving_body(n, time_step, half_square, cols, *refs),
        [me, *theirs], col_consts, col_shape, col_block, 1,
    )
    arriving, base, double = lax.optimization_barrier((arriving, base, double))
    double = exchange(double, "row").reshape(local_cols, local_rows)
    first = shift(turn(arriving), "col")
    last = operator(
        lambda n, *refs: added_body(n, cols, *refs),
        [me, base, *first], col_consts, parts, col_block, 1,
    )
    last = shift(last, "col")

    return call(
        functools.partial(finish_body, n),
        jax.ShapeDtypeStruct(pairs.shape, f32),
        [me, pairs, double, *last],
        [stage, pltpu.VMEM((local_cols, local_rows), f32)],
        moved=16 * size,
    )


def solution(mesh):
    body = functools.partial(shards, mesh.shape["row"], mesh.shape["col"])
    in_specs = (P("row", "col"), P(), P("row", "col", None), P())
    return jax.shard_map(
        body, mesh=mesh, in_specs=in_specs, out_specs=P("row", "col"), check_vma=False
    )
```

```python
import functools

import jax
import jax.numpy as jnp
from jax import lax
from jax.experimental import pallas as pl
from jax.experimental.pallas import tpu as pltpu
from jax.sharding import PartitionSpec as P

time_step = 0.15
vmem_limit = 60 * 1024 * 1024
f32, bf16 = jnp.float32, jnp.bfloat16


def halves(x):
    high = x.astype(bf16)
    return high, (x - high.astype(f32)).astype(bf16)


def dot(a, b):
    return lax.dot_general(a, b, (((1,), (0,)), ((), ())), preferred_element_type=f32)


def dot3(a, b):
    return dot(a[0], b[0]) + dot(a[0], b[1]) + dot(a[1], b[0])


def stacked(x):
    high, low = halves(x)
    return jnp.concatenate([high, high, low], axis=0)


def call(body, out_shape, operands, scratch=(), flops=0, moved=0):
    vmem, smem = pl.BlockSpec(memory_space=pltpu.VMEM), pl.BlockSpec(memory_space=pltpu.SMEM)
    return pl.pallas_call(
        body,
        in_specs=[smem if x.dtype == jnp.int32 else vmem for x in operands],
        out_specs=jax.tree.map(lambda _: vmem, out_shape),
        out_shape=out_shape,
        scratch_shapes=list(scratch),
        compiler_params=pltpu.CompilerParams(vmem_limit_bytes=vmem_limit),
        cost_estimate=pl.CostEstimate(flops=flops, bytes_accessed=moved, transcendentals=0),
    )(*operands)


def tiles(total, size=128):
    return [slice(start, min(start + size, total)) for start in range(0, total, size)]


def folded(batch, width):
    def cost(g):
        return -(-batch // g // 8) * -(-g * width // 128)

    return min([g for g in range(1, batch + 1) if g == 1 or batch % (8 * g) == 0], key=cost)


def wire(block):
    _, batch, width = block
    g = folded(batch, width)
    return jax.ShapeDtypeStruct((batch // g, g * width), f32)


def hand_out(me_ref, stage, outs):
    width = stage.shape[2]
    for s, out_ref in enumerate(outs):
        b, rows = lax.rem(me_ref[0] + s, len(outs)), out_ref.shape[0]
        parts = [
            stage[b, g * rows : (g + 1) * rows, :] for g in range(out_ref.shape[1] // width)
        ]
        out_ref[...] = jnp.concatenate(parts, axis=1) if len(parts) > 1 else parts[0]


def take_in(me_ref, ins, stage):
    width = stage.shape[2]
    for s, in_ref in enumerate(ins):
        b, rows = lax.rem(me_ref[0] + len(ins) - s, len(ins)), in_ref.shape[0]
        for g in range(in_ref.shape[1] // width):
            stage[b, g * rows : (g + 1) * rows, :] = in_ref[:, g * width : (g + 1) * width]


def rows_of(stage, span):
    batch = stage.shape[1]
    parts = []
    for b in range(span.start // batch, -(-span.stop // batch)):
        low, high = max(span.start - b * batch, 0), min(span.stop - b * batch, batch)
        parts.append(stage[b, low:high, :])
    return jnp.concatenate(parts, axis=0) if len(parts) > 1 else parts[0]


def cross_body(n, me_ref, x_ref, crossed_ref, *refs):
    *outs, stage = refs
    rows = tiles(x_ref.shape[0], n)
    for k in tiles(x_ref.shape[1], n):
        crossed_ref[k, :] = jnp.concatenate([x_ref[i, k] for i in rows], axis=1)
    batch = stage.shape[1]
    for b in range(stage.shape[0]):
        stage[b] = crossed_ref[b * batch : (b + 1) * batch, :]
    hand_out(me_ref, stage, outs)


def turn_body(me_ref, x_ref, *refs):
    *outs, stage = refs
    turn_rows(lambda strip: x_ref[strip, :], x_ref.shape[0], stage)
    hand_out(me_ref, stage, outs)


def turn_rows(rows, total, stage):
    count, batch, _ = stage.shape
    for strip in tiles(total):
        turned = rows(strip).T
        for b in range(count):
            stage[b, :, strip] = turned[b * batch : (b + 1) * batch]


def turn_arriving_body(count, row_ref, me_ref, *refs):
    ins, (*outs, arrived, stage) = refs[:count], refs[count:]
    take_in(row_ref, ins, arrived)
    turn_rows(lambda strip: rows_of(arrived, strip), arrived.shape[0] * arrived.shape[1], stage)
    hand_out(me_ref, stage, outs)


def finish_body(n, count, row_ref, me_ref, x_ref, *refs):
    crossed, (*ins, out_ref, arrived, stage, total) = refs[:count], refs[count:]
    take_in(row_ref, crossed, arrived)
    take_in(me_ref, ins, stage)
    for strip in tiles(total.shape[0]):
        turned = jnp.concatenate([stage[b, :, strip] for b in range(len(ins))], axis=0)
        total[strip, :] = rows_of(arrived, strip) + turned.T
    cols = tiles(x_ref.shape[1], n)
    for i in tiles(x_ref.shape[0], n):
        out_ref[i, :] = x_ref[i, :] + jnp.concatenate([total[k, i] for k in cols], axis=1)


def split_body(n, x_ref, high_ref, low_ref):
    wide = x_ref.shape[1] * x_ref.shape[0] // n
    each = n // x_ref.shape[0]
    for p in range(wide):
        parts = [x_ref[c, p * each : (p + 1) * each, :] for c in range(x_ref.shape[0])]
        rows = slice(p * n, (p + 1) * n)
        high_ref[rows, :], low_ref[rows, :] = halves(jnp.concatenate(parts, axis=0))


def take(ref, rows, batch):
    parts = [ref[t, rows, : min(128, batch - 128 * t)] for t in range(ref.shape[0])]
    return jnp.concatenate(parts, axis=1) if len(parts) > 1 else parts[0]


def put(ref, rows, value):
    for t in range(ref.shape[0]):
        part = value[:, 128 * t : 128 * (t + 1)]
        ref[t, rows, : part.shape[1]] = part


def apply_operator(
    n, keep, scale, field, target, high_ref, low_ref, weights_ref, major_ref, minor_ref, xp, zp
):
    blocks, batch, width = field.shape

    def span(r):
        return pl.ds(pl.multiple_of(r * width, 16), width)

    def project(r, total):
        x = field[r]
        put(xp, span(r), x.T)
        return total + dot3(halves(x), (high_ref[span(r), :], low_ref[span(r), :]))

    total = jnp.zeros((batch, high_ref.shape[1]), f32)
    total = lax.fori_loop(0, blocks, project, total)
    proj = halves((total * weights_ref[...]).T)

    group = 8 if n % 8 == 0 else 1

    def major(step, carry):
        for g in range(group):
            at = (pl.ds(step * group + g, n, stride=n), slice(None))
            parts = [xp[(t, *at)] for t in range(xp.shape[0])]
            x = jnp.concatenate(parts, axis=1) if len(parts) > 1 else parts[0]
            term = dot(major_ref[...], stacked(x))
            for t in range(xp.shape[0]):
                zp[(t, *at)] = term[:, 128 * t : 128 * (t + 1)]
        return carry

    lax.fori_loop(0, n // group, major, 0)

    def result(r, carry):
        total = dot3((high_ref[span(r), :], low_ref[span(r), :]), proj)
        minor = []
        for p in range(width // n):
            at = pl.ds(pl.multiple_of(r * width + p * n, 16), n)
            minor.append(dot(minor_ref[...], stacked(take(xp, at, batch))))
        total = total + jnp.concatenate(minor, axis=0) + take(zp, span(r), batch)
        if keep:
            target[r] = scale * total.T + keep * field[r]
        else:
            target[r] = scale * total.T
        return carry

    lax.fori_loop(0, blocks, result, 0)


def leaving_body(n, keep, scale, count, me_ref, x_ref, *refs):
    *consts, stage, xp, zp = refs
    consts, outs = consts[:-count], consts[-count:]
    apply_operator(n, keep, scale, x_ref, stage, *consts, xp, zp)
    hand_out(me_ref, stage, outs)


def arriving_body(n, keep, scale, count, me_ref, *refs):
    ins, (*consts, stage, xp, zp) = refs[:count], refs[count:]
    consts, (out_ref, *outs) = consts[:5], consts[5:]
    take_in(me_ref, ins, stage)
    apply_operator(n, keep, scale, stage, out_ref, *consts, xp, zp)
    hand_out(me_ref, out_ref, outs)


def added_body(n, count, me_ref, base_ref, *refs):
    ins, rest = refs[:count], refs[count:]
    consts, outs, (stage, xp, zp) = rest[:-3 - count], rest[-3 - count : -3], rest[-3:]
    take_in(me_ref, ins, stage)
    for b in range(count):
        stage[b] = base_ref[b] + (time_step * time_step) * stage[b]
    apply_operator(n, 0.0, 1.0, stage, stage, *consts, xp, zp)
    hand_out(me_ref, stage, outs)


def tripled(matrix):
    high = lax.reduce_precision(matrix, 8, 7)
    low = matrix - high
    return jnp.concatenate([high, low, high], axis=1).astype(bf16)


def shift(parts, axis):
    n = len(parts)
    return [parts[0]] + [
        lax.ppermute(parts[s], axis, [(d, (d + s) % n) for d in range(n)]) for s in range(1, n)
    ]


def shards(rows, cols, pairs, one_body, aux, weights):
    n = one_body.shape[0]
    naux = aux.shape[2]
    local_rows, local_cols = pairs.shape
    size = local_rows * local_cols
    row_me, col_me = (lax.axis_index(a).astype(jnp.int32).reshape(1) for a in ("row", "col"))

    row_block = (rows, local_cols // rows, local_rows)
    col_block = (cols, local_rows // cols, local_cols)
    row_wires, col_wires = [wire(row_block)] * rows, [wire(col_block)] * cols
    row_shape = jax.ShapeDtypeStruct(row_block, f32)
    col_shape = jax.ShapeDtypeStruct(col_block, f32)
    row_stage, col_stage = pltpu.VMEM(row_block, f32), pltpu.VMEM(col_block, f32)

    crossed, *mine = call(
        functools.partial(cross_body, n),
        [jax.ShapeDtypeStruct((local_cols, local_rows), f32), *row_wires],
        [row_me, pairs], [row_stage], moved=12 * size,
    )
    theirs = call(turn_body, col_wires, [col_me, crossed], [col_stage], moved=8 * size)

    mine[0], aux = lax.optimization_barrier((mine[0], aux))
    whole = lax.all_gather(aux.reshape(-1, naux), "row", axis=0, tiled=True)
    mine, theirs = shift(mine, "row"), shift(theirs, "col")
    early = rows // 2 + 1
    whole, mine[:early], theirs = lax.optimization_barrier((whole, mine[:early], theirs))
    whole = lax.all_gather(whole, "col", axis=0, tiled=False)
    group = 8 if n % 8 == 0 else n
    shape = jax.ShapeDtypeStruct((n * n, naux), bf16)
    high, low = pl.pallas_call(
        functools.partial(split_body, n),
        grid=(n // group,),
        in_specs=[pl.BlockSpec((cols, group * n // cols, naux), lambda s: (0, s, 0))],
        out_specs=[pl.BlockSpec((group * n, naux), lambda s: (s, 0))] * 2,
        out_shape=[shape, shape],
        compiler_params=pltpu.CompilerParams(vmem_limit_bytes=vmem_limit),
        cost_estimate=pl.CostEstimate(
            flops=2 * n * n * naux, bytes_accessed=8 * n * n * naux, transcendentals=0
        ),
    )(whole)

    left = tripled(one_body)
    right = tripled(-one_body.T)
    gain = weights.reshape(1, naux)
    half_square = time_step * time_step / 2.0

    def operator(body, arrays, consts, outs, block):
        blocks, batch, width = block
        work = pltpu.VMEM((-(-batch // 128), n * n, 128), f32)
        return call(
            functools.partial(body, n),
            outs,
            [*arrays, high, low, *consts],
            [pltpu.VMEM(block, f32), work, work],
            flops=12 * n * n * (naux + n) * batch,
            moved=4 * n * n * naux + 12 * size,
        )

    row_consts = [gain, left, right]
    col_consts = [-gain, right, left]

    first, *arriving = operator(
        lambda n, *refs: arriving_body(n, 0.0, 1.0, rows, *refs),
        [row_me, *mine], row_consts, [row_shape, *row_wires], row_block,
    )
    first, theirs = lax.optimization_barrier((first, theirs))
    arriving = shift(arriving, "row")
    double = operator(
        lambda n, *refs: leaving_body(n, time_step, half_square, rows, *refs),
        [row_me, first], row_consts, row_wires, row_block,
    )
    (base,) = operator(
        lambda n, *refs: arriving_body(n, time_step, half_square, cols, *refs),
        [col_me, *theirs], col_consts, [col_shape], col_block,
    )
    arriving, base, double = lax.optimization_barrier((arriving, base, double))
    double = shift(double, "row")
    first = call(
        functools.partial(turn_arriving_body, rows),
        col_wires, [row_me, col_me, *arriving], [row_stage, col_stage], moved=8 * size,
    )
    first = shift(first, "col")
    last = operator(
        lambda n, *refs: added_body(n, cols, *refs),
        [col_me, base, *first], col_consts, col_wires, col_block,
    )
    last = shift(last, "col")

    return call(
        functools.partial(finish_body, n, rows),
        jax.ShapeDtypeStruct(pairs.shape, f32),
        [row_me, col_me, pairs, *double, *last],
        [row_stage, col_stage, pltpu.VMEM((local_cols, local_rows), f32)],
        moved=16 * size,
    )


def solution(mesh):
    body = functools.partial(shards, mesh.shape["row"], mesh.shape["col"])
    in_specs = (P("row", "col"), P(), P("row", "col", None), P())
    return jax.shard_map(
        body, mesh=mesh, in_specs=in_specs, out_specs=P("row", "col"), check_vma=False
    )
```

```python
import functools

import jax
import jax.numpy as jnp
from jax import lax
from jax.experimental import pallas as pl
from jax.experimental.pallas import tpu as pltpu
from jax.sharding import PartitionSpec as P

time_step = 0.15
vmem_limit = 60 * 1024 * 1024
f32, bf16 = jnp.float32, jnp.bfloat16


def halves(x):
    high = x.astype(bf16)
    return high, (x - high.astype(f32)).astype(bf16)


def dot(a, b):
    return lax.dot_general(a, b, (((1,), (0,)), ((), ())), preferred_element_type=f32)


def dot3(a, b):
    return dot(a[0], b[0]) + dot(a[0], b[1]) + dot(a[1], b[0])


def stacked(x):
    high, low = halves(x)
    return jnp.concatenate([high, high, low], axis=0)


def call(body, out_shape, operands, scratch=(), flops=0, moved=0):
    vmem, smem = pl.BlockSpec(memory_space=pltpu.VMEM), pl.BlockSpec(memory_space=pltpu.SMEM)
    return pl.pallas_call(
        body,
        in_specs=[smem if x.dtype == jnp.int32 else vmem for x in operands],
        out_specs=jax.tree.map(lambda _: vmem, out_shape),
        out_shape=out_shape,
        scratch_shapes=list(scratch),
        compiler_params=pltpu.CompilerParams(vmem_limit_bytes=vmem_limit),
        cost_estimate=pl.CostEstimate(flops=flops, bytes_accessed=moved, transcendentals=0),
    )(*operands)


def tiles(total, size=128):
    return [slice(start, min(start + size, total)) for start in range(0, total, size)]


def folded(batch, width):
    def cost(g):
        return -(-batch // g // 8) * -(-g * width // 128)

    return min([g for g in range(1, batch + 1) if g == 1 or batch % (8 * g) == 0], key=cost)


def wire(block):
    _, batch, width = block
    g = folded(batch, width)
    return jax.ShapeDtypeStruct((batch // g, g * width), f32)


def fold(stage, b, out_ref):
    width, rows = stage.shape[2], out_ref.shape[0]
    parts = [stage[b, g * rows : (g + 1) * rows, :] for g in range(out_ref.shape[1] // width)]
    out_ref[...] = jnp.concatenate(parts, axis=1) if len(parts) > 1 else parts[0]


def unfold(in_ref, stage, b):
    width, rows = stage.shape[2], in_ref.shape[0]
    for g in range(in_ref.shape[1] // width):
        stage[b, g * rows : (g + 1) * rows, :] = in_ref[:, g * width : (g + 1) * width]


def hand_out(me_ref, stage, outs):
    for s, out_ref in enumerate(outs):
        fold(stage, lax.rem(me_ref[0] + s, len(outs)), out_ref)


def take_in(me_ref, ins, stage):
    for s, in_ref in enumerate(ins):
        unfold(in_ref, stage, lax.rem(me_ref[0] + len(ins) - s, len(ins)))


def rows_of(stage, span):
    batch = stage.shape[1]
    parts = []
    for b in range(span.start // batch, -(-span.stop // batch)):
        low, high = max(span.start - b * batch, 0), min(span.stop - b * batch, batch)
        parts.append(stage[b, low:high, :])
    return jnp.concatenate(parts, axis=0) if len(parts) > 1 else parts[0]


def cross_body(n, me_ref, x_ref, crossed_ref, *refs):
    *outs, stage = refs
    rows = tiles(x_ref.shape[0], n)
    for k in tiles(x_ref.shape[1], n):
        crossed_ref[k, :] = jnp.concatenate([x_ref[i, k] for i in rows], axis=1)
    batch = stage.shape[1]
    for b in range(stage.shape[0]):
        stage[b] = crossed_ref[b * batch : (b + 1) * batch, :]
    hand_out(me_ref, stage, outs)


def turn_body(me_ref, x_ref, *refs):
    *outs, stage = refs
    turn_rows(lambda strip: x_ref[strip, :], x_ref.shape[0], stage)
    hand_out(me_ref, stage, outs)


def turn_rows(rows, total, stage):
    count, batch, _ = stage.shape
    for strip in tiles(total):
        turned = rows(strip).T
        for b in range(count):
            stage[b, :, strip] = turned[b * batch : (b + 1) * batch]


def turn_arriving_body(count, row_ref, me_ref, *refs):
    ins, (*outs, arrived, stage) = refs[:count], refs[count:]
    take_in(row_ref, ins, arrived)
    turn_rows(lambda strip: rows_of(arrived, strip), arrived.shape[0] * arrived.shape[1], stage)
    hand_out(me_ref, stage, outs)


def finish_body(n, me_ref, x_ref, crossed_ref, *refs):
    *ins, out_ref, arrived, stage, total = refs
    for b in range(arrived.shape[0]):
        unfold(crossed_ref.at[b], arrived, b)
    take_in(me_ref, ins, stage)
    for strip in tiles(total.shape[0]):
        turned = jnp.concatenate([stage[b, :, strip] for b in range(len(ins))], axis=0)
        total[strip, :] = rows_of(arrived, strip) + turned.T
    cols = tiles(x_ref.shape[1], n)
    for i in tiles(x_ref.shape[0], n):
        out_ref[i, :] = x_ref[i, :] + jnp.concatenate([total[k, i] for k in cols], axis=1)


def split_body(n, places, row_ref, col_ref, *refs):
    *ins, high_ref, low_ref, stage = refs
    cols, rows, each, _ = stage.shape
    pieces = len(ins) // cols
    for index, in_ref in enumerate(ins):
        c = lax.bitwise_xor(col_ref[0], places[index // pieces])
        for u in range(rows // pieces):
            s = index % pieces * (rows // pieces) + u
            r = lax.rem(row_ref[0] + rows - s, rows)
            stage[c, r] = in_ref[u]
    wide = n // cols
    for p in range(n):
        r, at = p * wide // each, p * wide % each
        parts = [stage[c, r, at : at + wide, :] for c in range(cols)]
        span = slice(p * n, (p + 1) * n)
        high_ref[span, :], low_ref[span, :] = halves(jnp.concatenate(parts, axis=0))


def take(ref, rows, batch):
    parts = [ref[t, rows, : min(128, batch - 128 * t)] for t in range(ref.shape[0])]
    return jnp.concatenate(parts, axis=1) if len(parts) > 1 else parts[0]


def put(ref, rows, value):
    for t in range(ref.shape[0]):
        part = value[:, 128 * t : 128 * (t + 1)]
        ref[t, rows, : part.shape[1]] = part


def apply_operator(
    n, keep, scale, field, target, high_ref, low_ref, weights_ref, major_ref, minor_ref, xp, zp
):
    blocks, batch, width = field.shape

    def span(r):
        return pl.ds(pl.multiple_of(r * width, 16), width)

    def project(r, total):
        x = field[r]
        put(xp, span(r), x.T)
        return total + dot3(halves(x), (high_ref[span(r), :], low_ref[span(r), :]))

    total = jnp.zeros((batch, high_ref.shape[1]), f32)
    total = lax.fori_loop(0, blocks, project, total)
    proj = halves((total * weights_ref[...]).T)

    group = 8 if n % 8 == 0 else 1

    def major(step, carry):
        for g in range(group):
            at = (pl.ds(step * group + g, n, stride=n), slice(None))
            parts = [xp[(t, *at)] for t in range(xp.shape[0])]
            x = jnp.concatenate(parts, axis=1) if len(parts) > 1 else parts[0]
            term = dot(major_ref[...], stacked(x))
            for t in range(xp.shape[0]):
                zp[(t, *at)] = term[:, 128 * t : 128 * (t + 1)]
        return carry

    lax.fori_loop(0, n // group, major, 0)

    def result(r, carry):
        total = dot3((high_ref[span(r), :], low_ref[span(r), :]), proj)
        minor = []
        for p in range(width // n):
            at = pl.ds(pl.multiple_of(r * width + p * n, 16), n)
            minor.append(dot(minor_ref[...], stacked(take(xp, at, batch))))
        total = total + jnp.concatenate(minor, axis=0) + take(zp, span(r), batch)
        if keep:
            target[r] = scale * total.T + keep * field[r]
        else:
            target[r] = scale * total.T
        return carry

    lax.fori_loop(0, blocks, result, 0)


def leaving_body(n, keep, scale, x_ref, *refs):
    *consts, out_ref, stage, xp, zp = refs
    apply_operator(n, keep, scale, x_ref, stage, *consts, xp, zp)
    for b in range(stage.shape[0]):
        fold(stage, b, out_ref.at[b])


def arriving_body(n, keep, scale, count, me_ref, *refs):
    ins, (*consts, stage, xp, zp) = refs[:count], refs[count:]
    consts, (out_ref, *outs) = consts[:5], consts[5:]
    take_in(me_ref, ins, stage)
    apply_operator(n, keep, scale, stage, out_ref, *consts, xp, zp)
    hand_out(me_ref, out_ref, outs)


def added_body(n, count, me_ref, base_ref, *refs):
    ins, rest = refs[:count], refs[count:]
    consts, outs, (stage, xp, zp) = rest[:-3 - count], rest[-3 - count : -3], rest[-3:]
    take_in(me_ref, ins, stage)
    for b in range(count):
        stage[b] = base_ref[b] + (time_step * time_step) * stage[b]
    apply_operator(n, 0.0, 1.0, stage, stage, *consts, xp, zp)
    hand_out(me_ref, stage, outs)


def tripled(matrix):
    high = lax.reduce_precision(matrix, 8, 7)
    low = matrix - high
    return jnp.concatenate([high, low, high], axis=1).astype(bf16)


def shift(parts, axis):
    n = len(parts)
    return [parts[0]] + [
        lax.ppermute(parts[s], axis, [(d, (d + s) % n) for d in range(n)]) for s in range(1, n)
    ]


def swap(x, axis, n, bit):
    return lax.ppermute(x, axis, [(d, d ^ bit) for d in range(n)])


def shards(rows, cols, pairs, one_body, aux, weights):
    n = one_body.shape[0]
    naux = aux.shape[2]
    local_rows, local_cols = pairs.shape
    size = local_rows * local_cols
    row_me, col_me = (lax.axis_index(a).astype(jnp.int32).reshape(1) for a in ("row", "col"))

    row_block = (rows, local_cols // rows, local_rows)
    col_block = (cols, local_rows // cols, local_cols)
    row_wires, col_wires = [wire(row_block)] * rows, [wire(col_block)] * cols
    row_shape = jax.ShapeDtypeStruct(row_block, f32)
    col_shape = jax.ShapeDtypeStruct(col_block, f32)
    row_stage, col_stage = pltpu.VMEM(row_block, f32), pltpu.VMEM(col_block, f32)

    crossed, *mine = call(
        functools.partial(cross_body, n),
        [jax.ShapeDtypeStruct((local_cols, local_rows), f32), *row_wires],
        [row_me, pairs], [row_stage], moved=12 * size,
    )

    vectors = shift([aux.reshape(-1, naux)] * rows, "row")
    mine = shift(mine, "row")
    early = rows // 2
    near, far = jnp.stack(vectors[:early]), vectors[early:]
    far, mine[1:early] = lax.optimization_barrier((far, mine[1:early]))
    held = {0: [near, jnp.stack(far)]}
    bit = cols // 2
    while bit:
        for t in list(held):
            held[t ^ bit] = [swap(x, "col", cols, bit) for x in held[t]]
        if bit == cols // 2:
            crossed, held[bit] = lax.optimization_barrier((crossed, held[bit]))
        bit //= 2
    theirs = call(turn_body, col_wires, [col_me, crossed], [col_stage], moved=8 * size)
    theirs = shift(theirs, "col")
    places = list(held)
    shape = jax.ShapeDtypeStruct((n * n, naux), bf16)
    high, low = call(
        functools.partial(split_body, n, places),
        [shape, shape],
        [row_me, col_me, *[x for t in places for x in held[t]]],
        [pltpu.VMEM((cols, rows, n * n // cols // rows, naux), f32)],
        flops=2 * n * n * naux, moved=8 * n * n * naux,
    )

    left = tripled(one_body)
    right = tripled(-one_body.T)
    gain = weights.reshape(1, naux)
    half_square = time_step * time_step / 2.0

    def operator(body, arrays, consts, outs, block):
        blocks, batch, width = block
        work = pltpu.VMEM((-(-batch // 128), n * n, 128), f32)
        return call(
            functools.partial(body, n),
            outs,
            [*arrays, high, low, *consts],
            [pltpu.VMEM(block, f32), work, work],
            flops=12 * n * n * (naux + n) * batch,
            moved=4 * n * n * naux + 12 * size,
        )

    row_consts = [gain, left, right]
    col_consts = [-gain, right, left]

    first, *arriving = operator(
        lambda n, *refs: arriving_body(n, 0.0, 1.0, rows, *refs),
        [row_me, *mine], row_consts, [row_shape, *row_wires], row_block,
    )
    first, theirs = lax.optimization_barrier((first, theirs))
    arriving = shift(arriving, "row")
    double = operator(
        lambda n, *refs: leaving_body(n, time_step, half_square, *refs),
        [first], row_consts, jax.ShapeDtypeStruct((rows, *row_wires[0].shape), f32), row_block,
    )
    (base,) = operator(
        lambda n, *refs: arriving_body(n, time_step, half_square, cols, *refs),
        [col_me, *theirs], col_consts, [col_shape], col_block,
    )
    arriving, base, double = lax.optimization_barrier((arriving, base, double))
    double = lax.all_to_all(double, "row", split_axis=0, concat_axis=0, tiled=True)
    first = call(
        functools.partial(turn_arriving_body, rows),
        col_wires, [row_me, col_me, *arriving], [row_stage, col_stage], moved=8 * size,
    )
    first = shift(first, "col")
    last = operator(
        lambda n, *refs: added_body(n, cols, *refs),
        [col_me, base, *first], col_consts, col_wires, col_block,
    )
    last = shift(last, "col")

    return call(
        functools.partial(finish_body, n),
        jax.ShapeDtypeStruct(pairs.shape, f32),
        [col_me, pairs, double, *last],
        [row_stage, col_stage, pltpu.VMEM((local_cols, local_rows), f32)],
        moved=16 * size,
    )


def solution(mesh):
    body = functools.partial(shards, mesh.shape["row"], mesh.shape["col"])
    in_specs = (P("row", "col"), P(), P("row", "col", None), P())
    return jax.shard_map(
        body, mesh=mesh, in_specs=in_specs, out_specs=P("row", "col"), check_vma=False
    )
```

```python
import functools

import jax
import jax.numpy as jnp
from jax import lax
from jax.experimental import pallas as pl
from jax.experimental.pallas import tpu as pltpu
from jax.sharding import PartitionSpec as P

time_step = 0.15
vmem_limit = 60 * 1024 * 1024
f32, bf16 = jnp.float32, jnp.bfloat16


def halves(x):
    high = x.astype(bf16)
    return high, (x - high.astype(f32)).astype(bf16)


def dot(a, b):
    return lax.dot_general(a, b, (((1,), (0,)), ((), ())), preferred_element_type=f32)


def dot3(a, b):
    return dot(a[0], b[0]) + dot(a[0], b[1]) + dot(a[1], b[0])


def stacked(x):
    high, low = halves(x)
    return jnp.concatenate([high, high, low], axis=0)


def call(body, out_shape, operands, scratch=(), flops=0, moved=0):
    vmem, smem = pl.BlockSpec(memory_space=pltpu.VMEM), pl.BlockSpec(memory_space=pltpu.SMEM)
    return pl.pallas_call(
        body,
        in_specs=[smem if x.dtype == jnp.int32 else vmem for x in operands],
        out_specs=jax.tree.map(lambda _: vmem, out_shape),
        out_shape=out_shape,
        scratch_shapes=list(scratch),
        compiler_params=pltpu.CompilerParams(vmem_limit_bytes=vmem_limit),
        cost_estimate=pl.CostEstimate(flops=flops, bytes_accessed=moved, transcendentals=0),
    )(*operands)


def tiles(total, size=128):
    return [slice(start, min(start + size, total)) for start in range(0, total, size)]


def folded(batch, width):
    def cost(g):
        return -(-batch // g // 8) * -(-g * width // 128)

    return min([g for g in range(1, batch + 1) if g == 1 or batch % (8 * g) == 0], key=cost)


def wire(batch, width):
    g = folded(batch, width)
    return (batch // g, g * width)


def fold(block, shape):
    rows, g = shape[0], shape[1] // block.shape[1]
    parts = [block[h * rows : (h + 1) * rows, :] for h in range(g)]
    return jnp.concatenate(parts, axis=1) if g > 1 else block


def unfold(in_ref, width):
    parts = [in_ref[:, h * width : (h + 1) * width] for h in range(in_ref.shape[1] // width)]
    return jnp.concatenate(parts, axis=0) if len(parts) > 1 else parts[0]


def halved(batch):
    cut = -(-batch // 16) * 8
    return [(0, cut), (cut, batch)] if cut < batch else [(0, batch)]


def hand_out(me_ref, stage, outs):
    for s, out_ref in enumerate(outs):
        out_ref[...] = fold(stage[lax.rem(me_ref[0] + s, len(outs))], out_ref.shape)


def take_in(me_ref, ins, stage):
    for s, in_ref in enumerate(ins):
        stage[lax.rem(me_ref[0] + len(ins) - s, len(ins))] = unfold(in_ref, stage.shape[2])


def rows_of(stage, span):
    batch = stage.shape[1]
    parts = []
    for b in range(span.start // batch, -(-span.stop // batch)):
        low, high = max(span.start - b * batch, 0), min(span.stop - b * batch, batch)
        parts.append(stage[b, low:high, :])
    return jnp.concatenate(parts, axis=0) if len(parts) > 1 else parts[0]


def cross_body(n, x_ref, crossed_ref, out_ref):
    rows = tiles(x_ref.shape[0], n)
    for k in tiles(x_ref.shape[1], n):
        crossed_ref[k, :] = jnp.concatenate([x_ref[i, k] for i in rows], axis=1)
    count = out_ref.shape[0]
    batch = crossed_ref.shape[0] // count
    for b in range(count):
        block = crossed_ref[b * batch : (b + 1) * batch, :]
        out_ref[b] = fold(block, out_ref.shape[1:])


def turn_body(me_ref, x_ref, *refs):
    *outs, stage = refs
    turn_rows(lambda strip: x_ref[strip, :], x_ref.shape[0], stage)
    hand_out(me_ref, stage, outs)


def turn_rows(rows, total, stage):
    count, batch, _ = stage.shape
    for strip in tiles(total):
        turned = rows(strip).T
        for b in range(count):
            stage[b, :, strip] = turned[b * batch : (b + 1) * batch]


def turn_arriving_body(me_ref, x_ref, *refs):
    *outs, arrived, stage = refs
    for b in range(arrived.shape[0]):
        arrived[b] = unfold(x_ref.at[b], arrived.shape[2])
    turn_rows(lambda strip: rows_of(arrived, strip), arrived.shape[0] * arrived.shape[1], stage)
    hand_out(me_ref, stage, outs)


def finish_body(n, me_ref, x_ref, crossed_ref, *refs):
    *ins, out_ref, arrived, stage, total = refs
    for b in range(arrived.shape[0]):
        arrived[b] = unfold(crossed_ref.at[b], arrived.shape[2])
    take_in(me_ref, ins, stage)
    for strip in tiles(total.shape[0]):
        turned = jnp.concatenate([stage[b, :, strip] for b in range(len(ins))], axis=0)
        total[strip, :] = rows_of(arrived, strip) + turned.T
    cols = tiles(x_ref.shape[1], n)
    for i in tiles(x_ref.shape[0], n):
        out_ref[i, :] = x_ref[i, :] + jnp.concatenate([total[k, i] for k in cols], axis=1)


def split_body(n, x_ref, high_ref, low_ref):
    wide = x_ref.shape[1] * x_ref.shape[0] // n
    each = n // x_ref.shape[0]
    for p in range(wide):
        parts = [x_ref[c, p * each : (p + 1) * each, :] for c in range(x_ref.shape[0])]
        rows = slice(p * n, (p + 1) * n)
        high_ref[rows, :], low_ref[rows, :] = halves(jnp.concatenate(parts, axis=0))


def take(ref, rows, batch):
    parts = [ref[t, rows, : min(128, batch - 128 * t)] for t in range(ref.shape[0])]
    return jnp.concatenate(parts, axis=1) if len(parts) > 1 else parts[0]


def put(ref, rows, value):
    for t in range(ref.shape[0]):
        part = value[:, 128 * t : 128 * (t + 1)]
        ref[t, rows, : part.shape[1]] = part


def apply_operator(
    n, keep, scale, field, target, high_ref, low_ref, weights_ref, major_ref, minor_ref, xp, zp
):
    blocks, batch, width = field.shape

    def span(r):
        return pl.ds(pl.multiple_of(r * width, 16), width)

    def project(r, total):
        x = field[r]
        put(xp, span(r), x.T)
        return total + dot3(halves(x), (high_ref[span(r), :], low_ref[span(r), :]))

    total = jnp.zeros((batch, high_ref.shape[1]), f32)
    total = lax.fori_loop(0, blocks, project, total)
    proj = halves((total * weights_ref[...]).T)

    group = 8 if n % 8 == 0 else 1

    def major(step, carry):
        for g in range(group):
            at = (pl.ds(step * group + g, n, stride=n), slice(None))
            parts = [xp[(t, *at)] for t in range(xp.shape[0])]
            x = jnp.concatenate(parts, axis=1) if len(parts) > 1 else parts[0]
            term = dot(major_ref[...], stacked(x))
            for t in range(xp.shape[0]):
                zp[(t, *at)] = term[:, 128 * t : 128 * (t + 1)]
        return carry

    lax.fori_loop(0, n // group, major, 0)

    def result(r, carry):
        total = dot3((high_ref[span(r), :], low_ref[span(r), :]), proj)
        minor = []
        for p in range(width // n):
            at = pl.ds(pl.multiple_of(r * width + p * n, 16), n)
            minor.append(dot(minor_ref[...], stacked(take(xp, at, batch))))
        total = total + jnp.concatenate(minor, axis=0) + take(zp, span(r), batch)
        if keep:
            target[r] = scale * total.T + keep * field[r]
        else:
            target[r] = scale * total.T
        return carry

    lax.fori_loop(0, blocks, result, 0)


def send_left(spans, stage, outs):
    for b in range(stage.shape[0]):
        for (start, stop), out_ref in zip(spans, outs):
            out_ref[b] = fold(stage[b, start:stop, :], out_ref.shape[1:])


def left_body(n, spans, x_ref, *refs):
    *consts, out_ref = refs[:6]
    outs, (stage, xp, zp) = refs[6 : 6 + len(spans)], refs[6 + len(spans) :]
    for b in range(stage.shape[0]):
        stage[b] = unfold(x_ref.at[b], stage.shape[2])
    apply_operator(n, 0.0, 1.0, stage, out_ref, *consts, xp, zp)
    send_left(spans, out_ref, outs)


def left_again_body(n, x_ref, *refs):
    *consts, out_ref, stage, xp, zp = refs
    apply_operator(n, time_step, time_step * time_step / 2.0, x_ref, stage, *consts, xp, zp)
    send_left([(0, stage.shape[1])], stage, [out_ref])


def right_body(n, count, me_ref, *refs):
    ins, (*consts, out_ref, stage, xp, zp) = refs[:count], refs[count:]
    take_in(me_ref, ins, stage)
    apply_operator(
        n, time_step, time_step * time_step / 2.0, stage, out_ref, *consts, xp, zp
    )


def right_again_body(n, count, rows, spans, me_ref, base_ref, *refs):
    split = count * len(spans)
    ins, consts, outs = refs[:split], refs[split : split + 5], refs[split + 5 : split + 5 + count]
    stage, xp, zp, *arrived = refs[split + 5 + count :]
    for h, part in enumerate(arrived):
        take_in(me_ref, ins[h * count : (h + 1) * count], part)
    sizes = [stop - start for start, stop in spans]
    for b in range(count):
        parts = [
            part[b, :, r * size : (r + 1) * size]
            for r in range(rows)
            for part, size in zip(arrived, sizes)
        ]
        stage[b] = base_ref[b] + (time_step * time_step) * jnp.concatenate(parts, axis=1)
    apply_operator(n, 0.0, 1.0, stage, stage, *consts, xp, zp)
    hand_out(me_ref, stage, outs)


def tripled(matrix):
    high = lax.reduce_precision(matrix, 8, 7)
    low = matrix - high
    return jnp.concatenate([high, low, high], axis=1).astype(bf16)


def shift(parts, axis):
    n = len(parts)
    return [parts[0]] + [
        lax.ppermute(parts[s], axis, [(d, (d + s) % n) for d in range(n)]) for s in range(1, n)
    ]


def exchange(x, axis):
    return lax.all_to_all(x, axis, split_axis=0, concat_axis=0, tiled=True)


def shards(rows, cols, pairs, one_body, aux, weights):
    n = one_body.shape[0]
    naux = aux.shape[2]
    local_rows, local_cols = pairs.shape
    size = local_rows * local_cols
    me = lax.axis_index("col").astype(jnp.int32).reshape(1)

    row_block = (rows, local_cols // rows, local_rows)
    col_block = (cols, local_rows // cols, local_cols)
    spans = halved(row_block[1])

    def row_wire(batch):
        return jax.ShapeDtypeStruct((rows, *wire(batch, local_rows)), f32)

    def col_wires(width):
        return [jax.ShapeDtypeStruct(wire(col_block[1], width), f32)] * cols

    row_stage, col_stage = pltpu.VMEM(row_block, f32), pltpu.VMEM(col_block, f32)

    crossed, mine = call(
        functools.partial(cross_body, n),
        [jax.ShapeDtypeStruct((local_cols, local_rows), f32), row_wire(row_block[1])],
        [pairs], moved=12 * size,
    )

    whole = lax.all_gather(aux.reshape(-1, naux), "row", axis=0, tiled=True)
    whole = lax.all_gather(whole, "col", axis=0, tiled=False)
    mine = exchange(mine, "row")
    whole, crossed = lax.optimization_barrier((whole, crossed))
    theirs = call(turn_body, col_wires(local_cols), [me, crossed], [col_stage], moved=8 * size)
    mine, theirs = lax.optimization_barrier((mine, theirs))
    theirs = shift(theirs, "col")
    group = 8 if n % 8 == 0 else n
    shape = jax.ShapeDtypeStruct((n * n, naux), bf16)
    high, low = pl.pallas_call(
        functools.partial(split_body, n),
        grid=(n // group,),
        in_specs=[pl.BlockSpec((cols, group * n // cols, naux), lambda s: (0, s, 0))],
        out_specs=[pl.BlockSpec((group * n, naux), lambda s: (s, 0))] * 2,
        out_shape=[shape, shape],
        compiler_params=pltpu.CompilerParams(vmem_limit_bytes=vmem_limit),
        cost_estimate=pl.CostEstimate(
            flops=2 * n * n * naux, bytes_accessed=8 * n * n * naux, transcendentals=0
        ),
    )(whole)

    left = tripled(one_body)
    right = tripled(-one_body.T)
    gain = weights.reshape(1, naux)

    def operator(body, arrays, consts, outs, block, scratch=()):
        batch = block[1]
        work = pltpu.VMEM((-(-batch // 128), n * n, 128), f32)
        return call(
            functools.partial(body, n),
            outs,
            [*arrays, high, low, *consts],
            [pltpu.VMEM(block, f32), work, work, *scratch],
            flops=12 * n * n * (naux + n) * batch,
            moved=4 * n * n * naux + 12 * size,
        )

    row_consts = [gain, left, right]
    col_consts = [-gain, right, left]

    first, *parts = operator(
        lambda n, *refs: left_body(n, spans, *refs),
        [mine], row_consts,
        [jax.ShapeDtypeStruct(row_block, f32)] + [row_wire(b - a) for a, b in spans], row_block,
    )
    double = operator(left_again_body, [first], row_consts, row_wire(row_block[1]), row_block)
    double, theirs = lax.optimization_barrier((double, theirs))
    base = operator(
        lambda n, *refs: right_body(n, cols, *refs),
        [me, *theirs], col_consts, jax.ShapeDtypeStruct(col_block, f32), col_block,
    )
    arriving = []
    for h, (start, stop) in enumerate(spans):
        part = exchange(parts[h], "row")
        if h + 1 < len(spans):
            part, parts[h + 1] = lax.optimization_barrier((part, parts[h + 1]))
        else:
            part, double, base = lax.optimization_barrier((part, double, base))
        turned = call(
            turn_arriving_body, col_wires(rows * (stop - start)), [me, part],
            [
                pltpu.VMEM((rows, stop - start, local_rows), f32),
                pltpu.VMEM((*col_block[:2], rows * (stop - start)), f32),
            ],
            moved=8 * size // len(spans),
        )
        arriving += shift(turned, "col")
    double = exchange(double, "row")
    last = operator(
        lambda n, *refs: right_again_body(n, cols, rows, spans, *refs),
        [me, base, *arriving], col_consts, col_wires(local_cols), col_block,
        [pltpu.VMEM((*col_block[:2], rows * (b - a)), f32) for a, b in spans],
    )
    last = shift(last, "col")

    return call(
        functools.partial(finish_body, n),
        jax.ShapeDtypeStruct(pairs.shape, f32),
        [me, pairs, double, *last],
        [row_stage, col_stage, pltpu.VMEM((local_cols, local_rows), f32)],
        moved=16 * size,
    )


def solution(mesh):
    body = functools.partial(shards, mesh.shape["row"], mesh.shape["col"])
    in_specs = (P("row", "col"), P(), P("row", "col", None), P())
    return jax.shard_map(
        body, mesh=mesh, in_specs=in_specs, out_specs=P("row", "col"), check_vma=False
    )
```

```python
import functools

import jax
import jax.numpy as jnp
from jax import lax
from jax.experimental import pallas as pl
from jax.experimental.pallas import tpu as pltpu
from jax.sharding import PartitionSpec as P

time_step = 0.15
vmem_limit = 60 * 1024 * 1024
f32, bf16 = jnp.float32, jnp.bfloat16


def halves(x):
    high = x.astype(bf16)
    return high, (x - high.astype(f32)).astype(bf16)


def dot(a, b):
    return lax.dot_general(a, b, (((1,), (0,)), ((), ())), preferred_element_type=f32)


def dot3(a, b):
    return dot(a[0], b[0]) + dot(a[0], b[1]) + dot(a[1], b[0])


def stacked(x):
    high, low = halves(x)
    return jnp.concatenate([high, high, low], axis=0)


def call(body, out_shape, operands, scratch=(), flops=0, moved=0):
    vmem, smem = pl.BlockSpec(memory_space=pltpu.VMEM), pl.BlockSpec(memory_space=pltpu.SMEM)
    return pl.pallas_call(
        body,
        in_specs=[smem if x.dtype == jnp.int32 else vmem for x in operands],
        out_specs=jax.tree.map(lambda _: vmem, out_shape),
        out_shape=out_shape,
        scratch_shapes=list(scratch),
        compiler_params=pltpu.CompilerParams(vmem_limit_bytes=vmem_limit),
        cost_estimate=pl.CostEstimate(flops=flops, bytes_accessed=moved, transcendentals=0),
    )(*operands)


def tiles(total, size=128):
    return [slice(start, min(start + size, total)) for start in range(0, total, size)]


def folded(batch, width):
    def cost(g):
        return -(-batch // g // 8) * -(-g * width // 128)

    return min([g for g in range(1, batch + 1) if g == 1 or batch % (8 * g) == 0], key=cost)


def wire(batch, width):
    g = folded(batch, width)
    return (batch // g, g * width)


def fold(block, shape):
    rows, g = shape[0], shape[1] // block.shape[1]
    parts = [block[h * rows : (h + 1) * rows, :] for h in range(g)]
    return jnp.concatenate(parts, axis=1) if g > 1 else block


def unfold(in_ref, width):
    parts = [in_ref[:, h * width : (h + 1) * width] for h in range(in_ref.shape[1] // width)]
    return jnp.concatenate(parts, axis=0) if len(parts) > 1 else parts[0]


def halved(batch):
    cut = -(-batch // 16) * 8
    return [(0, cut), (cut, batch)] if cut < batch else [(0, batch)]


def hand_out(me_ref, stage, outs):
    for s, out_ref in enumerate(outs):
        out_ref[...] = fold(stage[lax.rem(me_ref[0] + s, len(outs))], out_ref.shape)


def take_in(me_ref, ins, stage):
    for s, in_ref in enumerate(ins):
        stage[lax.rem(me_ref[0] + len(ins) - s, len(ins))] = unfold(in_ref, stage.shape[2])


def rows_of(stage, span):
    batch = stage.shape[1]
    parts = []
    for b in range(span.start // batch, -(-span.stop // batch)):
        low, high = max(span.start - b * batch, 0), min(span.stop - b * batch, batch)
        parts.append(stage[b, low:high, :])
    return jnp.concatenate(parts, axis=0) if len(parts) > 1 else parts[0]


def cross_body(n, x_ref, crossed_ref, out_ref):
    rows = tiles(x_ref.shape[0], n)
    for k in tiles(x_ref.shape[1], n):
        crossed_ref[k, :] = jnp.concatenate([x_ref[i, k] for i in rows], axis=1)
    count = out_ref.shape[0]
    batch = crossed_ref.shape[0] // count
    for b in range(count):
        block = crossed_ref[b * batch : (b + 1) * batch, :]
        out_ref[b] = fold(block, out_ref.shape[1:])


def turn_body(me_ref, x_ref, *refs):
    *outs, stage = refs
    turn_rows(lambda strip: x_ref[strip, :], x_ref.shape[0], stage)
    hand_out(me_ref, stage, outs)


def turn_rows(rows, total, stage):
    count, batch, _ = stage.shape
    for strip in tiles(total):
        turned = rows(strip).T
        for b in range(count):
            stage[b, :, strip] = turned[b * batch : (b + 1) * batch]


def turn_arriving_body(me_ref, x_ref, *refs):
    *outs, arrived, stage = refs
    for b in range(arrived.shape[0]):
        arrived[b] = unfold(x_ref.at[b], arrived.shape[2])
    turn_rows(lambda strip: rows_of(arrived, strip), arrived.shape[0] * arrived.shape[1], stage)
    hand_out(me_ref, stage, outs)


def finish_body(n, me_ref, x_ref, crossed_ref, *refs):
    *ins, out_ref, arrived, stage, total = refs
    for b in range(arrived.shape[0]):
        arrived[b] = unfold(crossed_ref.at[b], arrived.shape[2])
    take_in(me_ref, ins, stage)
    for strip in tiles(total.shape[0]):
        turned = jnp.concatenate([stage[b, :, strip] for b in range(len(ins))], axis=0)
        total[strip, :] = rows_of(arrived, strip) + turned.T
    cols = tiles(x_ref.shape[1], n)
    for i in tiles(x_ref.shape[0], n):
        out_ref[i, :] = x_ref[i, :] + jnp.concatenate([total[k, i] for k in cols], axis=1)


def split_body(n, x_ref, high_ref, low_ref):
    wide = x_ref.shape[1] * x_ref.shape[0] // n
    each = n // x_ref.shape[0]
    for p in range(wide):
        parts = [x_ref[c, p * each : (p + 1) * each, :] for c in range(x_ref.shape[0])]
        rows = slice(p * n, (p + 1) * n)
        high_ref[rows, :], low_ref[rows, :] = halves(jnp.concatenate(parts, axis=0))


def take(ref, rows, batch):
    parts = [ref[t, rows, : min(128, batch - 128 * t)] for t in range(ref.shape[0])]
    return jnp.concatenate(parts, axis=1) if len(parts) > 1 else parts[0]


def put(ref, rows, value):
    for t in range(ref.shape[0]):
        part = value[:, 128 * t : 128 * (t + 1)]
        ref[t, rows, : part.shape[1]] = part


def apply_operator(
    n, keep, scale, field, target, high_ref, low_ref, weights_ref, major_ref, minor_ref, xp, zp
):
    blocks, batch, width = field.shape

    def span(r):
        return pl.ds(pl.multiple_of(r * width, 16), width)

    def project(r, total):
        x = field[r]
        put(xp, span(r), x.T)
        return total + dot3(halves(x), (high_ref[span(r), :], low_ref[span(r), :]))

    total = jnp.zeros((batch, high_ref.shape[1]), f32)
    total = lax.fori_loop(0, blocks, project, total)
    proj = halves((total * weights_ref[...]).T)

    group = 8 if n % 8 == 0 else 1

    def major(step, carry):
        for g in range(group):
            at = (pl.ds(step * group + g, n, stride=n), slice(None))
            parts = [xp[(t, *at)] for t in range(xp.shape[0])]
            x = jnp.concatenate(parts, axis=1) if len(parts) > 1 else parts[0]
            term = dot(major_ref[...], stacked(x))
            for t in range(xp.shape[0]):
                zp[(t, *at)] = term[:, 128 * t : 128 * (t + 1)]
        return carry

    lax.fori_loop(0, n // group, major, 0)

    def result(r, carry):
        total = dot3((high_ref[span(r), :], low_ref[span(r), :]), proj)
        minor = []
        for p in range(width // n):
            at = pl.ds(pl.multiple_of(r * width + p * n, 16), n)
            minor.append(dot(minor_ref[...], stacked(take(xp, at, batch))))
        total = total + jnp.concatenate(minor, axis=0) + take(zp, span(r), batch)
        if keep:
            target[r] = scale * total.T + keep * field[r]
        else:
            target[r] = scale * total.T
        return carry

    lax.fori_loop(0, blocks, result, 0)


def send_left(spans, stage, outs):
    for b in range(stage.shape[0]):
        for (start, stop), out_ref in zip(spans, outs):
            out_ref[b] = fold(stage[b, start:stop, :], out_ref.shape[1:])


def left_body(n, spans, x_ref, *refs):
    *consts, out_ref = refs[:6]
    outs, (stage, xp, zp) = refs[6 : 6 + len(spans)], refs[6 + len(spans) :]
    for b in range(stage.shape[0]):
        stage[b] = unfold(x_ref.at[b], stage.shape[2])
    apply_operator(n, 0.0, 1.0, stage, out_ref, *consts, xp, zp)
    send_left(spans, out_ref, outs)


def left_again_body(n, x_ref, *refs):
    *consts, out_ref, stage, xp, zp = refs
    apply_operator(n, time_step, time_step * time_step / 2.0, x_ref, stage, *consts, xp, zp)
    send_left([(0, stage.shape[1])], stage, [out_ref])


def right_body(n, count, me_ref, *refs):
    ins, (*consts, out_ref, stage, xp, zp) = refs[:count], refs[count:]
    take_in(me_ref, ins, stage)
    apply_operator(
        n, time_step, time_step * time_step / 2.0, stage, out_ref, *consts, xp, zp
    )


def right_again_body(n, count, rows, spans, me_ref, base_ref, *refs):
    split = count * len(spans)
    ins, consts, outs = refs[:split], refs[split : split + 5], refs[split + 5 : split + 5 + count]
    stage, xp, zp, *arrived = refs[split + 5 + count :]
    for h, part in enumerate(arrived):
        take_in(me_ref, ins[h * count : (h + 1) * count], part)
    sizes = [stop - start for start, stop in spans]
    for b in range(count):
        parts = [
            part[b, :, r * size : (r + 1) * size]
            for r in range(rows)
            for part, size in zip(arrived, sizes)
        ]
        stage[b] = base_ref[b] + (time_step * time_step) * jnp.concatenate(parts, axis=1)
    apply_operator(n, 0.0, 1.0, stage, stage, *consts, xp, zp)
    hand_out(me_ref, stage, outs)


def tripled(matrix):
    high = lax.reduce_precision(matrix, 8, 7)
    low = matrix - high
    return jnp.concatenate([high, low, high], axis=1).astype(bf16)


def shift(parts, axis):
    n = len(parts)
    return [parts[0]] + [
        lax.ppermute(parts[s], axis, [(d, (d + s) % n) for d in range(n)]) for s in range(1, n)
    ]


def after(x, y):
    return lax.optimization_barrier((x, y))[0]


def exchange(x, axis):
    return lax.all_to_all(x, axis, split_axis=0, concat_axis=0, tiled=True)


def shards(rows, cols, pairs, one_body, aux, weights):
    n = one_body.shape[0]
    naux = aux.shape[2]
    local_rows, local_cols = pairs.shape
    size = local_rows * local_cols
    me = lax.axis_index("col").astype(jnp.int32).reshape(1)

    row_block = (rows, local_cols // rows, local_rows)
    col_block = (cols, local_rows // cols, local_cols)
    spans = halved(row_block[1])

    def row_wire(batch):
        return jax.ShapeDtypeStruct((rows, *wire(batch, local_rows)), f32)

    def col_wires(width):
        return [jax.ShapeDtypeStruct(wire(col_block[1], width), f32)] * cols

    row_stage, col_stage = pltpu.VMEM(row_block, f32), pltpu.VMEM(col_block, f32)

    crossed, mine = call(
        functools.partial(cross_body, n),
        [jax.ShapeDtypeStruct((local_cols, local_rows), f32), row_wire(row_block[1])],
        [pairs], moved=12 * size,
    )

    aux = after(aux, mine)
    whole = lax.all_gather(aux.reshape(-1, naux), "row", axis=0, tiled=True)
    whole = lax.all_gather(whole, "col", axis=0, tiled=False)
    mine = exchange(mine, "row")
    turned = call(
        turn_body, col_wires(local_cols), [me, after(crossed, whole)], [col_stage], moved=8 * size
    )
    theirs = shift(turned, "col")
    group = 8 if n % 8 == 0 else n
    shape = jax.ShapeDtypeStruct((n * n, naux), bf16)
    high, low = pl.pallas_call(
        functools.partial(split_body, n),
        grid=(n // group,),
        in_specs=[pl.BlockSpec((cols, group * n // cols, naux), lambda s: (0, s, 0))],
        out_specs=[pl.BlockSpec((group * n, naux), lambda s: (s, 0))] * 2,
        out_shape=[shape, shape],
        compiler_params=pltpu.CompilerParams(vmem_limit_bytes=vmem_limit),
        cost_estimate=pl.CostEstimate(
            flops=2 * n * n * naux, bytes_accessed=8 * n * n * naux, transcendentals=0
        ),
    )(whole)

    left = tripled(one_body)
    right = tripled(-one_body.T)
    gain = weights.reshape(1, naux)

    def operator(body, arrays, consts, outs, block, scratch=()):
        batch = block[1]
        work = pltpu.VMEM((-(-batch // 128), n * n, 128), f32)
        return call(
            functools.partial(body, n),
            outs,
            [*arrays, high, low, *consts],
            [pltpu.VMEM(block, f32), work, work, *scratch],
            flops=12 * n * n * (naux + n) * batch,
            moved=4 * n * n * naux + 12 * size,
        )

    row_consts = [gain, left, right]
    col_consts = [-gain, right, left]

    first, *parts = operator(
        lambda n, *refs: left_body(n, spans, *refs),
        [after(mine, turned)], row_consts,
        [jax.ShapeDtypeStruct(row_block, f32)] + [row_wire(b - a) for a, b in spans], row_block,
    )
    double = operator(left_again_body, [first], row_consts, row_wire(row_block[1]), row_block)
    base = operator(
        lambda n, *refs: right_body(n, cols, *refs),
        [me, *after(theirs, double)], col_consts, jax.ShapeDtypeStruct(col_block, f32), col_block,
    )
    arriving, part = [], double
    for h, (start, stop) in enumerate(spans):
        part = exchange(after(parts[h], (part, double)) if h else parts[h], "row")
        if h + 1 == len(spans):
            double = after(double, part)
            part = after(part, base)
        turned = call(
            turn_arriving_body, col_wires(rows * (stop - start)), [me, part],
            [
                pltpu.VMEM((rows, stop - start, local_rows), f32),
                pltpu.VMEM((*col_block[:2], rows * (stop - start)), f32),
            ],
            moved=8 * size // len(spans),
        )
        arriving += shift(turned, "col")
    double = exchange(double, "row")
    last = operator(
        lambda n, *refs: right_again_body(n, cols, rows, spans, *refs),
        [me, base, *arriving], col_consts, col_wires(local_cols), col_block,
        [pltpu.VMEM((*col_block[:2], rows * (b - a)), f32) for a, b in spans],
    )
    last = shift(last, "col")

    return call(
        functools.partial(finish_body, n),
        jax.ShapeDtypeStruct(pairs.shape, f32),
        [me, pairs, double, *last],
        [row_stage, col_stage, pltpu.VMEM((local_cols, local_rows), f32)],
        moved=16 * size,
    )


def solution(mesh):
    body = functools.partial(shards, mesh.shape["row"], mesh.shape["col"])
    in_specs = (P("row", "col"), P(), P("row", "col", None), P())
    return jax.shard_map(
        body, mesh=mesh, in_specs=in_specs, out_specs=P("row", "col"), check_vma=False
    )
```

```python
import functools

import jax
import jax.numpy as jnp
from jax import lax
from jax.experimental import pallas as pl
from jax.experimental.pallas import tpu as pltpu
from jax.sharding import PartitionSpec as P

time_step = 0.15
vmem_limit = 60 * 1024 * 1024
f32, bf16 = jnp.float32, jnp.bfloat16


def halves(x):
    high = x.astype(bf16)
    return high, (x - high.astype(f32)).astype(bf16)


def dot(a, b):
    return lax.dot_general(a, b, (((1,), (0,)), ((), ())), preferred_element_type=f32)


def dot3(a, b):
    return dot(a[0], b[0]) + dot(a[0], b[1]) + dot(a[1], b[0])


def stacked(x):
    high, low = halves(x)
    return jnp.concatenate([high, high, low], axis=0)


def call(body, out_shape, operands, scratch=(), flops=0, moved=0):
    vmem, smem = pl.BlockSpec(memory_space=pltpu.VMEM), pl.BlockSpec(memory_space=pltpu.SMEM)
    return pl.pallas_call(
        body,
        in_specs=[smem if x.dtype == jnp.int32 else vmem for x in operands],
        out_specs=jax.tree.map(lambda _: vmem, out_shape),
        out_shape=out_shape,
        scratch_shapes=list(scratch),
        compiler_params=pltpu.CompilerParams(vmem_limit_bytes=vmem_limit),
        cost_estimate=pl.CostEstimate(flops=flops, bytes_accessed=moved, transcendentals=0),
    )(*operands)


def tiles(total, size=128):
    return [slice(start, min(start + size, total)) for start in range(0, total, size)]


def folded(batch, width):
    def cost(g):
        return -(-batch // g // 8) * -(-g * width // 128)

    return min([g for g in range(1, batch + 1) if g == 1 or batch % (8 * g) == 0], key=cost)


def wire(batch, width):
    g = folded(batch, width)
    return (batch // g, g * width)


def fold(block, shape):
    rows, g = shape[0], shape[1] // block.shape[1]
    parts = [block[h * rows : (h + 1) * rows, :] for h in range(g)]
    return jnp.concatenate(parts, axis=1) if g > 1 else block


def unfold(in_ref, width):
    parts = [in_ref[:, h * width : (h + 1) * width] for h in range(in_ref.shape[1] // width)]
    return jnp.concatenate(parts, axis=0) if len(parts) > 1 else parts[0]


def halved(batch):
    cut = -(-batch // 16) * 8
    return [(0, cut), (cut, batch)] if cut < batch else [(0, batch)]


def hand_out(me_ref, stage, outs):
    for s, out_ref in enumerate(outs):
        out_ref[...] = fold(stage[lax.rem(me_ref[0] + s, len(outs))], out_ref.shape)


def take_in(me_ref, ins, stage):
    for s, in_ref in enumerate(ins):
        stage[lax.rem(me_ref[0] + len(ins) - s, len(ins))] = unfold(in_ref, stage.shape[2])


def rows_of(stage, span):
    batch = stage.shape[1]
    parts = []
    for b in range(span.start // batch, -(-span.stop // batch)):
        low, high = max(span.start - b * batch, 0), min(span.stop - b * batch, batch)
        parts.append(stage[b, low:high, :])
    return jnp.concatenate(parts, axis=0) if len(parts) > 1 else parts[0]


def cross_body(n, x_ref, crossed_ref, out_ref):
    rows = tiles(x_ref.shape[0], n)
    for k in tiles(x_ref.shape[1], n):
        crossed_ref[k, :] = jnp.concatenate([x_ref[i, k] for i in rows], axis=1)
    count = out_ref.shape[0]
    batch = crossed_ref.shape[0] // count
    for b in range(count):
        block = crossed_ref[b * batch : (b + 1) * batch, :]
        out_ref[b] = fold(block, out_ref.shape[1:])


def turn_body(me_ref, x_ref, *refs):
    *outs, stage = refs
    turn_rows(lambda strip: x_ref[strip, :], x_ref.shape[0], stage)
    hand_out(me_ref, stage, outs)


def turn_rows(rows, total, stage):
    count, batch, _ = stage.shape
    for strip in tiles(total):
        turned = rows(strip).T
        for b in range(count):
            stage[b, :, strip] = turned[b * batch : (b + 1) * batch]


def turn_arriving_body(me_ref, x_ref, *refs):
    *outs, arrived, stage = refs
    for b in range(arrived.shape[0]):
        arrived[b] = unfold(x_ref.at[b], arrived.shape[2])
    turn_rows(lambda strip: rows_of(arrived, strip), arrived.shape[0] * arrived.shape[1], stage)
    hand_out(me_ref, stage, outs)


def finish_body(n, me_ref, x_ref, crossed_ref, *refs):
    *ins, out_ref, arrived, stage, total = refs
    for b in range(arrived.shape[0]):
        arrived[b] = unfold(crossed_ref.at[b], arrived.shape[2])
    take_in(me_ref, ins, stage)
    for strip in tiles(total.shape[0]):
        turned = jnp.concatenate([stage[b, :, strip] for b in range(len(ins))], axis=0)
        total[strip, :] = rows_of(arrived, strip) + turned.T
    cols = tiles(x_ref.shape[1], n)
    for i in tiles(x_ref.shape[0], n):
        out_ref[i, :] = x_ref[i, :] + jnp.concatenate([total[k, i] for k in cols], axis=1)


def split_body(n, x_ref, high_ref, low_ref):
    wide = x_ref.shape[1] * x_ref.shape[0] // n
    each = n // x_ref.shape[0]
    for p in range(wide):
        parts = [x_ref[c, p * each : (p + 1) * each, :] for c in range(x_ref.shape[0])]
        rows = slice(p * n, (p + 1) * n)
        high_ref[rows, :], low_ref[rows, :] = halves(jnp.concatenate(parts, axis=0))


def take(ref, rows, batch):
    parts = [ref[t, rows, : min(128, batch - 128 * t)] for t in range(ref.shape[0])]
    return jnp.concatenate(parts, axis=1) if len(parts) > 1 else parts[0]


def put(ref, rows, value):
    for t in range(ref.shape[0]):
        part = value[:, 128 * t : 128 * (t + 1)]
        ref[t, rows, : part.shape[1]] = part


def apply_operator(
    n, keep, scale, field, target, high_ref, low_ref, weights_ref, major_ref, minor_ref, xp, zp
):
    blocks, batch, width = field.shape

    def span(r):
        return pl.ds(pl.multiple_of(r * width, 16), width)

    def project(r, total):
        x = field[r]
        put(xp, span(r), x.T)
        return total + dot3(halves(x), (high_ref[span(r), :], low_ref[span(r), :]))

    total = jnp.zeros((batch, high_ref.shape[1]), f32)
    total = lax.fori_loop(0, blocks, project, total)
    proj = halves((total * weights_ref[...]).T)

    group = 8 if n % 8 == 0 else 1

    def major(step, carry):
        for g in range(group):
            at = (pl.ds(step * group + g, n, stride=n), slice(None))
            parts = [xp[(t, *at)] for t in range(xp.shape[0])]
            x = jnp.concatenate(parts, axis=1) if len(parts) > 1 else parts[0]
            term = dot(major_ref[...], stacked(x))
            for t in range(xp.shape[0]):
                zp[(t, *at)] = term[:, 128 * t : 128 * (t + 1)]
        return carry

    lax.fori_loop(0, n // group, major, 0)

    def result(r, carry):
        total = dot3((high_ref[span(r), :], low_ref[span(r), :]), proj)
        minor = []
        for p in range(width // n):
            at = pl.ds(pl.multiple_of(r * width + p * n, 16), n)
            minor.append(dot(minor_ref[...], stacked(take(xp, at, batch))))
        total = total + jnp.concatenate(minor, axis=0) + take(zp, span(r), batch)
        if keep:
            target[r] = scale * total.T + keep * field[r]
        else:
            target[r] = scale * total.T
        return carry

    lax.fori_loop(0, blocks, result, 0)


def send_left(spans, stage, outs):
    for b in range(stage.shape[0]):
        for (start, stop), out_ref in zip(spans, outs):
            out_ref[b] = fold(stage[b, start:stop, :], out_ref.shape[1:])


def left_body(n, spans, x_ref, *refs):
    *consts, out_ref = refs[:6]
    outs, (stage, xp, zp) = refs[6 : 6 + len(spans)], refs[6 + len(spans) :]
    for b in range(stage.shape[0]):
        stage[b] = unfold(x_ref.at[b], stage.shape[2])
    apply_operator(n, 0.0, 1.0, stage, out_ref, *consts, xp, zp)
    send_left(spans, out_ref, outs)


def left_again_body(n, x_ref, *refs):
    *consts, out_ref, stage, xp, zp = refs
    apply_operator(n, time_step, time_step * time_step / 2.0, x_ref, stage, *consts, xp, zp)
    send_left([(0, stage.shape[1])], stage, [out_ref])


def right_body(n, count, me_ref, *refs):
    ins, (*consts, out_ref, stage, xp, zp) = refs[:count], refs[count:]
    take_in(me_ref, ins, stage)
    apply_operator(
        n, time_step, time_step * time_step / 2.0, stage, out_ref, *consts, xp, zp
    )


def right_again_body(n, count, rows, spans, me_ref, base_ref, *refs):
    split = count * len(spans)
    ins, consts, outs = refs[:split], refs[split : split + 5], refs[split + 5 : split + 5 + count]
    stage, xp, zp, *arrived = refs[split + 5 + count :]
    for h, part in enumerate(arrived):
        take_in(me_ref, ins[h * count : (h + 1) * count], part)
    sizes = [stop - start for start, stop in spans]
    for b in range(count):
        parts = [
            part[b, :, r * size : (r + 1) * size]
            for r in range(rows)
            for part, size in zip(arrived, sizes)
        ]
        stage[b] = base_ref[b] + (time_step * time_step) * jnp.concatenate(parts, axis=1)
    apply_operator(n, 0.0, 1.0, stage, stage, *consts, xp, zp)
    hand_out(me_ref, stage, outs)


def tripled(matrix):
    high = lax.reduce_precision(matrix, 8, 7)
    low = matrix - high
    return jnp.concatenate([high, low, high], axis=1).astype(bf16)


def shift(parts, axis):
    n = len(parts)
    return [parts[0]] + [
        lax.ppermute(parts[s], axis, [(d, (d + s) % n) for d in range(n)]) for s in range(1, n)
    ]


def after(x, y):
    return lax.optimization_barrier((x, y))[0]


def exchange(x, axis):
    return lax.all_to_all(x, axis, split_axis=0, concat_axis=0, tiled=True)


def shards(rows, cols, pairs, one_body, aux, weights):
    n = one_body.shape[0]
    naux = aux.shape[2]
    local_rows, local_cols = pairs.shape
    size = local_rows * local_cols
    me = lax.axis_index("col").astype(jnp.int32).reshape(1)

    row_block = (rows, local_cols // rows, local_rows)
    col_block = (cols, local_rows // cols, local_cols)
    spans = halved(row_block[1])

    def row_wire(batch):
        return jax.ShapeDtypeStruct((rows, *wire(batch, local_rows)), f32)

    def col_wires(width):
        return [jax.ShapeDtypeStruct(wire(col_block[1], width), f32)] * cols

    row_stage, col_stage = pltpu.VMEM(row_block, f32), pltpu.VMEM(col_block, f32)

    crossed, mine = call(
        functools.partial(cross_body, n),
        [jax.ShapeDtypeStruct((local_cols, local_rows), f32), row_wire(row_block[1])],
        [pairs], moved=12 * size,
    )

    aux = after(aux, mine)
    whole = lax.all_gather(aux.reshape(-1, naux), "row", axis=0, tiled=True)
    mine = exchange(mine, "row")
    turned = call(turn_body, col_wires(local_cols), [me, crossed], [col_stage], moved=8 * size)
    theirs = shift(turned, "col")
    whole = lax.all_gather(after(whole, theirs), "col", axis=0, tiled=False)
    group = 8 if n % 8 == 0 else n
    shape = jax.ShapeDtypeStruct((n * n, naux), bf16)
    high, low = pl.pallas_call(
        functools.partial(split_body, n),
        grid=(n // group,),
        in_specs=[pl.BlockSpec((cols, group * n // cols, naux), lambda s: (0, s, 0))],
        out_specs=[pl.BlockSpec((group * n, naux), lambda s: (s, 0))] * 2,
        out_shape=[shape, shape],
        compiler_params=pltpu.CompilerParams(vmem_limit_bytes=vmem_limit),
        cost_estimate=pl.CostEstimate(
            flops=2 * n * n * naux, bytes_accessed=8 * n * n * naux, transcendentals=0
        ),
    )(whole)

    left = tripled(one_body)
    right = tripled(-one_body.T)
    gain = weights.reshape(1, naux)

    def operator(body, arrays, consts, outs, block, scratch=()):
        batch = block[1]
        work = pltpu.VMEM((-(-batch // 128), n * n, 128), f32)
        return call(
            functools.partial(body, n),
            outs,
            [*arrays, high, low, *consts],
            [pltpu.VMEM(block, f32), work, work, *scratch],
            flops=12 * n * n * (naux + n) * batch,
            moved=4 * n * n * naux + 12 * size,
        )

    row_consts = [gain, left, right]
    col_consts = [-gain, right, left]

    first, *parts = operator(
        lambda n, *refs: left_body(n, spans, *refs),
        [mine], row_consts,
        [jax.ShapeDtypeStruct(row_block, f32)] + [row_wire(b - a) for a, b in spans], row_block,
    )
    double = operator(left_again_body, [first], row_consts, row_wire(row_block[1]), row_block)
    base = operator(
        lambda n, *refs: right_body(n, cols, *refs),
        [me, *after(theirs, double)], col_consts, jax.ShapeDtypeStruct(col_block, f32), col_block,
    )
    arriving, part = [], double
    for h, (start, stop) in enumerate(spans):
        part = exchange(after(parts[h], (part, base)) if h else parts[h], "row")
        if h + 1 == len(spans):
            double = after(double, part)
        if h:
            part = after(part, turned)
        turned = call(
            turn_arriving_body, col_wires(rows * (stop - start)), [me, part],
            [
                pltpu.VMEM((rows, stop - start, local_rows), f32),
                pltpu.VMEM((*col_block[:2], rows * (stop - start)), f32),
            ],
            moved=8 * size // len(spans),
        )
        arriving += shift(turned, "col")
    double = exchange(double, "row")
    last = operator(
        lambda n, *refs: right_again_body(n, cols, rows, spans, *refs),
        [me, base, *arriving], col_consts, col_wires(local_cols), col_block,
        [pltpu.VMEM((*col_block[:2], rows * (b - a)), f32) for a, b in spans],
    )
    last = shift(last, "col")

    return call(
        functools.partial(finish_body, n),
        jax.ShapeDtypeStruct(pairs.shape, f32),
        [me, pairs, double, *last],
        [row_stage, col_stage, pltpu.VMEM((local_cols, local_rows), f32)],
        moved=16 * size,
    )


def solution(mesh):
    body = functools.partial(shards, mesh.shape["row"], mesh.shape["col"])
    in_specs = (P("row", "col"), P(), P("row", "col", None), P())
    return jax.shard_map(
        body, mesh=mesh, in_specs=in_specs, out_specs=P("row", "col"), check_vma=False
    )
```

```python
import functools

import jax
import jax.numpy as jnp
from jax import lax
from jax.experimental import pallas as pl
from jax.experimental.pallas import tpu as pltpu
from jax.sharding import PartitionSpec as P

time_step = 0.15
vmem_limit = 60 * 1024 * 1024
f32, bf16 = jnp.float32, jnp.bfloat16


def halves(x):
    high = x.astype(bf16)
    return high, (x - high.astype(f32)).astype(bf16)


def dot(a, b):
    return lax.dot_general(a, b, (((1,), (0,)), ((), ())), preferred_element_type=f32)


def dot3(a, b):
    return dot(a[0], b[0]) + dot(a[0], b[1]) + dot(a[1], b[0])


def stacked(x):
    high, low = halves(x)
    return jnp.concatenate([high, high, low], axis=0)


def call(body, out_shape, operands, scratch=(), flops=0, moved=0):
    vmem, smem = pl.BlockSpec(memory_space=pltpu.VMEM), pl.BlockSpec(memory_space=pltpu.SMEM)
    return pl.pallas_call(
        body,
        in_specs=[smem if x.dtype == jnp.int32 else vmem for x in operands],
        out_specs=jax.tree.map(lambda _: vmem, out_shape),
        out_shape=out_shape,
        scratch_shapes=list(scratch),
        compiler_params=pltpu.CompilerParams(vmem_limit_bytes=vmem_limit),
        cost_estimate=pl.CostEstimate(flops=flops, bytes_accessed=moved, transcendentals=0),
    )(*operands)


def tiles(total, size=128):
    return [slice(start, min(start + size, total)) for start in range(0, total, size)]


def folded(batch, width):
    def cost(g):
        return -(-batch // g // 8) * -(-g * width // 128)

    return min([g for g in range(1, batch + 1) if g == 1 or batch % (8 * g) == 0], key=cost)


def wire(batch, width):
    g = folded(batch, width)
    return (batch // g, g * width)


def fold(block, shape):
    rows, g = shape[0], shape[1] // block.shape[1]
    parts = [block[h * rows : (h + 1) * rows, :] for h in range(g)]
    return jnp.concatenate(parts, axis=1) if g > 1 else block


def unfold(in_ref, width):
    parts = [in_ref[:, h * width : (h + 1) * width] for h in range(in_ref.shape[1] // width)]
    return jnp.concatenate(parts, axis=0) if len(parts) > 1 else parts[0]


def halved(batch):
    cut = -(-batch // 16) * 8
    return [(0, cut), (cut, batch)] if cut < batch else [(0, batch)]


def hand_out(me_ref, stage, outs):
    for s, out_ref in enumerate(outs):
        out_ref[...] = fold(stage[lax.rem(me_ref[0] + s, len(outs))], out_ref.shape)


def take_in(me_ref, ins, stage):
    for s, in_ref in enumerate(ins):
        stage[lax.rem(me_ref[0] + len(ins) - s, len(ins))] = unfold(in_ref, stage.shape[2])


def rows_of(stage, span):
    batch = stage.shape[1]
    parts = []
    for b in range(span.start // batch, -(-span.stop // batch)):
        low, high = max(span.start - b * batch, 0), min(span.stop - b * batch, batch)
        parts.append(stage[b, low:high, :])
    return jnp.concatenate(parts, axis=0) if len(parts) > 1 else parts[0]


def cross_body(n, x_ref, crossed_ref, out_ref):
    rows = tiles(x_ref.shape[0], n)
    for k in tiles(x_ref.shape[1], n):
        crossed_ref[k, :] = jnp.concatenate([x_ref[i, k] for i in rows], axis=1)
    count = out_ref.shape[0]
    batch = crossed_ref.shape[0] // count
    for b in range(count):
        block = crossed_ref[b * batch : (b + 1) * batch, :]
        out_ref[b] = fold(block, out_ref.shape[1:])


def turn_body(me_ref, x_ref, *refs):
    *outs, stage = refs
    turn_rows(lambda strip: x_ref[strip, :], x_ref.shape[0], stage)
    hand_out(me_ref, stage, outs)


def turn_rows(rows, total, stage):
    count, batch, _ = stage.shape
    for strip in tiles(total):
        turned = rows(strip).T
        for b in range(count):
            stage[b, :, strip] = turned[b * batch : (b + 1) * batch]


def turn_arriving_body(me_ref, x_ref, *refs):
    *outs, arrived, stage = refs
    for b in range(arrived.shape[0]):
        arrived[b] = unfold(x_ref.at[b], arrived.shape[2])
    turn_rows(lambda strip: rows_of(arrived, strip), arrived.shape[0] * arrived.shape[1], stage)
    hand_out(me_ref, stage, outs)


def finish_body(n, me_ref, x_ref, crossed_ref, *refs):
    *ins, out_ref, arrived, stage, total = refs
    for b in range(arrived.shape[0]):
        arrived[b] = unfold(crossed_ref.at[b], arrived.shape[2])
    take_in(me_ref, ins, stage)
    for strip in tiles(total.shape[0]):
        turned = jnp.concatenate([stage[b, :, strip] for b in range(len(ins))], axis=0)
        total[strip, :] = rows_of(arrived, strip) + turned.T
    cols = tiles(x_ref.shape[1], n)
    for i in tiles(x_ref.shape[0], n):
        out_ref[i, :] = x_ref[i, :] + jnp.concatenate([total[k, i] for k in cols], axis=1)


def split_body(n, x_ref, high_ref, low_ref):
    wide = x_ref.shape[1] * x_ref.shape[0] // n
    each = n // x_ref.shape[0]
    for p in range(wide):
        parts = [x_ref[c, p * each : (p + 1) * each, :] for c in range(x_ref.shape[0])]
        rows = slice(p * n, (p + 1) * n)
        high_ref[rows, :], low_ref[rows, :] = halves(jnp.concatenate(parts, axis=0))


def take(ref, rows, batch):
    parts = [ref[t, rows, : min(128, batch - 128 * t)] for t in range(ref.shape[0])]
    return jnp.concatenate(parts, axis=1) if len(parts) > 1 else parts[0]


def put(ref, rows, value):
    for t in range(ref.shape[0]):
        part = value[:, 128 * t : 128 * (t + 1)]
        ref[t, rows, : part.shape[1]] = part


def apply_operator(
    n, keep, scale, field, target, high_ref, low_ref, weights_ref, major_ref, minor_ref, xp, zp
):
    blocks, batch, width = field.shape

    def span(r):
        return pl.ds(pl.multiple_of(r * width, 16), width)

    def project(r, total):
        x = field[r]
        put(xp, span(r), x.T)
        return total + dot3(halves(x), (high_ref[span(r), :], low_ref[span(r), :]))

    total = jnp.zeros((batch, high_ref.shape[1]), f32)
    total = lax.fori_loop(0, blocks, project, total)
    proj = halves((total * weights_ref[...]).T)

    group = 8 if n % 8 == 0 else 1

    def major(step, carry):
        for g in range(group):
            at = (pl.ds(step * group + g, n, stride=n), slice(None))
            parts = [xp[(t, *at)] for t in range(xp.shape[0])]
            x = jnp.concatenate(parts, axis=1) if len(parts) > 1 else parts[0]
            term = dot(major_ref[...], stacked(x))
            for t in range(xp.shape[0]):
                zp[(t, *at)] = term[:, 128 * t : 128 * (t + 1)]
        return carry

    lax.fori_loop(0, n // group, major, 0)

    def result(r, carry):
        total = dot3((high_ref[span(r), :], low_ref[span(r), :]), proj)
        minor = []
        for p in range(width // n):
            at = pl.ds(pl.multiple_of(r * width + p * n, 16), n)
            minor.append(dot(minor_ref[...], stacked(take(xp, at, batch))))
        total = total + jnp.concatenate(minor, axis=0) + take(zp, span(r), batch)
        if keep:
            target[r] = scale * total.T + keep * field[r]
        else:
            target[r] = scale * total.T
        return carry

    lax.fori_loop(0, blocks, result, 0)


def send_left(spans, stage, outs):
    for b in range(stage.shape[0]):
        for (start, stop), out_ref in zip(spans, outs):
            out_ref[b] = fold(stage[b, start:stop, :], out_ref.shape[1:])


def left_body(n, spans, x_ref, *refs):
    *consts, out_ref = refs[:6]
    outs, (stage, xp, zp) = refs[6 : 6 + len(spans)], refs[6 + len(spans) :]
    for b in range(stage.shape[0]):
        stage[b] = unfold(x_ref.at[b], stage.shape[2])
    apply_operator(n, 0.0, 1.0, stage, out_ref, *consts, xp, zp)
    send_left(spans, out_ref, outs)


def left_again_body(n, x_ref, *refs):
    *consts, out_ref, stage, xp, zp = refs
    apply_operator(n, time_step, time_step * time_step / 2.0, x_ref, stage, *consts, xp, zp)
    send_left([(0, stage.shape[1])], stage, [out_ref])


def right_body(n, count, me_ref, *refs):
    ins, (*consts, out_ref, stage, xp, zp) = refs[:count], refs[count:]
    take_in(me_ref, ins, stage)
    apply_operator(
        n, time_step, time_step * time_step / 2.0, stage, out_ref, *consts, xp, zp
    )


def right_again_body(n, count, rows, spans, me_ref, base_ref, *refs):
    split = count * len(spans)
    ins, consts, outs = refs[:split], refs[split : split + 5], refs[split + 5 : split + 5 + count]
    stage, xp, zp, *arrived = refs[split + 5 + count :]
    for h, part in enumerate(arrived):
        take_in(me_ref, ins[h * count : (h + 1) * count], part)
    sizes = [stop - start for start, stop in spans]
    for b in range(count):
        parts = [
            part[b, :, r * size : (r + 1) * size]
            for r in range(rows)
            for part, size in zip(arrived, sizes)
        ]
        stage[b] = base_ref[b] + (time_step * time_step) * jnp.concatenate(parts, axis=1)
    apply_operator(n, 0.0, 1.0, stage, stage, *consts, xp, zp)
    hand_out(me_ref, stage, outs)


def tripled(matrix):
    high = lax.reduce_precision(matrix, 8, 7)
    low = matrix - high
    return jnp.concatenate([high, low, high], axis=1).astype(bf16)


def shift(parts, axis):
    n = len(parts)
    return [parts[0]] + [
        lax.ppermute(parts[s], axis, [(d, (d + s) % n) for d in range(n)]) for s in range(1, n)
    ]


def after(x, y):
    return lax.optimization_barrier((x, y))[0]


def exchange(x, axis):
    return lax.all_to_all(x, axis, split_axis=0, concat_axis=0, tiled=True)


def shards(rows, cols, pairs, one_body, aux, weights):
    n = one_body.shape[0]
    naux = aux.shape[2]
    local_rows, local_cols = pairs.shape
    size = local_rows * local_cols
    me = lax.axis_index("col").astype(jnp.int32).reshape(1)

    row_block = (rows, local_cols // rows, local_rows)
    col_block = (cols, local_rows // cols, local_cols)
    spans = halved(row_block[1])

    def row_wire(batch):
        return jax.ShapeDtypeStruct((rows, *wire(batch, local_rows)), f32)

    def col_wires(width):
        return [jax.ShapeDtypeStruct(wire(col_block[1], width), f32)] * cols

    row_stage, col_stage = pltpu.VMEM(row_block, f32), pltpu.VMEM(col_block, f32)

    crossed, mine = call(
        functools.partial(cross_body, n),
        [jax.ShapeDtypeStruct((local_cols, local_rows), f32), row_wire(row_block[1])],
        [pairs], moved=12 * size,
    )

    aux = after(aux, mine)
    whole = lax.all_gather(aux.reshape(-1, naux), "row", axis=0, tiled=True)
    mine = exchange(mine, "row")
    turned = call(turn_body, col_wires(local_cols), [me, crossed], [col_stage], moved=8 * size)
    theirs = shift(turned, "col")
    whole = lax.all_gather(after(whole, theirs), "col", axis=0, tiled=False)
    group = 8 if n % 8 == 0 else n
    shape = jax.ShapeDtypeStruct((n * n, naux), bf16)
    high, low = pl.pallas_call(
        functools.partial(split_body, n),
        grid=(n // group,),
        in_specs=[pl.BlockSpec((cols, group * n // cols, naux), lambda s: (0, s, 0))],
        out_specs=[pl.BlockSpec((group * n, naux), lambda s: (s, 0))] * 2,
        out_shape=[shape, shape],
        compiler_params=pltpu.CompilerParams(vmem_limit_bytes=vmem_limit),
        cost_estimate=pl.CostEstimate(
            flops=2 * n * n * naux, bytes_accessed=8 * n * n * naux, transcendentals=0
        ),
    )(whole)

    left = tripled(one_body)
    right = tripled(-one_body.T)
    gain = weights.reshape(1, naux)

    def operator(body, arrays, consts, outs, block, scratch=()):
        batch = block[1]
        work = pltpu.VMEM((-(-batch // 128), n * n, 128), f32)
        return call(
            functools.partial(body, n),
            outs,
            [*arrays, high, low, *consts],
            [pltpu.VMEM(block, f32), work, work, *scratch],
            flops=12 * n * n * (naux + n) * batch,
            moved=4 * n * n * naux + 12 * size,
        )

    row_consts = [gain, left, right]
    col_consts = [-gain, right, left]

    first, *parts = operator(
        lambda n, *refs: left_body(n, spans, *refs),
        [mine], row_consts,
        [jax.ShapeDtypeStruct(row_block, f32)] + [row_wire(b - a) for a, b in spans], row_block,
    )
    double = operator(left_again_body, [first], row_consts, row_wire(row_block[1]), row_block)
    base = operator(
        lambda n, *refs: right_body(n, cols, *refs),
        [me, *after(theirs, double)], col_consts, jax.ShapeDtypeStruct(col_block, f32), col_block,
    )
    arriving, part = [], double
    for h, (start, stop) in enumerate(spans):
        part = exchange(after(parts[h], (part, base)) if h else parts[h], "row")
        if h + 1 == len(spans):
            double = after(double, part)
        if h:
            part = after(part, arriving)
        turned = call(
            turn_arriving_body, col_wires(rows * (stop - start)), [me, part],
            [
                pltpu.VMEM((rows, stop - start, local_rows), f32),
                pltpu.VMEM((*col_block[:2], rows * (stop - start)), f32),
            ],
            moved=8 * size // len(spans),
        )
        arriving += shift(turned, "col")
    double = exchange(double, "row")
    last = operator(
        lambda n, *refs: right_again_body(n, cols, rows, spans, *refs),
        [me, base, *arriving], col_consts, col_wires(local_cols), col_block,
        [pltpu.VMEM((*col_block[:2], rows * (b - a)), f32) for a, b in spans],
    )
    last = shift(last, "col")

    return call(
        functools.partial(finish_body, n),
        jax.ShapeDtypeStruct(pairs.shape, f32),
        [me, pairs, double, *last],
        [row_stage, col_stage, pltpu.VMEM((local_cols, local_rows), f32)],
        moved=16 * size,
    )


def solution(mesh):
    body = functools.partial(shards, mesh.shape["row"], mesh.shape["col"])
    in_specs = (P("row", "col"), P(), P("row", "col", None), P())
    return jax.shard_map(
        body, mesh=mesh, in_specs=in_specs, out_specs=P("row", "col"), check_vma=False
    )
```

```python
import functools

import jax
import jax.numpy as jnp
from jax import lax
from jax.experimental import pallas as pl
from jax.experimental.pallas import tpu as pltpu
from jax.sharding import PartitionSpec as P

time_step = 0.15
vmem_limit = 60 * 1024 * 1024
f32, bf16 = jnp.float32, jnp.bfloat16


def halves(x):
    high = x.astype(bf16)
    return high, (x - high.astype(f32)).astype(bf16)


def dot(a, b):
    return lax.dot_general(a, b, (((1,), (0,)), ((), ())), preferred_element_type=f32)


def dot3(a, b):
    return dot(a[0], b[0]) + dot(a[0], b[1]) + dot(a[1], b[0])


def stacked(x):
    high, low = halves(x)
    return jnp.concatenate([high, high, low], axis=0)


def call(body, out_shape, operands, scratch=(), flops=0, moved=0):
    vmem, smem = pl.BlockSpec(memory_space=pltpu.VMEM), pl.BlockSpec(memory_space=pltpu.SMEM)
    return pl.pallas_call(
        body,
        in_specs=[smem if x.dtype == jnp.int32 else vmem for x in operands],
        out_specs=jax.tree.map(lambda _: vmem, out_shape),
        out_shape=out_shape,
        scratch_shapes=list(scratch),
        compiler_params=pltpu.CompilerParams(vmem_limit_bytes=vmem_limit),
        cost_estimate=pl.CostEstimate(flops=flops, bytes_accessed=moved, transcendentals=0),
    )(*operands)


def tiles(total, size=128):
    return [slice(start, min(start + size, total)) for start in range(0, total, size)]


def folded(batch, width):
    def cost(g):
        return -(-batch // g // 8) * -(-g * width // 128)

    return min([g for g in range(1, batch + 1) if g == 1 or batch % (8 * g) == 0], key=cost)


def wire(batch, width):
    g = folded(batch, width)
    return (batch // g, g * width)


def fold(block, shape):
    rows, g = shape[0], shape[1] // block.shape[1]
    parts = [block[h * rows : (h + 1) * rows, :] for h in range(g)]
    return jnp.concatenate(parts, axis=1) if g > 1 else block


def unfold(in_ref, width):
    parts = [in_ref[:, h * width : (h + 1) * width] for h in range(in_ref.shape[1] // width)]
    return jnp.concatenate(parts, axis=0) if len(parts) > 1 else parts[0]


def halved(batch):
    cut = -(-batch // 16) * 8
    return [(0, cut), (cut, batch)] if cut < batch else [(0, batch)]


def hand_out(me_ref, stage, outs):
    for s, out_ref in enumerate(outs):
        out_ref[...] = fold(stage[lax.rem(me_ref[0] + s, len(outs))], out_ref.shape)


def take_in(me_ref, ins, stage):
    for s, in_ref in enumerate(ins):
        stage[lax.rem(me_ref[0] + len(ins) - s, len(ins))] = unfold(in_ref, stage.shape[2])


def rows_of(stage, span):
    batch = stage.shape[1]
    parts = []
    for b in range(span.start // batch, -(-span.stop // batch)):
        low, high = max(span.start - b * batch, 0), min(span.stop - b * batch, batch)
        parts.append(stage[b, low:high, :])
    return jnp.concatenate(parts, axis=0) if len(parts) > 1 else parts[0]


def cross_body(n, x_ref, crossed_ref, out_ref):
    rows = tiles(x_ref.shape[0], n)
    for k in tiles(x_ref.shape[1], n):
        crossed_ref[k, :] = jnp.concatenate([x_ref[i, k] for i in rows], axis=1)
    count = out_ref.shape[0]
    batch = crossed_ref.shape[0] // count
    for b in range(count):
        block = crossed_ref[b * batch : (b + 1) * batch, :]
        out_ref[b] = fold(block, out_ref.shape[1:])


def turn_body(me_ref, x_ref, *refs):
    *outs, stage = refs
    turn_rows(lambda strip: x_ref[strip, :], x_ref.shape[0], stage)
    hand_out(me_ref, stage, outs)


def turn_rows(rows, total, stage):
    count, batch, _ = stage.shape
    for strip in tiles(total):
        turned = rows(strip).T
        for b in range(count):
            stage[b, :, strip] = turned[b * batch : (b + 1) * batch]


def turn_arriving_body(me_ref, x_ref, *refs):
    *outs, arrived, stage = refs
    for b in range(arrived.shape[0]):
        arrived[b] = unfold(x_ref.at[b], arrived.shape[2])
    turn_rows(lambda strip: rows_of(arrived, strip), arrived.shape[0] * arrived.shape[1], stage)
    hand_out(me_ref, stage, outs)


def finish_body(n, me_ref, x_ref, crossed_ref, *refs):
    *ins, out_ref, arrived, stage, total = refs
    for b in range(arrived.shape[0]):
        arrived[b] = unfold(crossed_ref.at[b], arrived.shape[2])
    take_in(me_ref, ins, stage)
    for strip in tiles(total.shape[0]):
        turned = jnp.concatenate([stage[b, :, strip] for b in range(len(ins))], axis=0)
        total[strip, :] = rows_of(arrived, strip) + turned.T
    cols = tiles(x_ref.shape[1], n)
    for i in tiles(x_ref.shape[0], n):
        out_ref[i, :] = x_ref[i, :] + jnp.concatenate([total[k, i] for k in cols], axis=1)


def split_body(n, x_ref, high_ref, low_ref):
    wide = x_ref.shape[1] * x_ref.shape[0] // n
    each = n // x_ref.shape[0]
    for p in range(wide):
        parts = [x_ref[c, p * each : (p + 1) * each, :] for c in range(x_ref.shape[0])]
        rows = slice(p * n, (p + 1) * n)
        high_ref[rows, :], low_ref[rows, :] = halves(jnp.concatenate(parts, axis=0))


def take(ref, rows, batch):
    parts = [ref[t, rows, : min(128, batch - 128 * t)] for t in range(ref.shape[0])]
    return jnp.concatenate(parts, axis=1) if len(parts) > 1 else parts[0]


def put(ref, rows, value):
    for t in range(ref.shape[0]):
        part = value[:, 128 * t : 128 * (t + 1)]
        ref[t, rows, : part.shape[1]] = part


def apply_operator(
    n, keep, scale, field, target, high_ref, low_ref, weights_ref, major_ref, minor_ref, xp, zp
):
    blocks, batch, width = field.shape

    def span(r):
        return pl.ds(pl.multiple_of(r * width, 16), width)

    def project(r, total):
        x = field[r]
        put(xp, span(r), x.T)
        return total + dot3(halves(x), (high_ref[span(r), :], low_ref[span(r), :]))

    total = jnp.zeros((batch, high_ref.shape[1]), f32)
    total = lax.fori_loop(0, blocks, project, total)
    proj = halves((total * weights_ref[...]).T)

    group = 8 if n % 8 == 0 else 1

    def major(step, carry):
        for g in range(group):
            at = (pl.ds(step * group + g, n, stride=n), slice(None))
            parts = [xp[(t, *at)] for t in range(xp.shape[0])]
            x = jnp.concatenate(parts, axis=1) if len(parts) > 1 else parts[0]
            term = dot(major_ref[...], stacked(x))
            for t in range(xp.shape[0]):
                zp[(t, *at)] = term[:, 128 * t : 128 * (t + 1)]
        return carry

    lax.fori_loop(0, n // group, major, 0)

    def result(r, carry):
        total = dot3((high_ref[span(r), :], low_ref[span(r), :]), proj)
        minor = []
        for p in range(width // n):
            at = pl.ds(pl.multiple_of(r * width + p * n, 16), n)
            minor.append(dot(minor_ref[...], stacked(take(xp, at, batch))))
        total = total + jnp.concatenate(minor, axis=0) + take(zp, span(r), batch)
        if keep:
            target[r] = scale * total.T + keep * field[r]
        else:
            target[r] = scale * total.T
        return carry

    lax.fori_loop(0, blocks, result, 0)


def send_left(spans, stage, outs):
    for b in range(stage.shape[0]):
        for (start, stop), out_ref in zip(spans, outs):
            out_ref[b] = fold(stage[b, start:stop, :], out_ref.shape[1:])


def left_body(n, spans, x_ref, *refs):
    *consts, out_ref = refs[:6]
    outs, (stage, xp, zp) = refs[6 : 6 + len(spans)], refs[6 + len(spans) :]
    for b in range(stage.shape[0]):
        stage[b] = unfold(x_ref.at[b], stage.shape[2])
    apply_operator(n, 0.0, 1.0, stage, out_ref, *consts, xp, zp)
    send_left(spans, out_ref, outs)


def left_again_body(n, x_ref, *refs):
    *consts, out_ref, stage, xp, zp = refs
    apply_operator(n, time_step, time_step * time_step / 2.0, x_ref, stage, *consts, xp, zp)
    send_left([(0, stage.shape[1])], stage, [out_ref])


def right_body(n, count, me_ref, *refs):
    ins, (*consts, out_ref, stage, xp, zp) = refs[:count], refs[count:]
    take_in(me_ref, ins, stage)
    apply_operator(
        n, time_step, time_step * time_step / 2.0, stage, out_ref, *consts, xp, zp
    )


def right_again_body(n, count, rows, spans, me_ref, base_ref, *refs):
    split = count * len(spans)
    ins, consts, outs = refs[:split], refs[split : split + 5], refs[split + 5 : split + 5 + count]
    stage, xp, zp, *arrived = refs[split + 5 + count :]
    for h, part in enumerate(arrived):
        take_in(me_ref, ins[h * count : (h + 1) * count], part)
    sizes = [stop - start for start, stop in spans]
    for b in range(count):
        parts = [
            part[b, :, r * size : (r + 1) * size]
            for r in range(rows)
            for part, size in zip(arrived, sizes)
        ]
        stage[b] = base_ref[b] + (time_step * time_step) * jnp.concatenate(parts, axis=1)
    apply_operator(n, 0.0, 1.0, stage, stage, *consts, xp, zp)
    hand_out(me_ref, stage, outs)


def tripled(matrix):
    high = lax.reduce_precision(matrix, 8, 7)
    low = matrix - high
    return jnp.concatenate([high, low, high], axis=1).astype(bf16)


def shift(parts, axis):
    n = len(parts)
    return [parts[0]] + [
        lax.ppermute(parts[s], axis, [(d, (d + s) % n) for d in range(n)]) for s in range(1, n)
    ]


def after(x, y):
    return lax.optimization_barrier((x, y))[0]


def exchange(x, axis):
    return lax.all_to_all(x, axis, split_axis=0, concat_axis=0, tiled=True)


def shards(rows, cols, pairs, one_body, aux, weights):
    n = one_body.shape[0]
    naux = aux.shape[2]
    local_rows, local_cols = pairs.shape
    size = local_rows * local_cols
    me = lax.axis_index("col").astype(jnp.int32).reshape(1)

    row_block = (rows, local_cols // rows, local_rows)
    col_block = (cols, local_rows // cols, local_cols)
    spans = halved(row_block[1])

    def row_wire(batch):
        return jax.ShapeDtypeStruct((rows, *wire(batch, local_rows)), f32)

    def col_wires(width):
        return [jax.ShapeDtypeStruct(wire(col_block[1], width), f32)] * cols

    row_stage, col_stage = pltpu.VMEM(row_block, f32), pltpu.VMEM(col_block, f32)

    crossed, mine = call(
        functools.partial(cross_body, n),
        [jax.ShapeDtypeStruct((local_cols, local_rows), f32), row_wire(row_block[1])],
        [pairs], moved=12 * size,
    )

    aux = after(aux, mine)
    whole = lax.all_gather(aux.reshape(-1, naux), "row", axis=0, tiled=True)
    mine = exchange(mine, "row")
    turned = call(turn_body, col_wires(local_cols), [me, crossed], [col_stage], moved=8 * size)
    theirs = shift(turned, "col")
    whole = lax.all_gather(after(whole, theirs), "col", axis=0, tiled=False)
    group = 8 if n % 8 == 0 else n
    shape = jax.ShapeDtypeStruct((n * n, naux), bf16)
    high, low = pl.pallas_call(
        functools.partial(split_body, n),
        grid=(n // group,),
        in_specs=[pl.BlockSpec((cols, group * n // cols, naux), lambda s: (0, s, 0))],
        out_specs=[pl.BlockSpec((group * n, naux), lambda s: (s, 0))] * 2,
        out_shape=[shape, shape],
        compiler_params=pltpu.CompilerParams(vmem_limit_bytes=vmem_limit),
        cost_estimate=pl.CostEstimate(
            flops=2 * n * n * naux, bytes_accessed=8 * n * n * naux, transcendentals=0
        ),
    )(whole)

    left = tripled(one_body)
    right = tripled(-one_body.T)
    gain = weights.reshape(1, naux)

    def operator(body, arrays, consts, outs, block, scratch=()):
        batch = block[1]
        work = pltpu.VMEM((-(-batch // 128), n * n, 128), f32)
        return call(
            functools.partial(body, n),
            outs,
            [*arrays, high, low, *consts],
            [pltpu.VMEM(block, f32), work, work, *scratch],
            flops=12 * n * n * (naux + n) * batch,
            moved=4 * n * n * naux + 12 * size,
        )

    row_consts = [gain, left, right]
    col_consts = [-gain, right, left]

    first, *parts = operator(
        lambda n, *refs: left_body(n, spans, *refs),
        [mine], row_consts,
        [jax.ShapeDtypeStruct(row_block, f32)] + [row_wire(b - a) for a, b in spans], row_block,
    )
    double = operator(left_again_body, [first], row_consts, row_wire(row_block[1]), row_block)
    base = operator(
        lambda n, *refs: right_body(n, cols, *refs),
        [me, *after(theirs, double)], col_consts, jax.ShapeDtypeStruct(col_block, f32), col_block,
    )
    arriving, part = [], double
    for h, (start, stop) in enumerate(spans):
        part = exchange(after(parts[h], (part, base)) if h else parts[h], "row")
        if h + 1 == len(spans):
            double = after(double, (part, arriving))
        if h:
            part = after(part, arriving)
        turned = call(
            turn_arriving_body, col_wires(rows * (stop - start)), [me, part],
            [
                pltpu.VMEM((rows, stop - start, local_rows), f32),
                pltpu.VMEM((*col_block[:2], rows * (stop - start)), f32),
            ],
            moved=8 * size // len(spans),
        )
        arriving += shift(turned, "col")
    double = exchange(double, "row")
    last = operator(
        lambda n, *refs: right_again_body(n, cols, rows, spans, *refs),
        [me, base, *arriving], col_consts, col_wires(local_cols), col_block,
        [pltpu.VMEM((*col_block[:2], rows * (b - a)), f32) for a, b in spans],
    )
    last = shift(last, "col")

    return call(
        functools.partial(finish_body, n),
        jax.ShapeDtypeStruct(pairs.shape, f32),
        [me, pairs, double, *last],
        [row_stage, col_stage, pltpu.VMEM((local_cols, local_rows), f32)],
        moved=16 * size,
    )


def solution(mesh):
    body = functools.partial(shards, mesh.shape["row"], mesh.shape["col"])
    in_specs = (P("row", "col"), P(), P("row", "col", None), P())
    return jax.shard_map(
        body, mesh=mesh, in_specs=in_specs, out_specs=P("row", "col"), check_vma=False
    )
```

```python
import functools

import jax
import jax.numpy as jnp
from jax import lax
from jax.experimental import pallas as pl
from jax.experimental.pallas import tpu as pltpu
from jax.sharding import PartitionSpec as P

time_step = 0.15
vmem_limit = 60 * 1024 * 1024
f32, bf16 = jnp.float32, jnp.bfloat16


def halves(x):
    high = x.astype(bf16)
    return high, (x - high.astype(f32)).astype(bf16)


def dot(a, b):
    return lax.dot_general(a, b, (((1,), (0,)), ((), ())), preferred_element_type=f32)


def dot3(a, b):
    return dot(a[0], b[0]) + dot(a[0], b[1]) + dot(a[1], b[0])


def stacked(x):
    high, low = halves(x)
    return jnp.concatenate([high, high, low], axis=0)


def call(body, out_shape, operands, scratch=(), flops=0, moved=0):
    vmem, smem = pl.BlockSpec(memory_space=pltpu.VMEM), pl.BlockSpec(memory_space=pltpu.SMEM)
    return pl.pallas_call(
        body,
        in_specs=[smem if x.dtype == jnp.int32 else vmem for x in operands],
        out_specs=jax.tree.map(lambda _: vmem, out_shape),
        out_shape=out_shape,
        scratch_shapes=list(scratch),
        compiler_params=pltpu.CompilerParams(vmem_limit_bytes=vmem_limit),
        cost_estimate=pl.CostEstimate(flops=flops, bytes_accessed=moved, transcendentals=0),
    )(*operands)


def tiles(total, size=128):
    return [slice(start, min(start + size, total)) for start in range(0, total, size)]


def folded(batch, width):
    def cost(g):
        return -(-batch // g // 8) * -(-g * width // 128)

    return min([g for g in range(1, batch + 1) if g == 1 or batch % (8 * g) == 0], key=cost)


def wire(batch, width):
    g = folded(batch, width)
    return (batch // g, g * width)


def fold(block, shape):
    rows, g = shape[0], shape[1] // block.shape[1]
    parts = [block[h * rows : (h + 1) * rows, :] for h in range(g)]
    return jnp.concatenate(parts, axis=1) if g > 1 else block


def unfold(in_ref, width):
    parts = [in_ref[:, h * width : (h + 1) * width] for h in range(in_ref.shape[1] // width)]
    return jnp.concatenate(parts, axis=0) if len(parts) > 1 else parts[0]


def halved(batch):
    cut = -(-batch * 16 // 25 // 8) * 8
    return [(0, cut), (cut, batch)] if cut < batch else [(0, batch)]


def hand_out(me_ref, stage, outs):
    for s, out_ref in enumerate(outs):
        out_ref[...] = fold(stage[lax.rem(me_ref[0] + s, len(outs))], out_ref.shape)


def take_in(me_ref, ins, stage):
    for s, in_ref in enumerate(ins):
        stage[lax.rem(me_ref[0] + len(ins) - s, len(ins))] = unfold(in_ref, stage.shape[2])


def rows_of(stage, span):
    batch = stage.shape[1]
    parts = []
    for b in range(span.start // batch, -(-span.stop // batch)):
        low, high = max(span.start - b * batch, 0), min(span.stop - b * batch, batch)
        parts.append(stage[b, low:high, :])
    return jnp.concatenate(parts, axis=0) if len(parts) > 1 else parts[0]


def cross_body(n, spans, x_ref, crossed_ref, *outs):
    rows = tiles(x_ref.shape[0], n)
    for k in tiles(x_ref.shape[1], n):
        crossed_ref[k, :] = jnp.concatenate([x_ref[i, k] for i in rows], axis=1)
    count = outs[0].shape[0]
    batch = crossed_ref.shape[0] // count
    for b in range(count):
        for (start, stop), out_ref in zip(spans, outs):
            block = crossed_ref[b * batch + start : b * batch + stop, :]
            out_ref[b] = fold(block, out_ref.shape[1:])


def turn_body(me_ref, x_ref, *refs):
    *outs, stage = refs
    turn_rows(lambda strip: x_ref[strip, :], x_ref.shape[0], stage)
    hand_out(me_ref, stage, outs)


def turn_rows(rows, total, stage):
    count, batch, _ = stage.shape
    for strip in tiles(total):
        turned = rows(strip).T
        for b in range(count):
            stage[b, :, strip] = turned[b * batch : (b + 1) * batch]


def turn_arriving_body(me_ref, x_ref, *refs):
    *outs, arrived, stage = refs
    for b in range(arrived.shape[0]):
        arrived[b] = unfold(x_ref.at[b], arrived.shape[2])
    turn_rows(lambda strip: rows_of(arrived, strip), arrived.shape[0] * arrived.shape[1], stage)
    hand_out(me_ref, stage, outs)


def finish_body(n, parts, me_ref, x_ref, crossed_ref, *refs):
    stages, (arrived, total) = refs[-2 - parts : -2], refs[-2:]
    *ins, out_ref = refs[: -2 - parts]
    for b in range(arrived.shape[0]):
        arrived[b] = unfold(crossed_ref.at[b], arrived.shape[2])
    count = len(ins) // parts
    for h, stage in enumerate(stages):
        take_in(me_ref, ins[h * count : (h + 1) * count], stage)
    for strip in tiles(total.shape[0]):
        turned = [stage[b, :, strip] for b in range(count) for stage in stages]
        total[strip, :] = rows_of(arrived, strip) + jnp.concatenate(turned, axis=0).T
    cols = tiles(x_ref.shape[1], n)
    for i in tiles(x_ref.shape[0], n):
        out_ref[i, :] = x_ref[i, :] + jnp.concatenate([total[k, i] for k in cols], axis=1)


def split_body(n, x_ref, high_ref, low_ref):
    wide = x_ref.shape[1] * x_ref.shape[0] // n
    each = n // x_ref.shape[0]
    for p in range(wide):
        parts = [x_ref[c, p * each : (p + 1) * each, :] for c in range(x_ref.shape[0])]
        rows = slice(p * n, (p + 1) * n)
        high_ref[rows, :], low_ref[rows, :] = halves(jnp.concatenate(parts, axis=0))


def take(ref, rows, batch):
    parts = [ref[t, rows, : min(128, batch - 128 * t)] for t in range(ref.shape[0])]
    return jnp.concatenate(parts, axis=1) if len(parts) > 1 else parts[0]


def put(ref, rows, value):
    for t in range(ref.shape[0]):
        part = value[:, 128 * t : 128 * (t + 1)]
        ref[t, rows, : part.shape[1]] = part


def apply_operator(
    n, keep, scale, field, target, high_ref, low_ref, weights_ref, major_ref, minor_ref, xp, zp
):
    blocks, batch, width = field.shape

    def span(r):
        return pl.ds(pl.multiple_of(r * width, 16), width)

    def project(r, total):
        x = field[r]
        put(xp, span(r), x.T)
        return total + dot3(halves(x), (high_ref[span(r), :], low_ref[span(r), :]))

    total = jnp.zeros((batch, high_ref.shape[1]), f32)
    total = lax.fori_loop(0, blocks, project, total)
    proj = halves((total * weights_ref[...]).T)

    group = 8 if n % 8 == 0 else 1

    def major(step, carry):
        for g in range(group):
            at = (pl.ds(step * group + g, n, stride=n), slice(None))
            parts = [xp[(t, *at)] for t in range(xp.shape[0])]
            x = jnp.concatenate(parts, axis=1) if len(parts) > 1 else parts[0]
            term = dot(major_ref[...], stacked(x))
            for t in range(xp.shape[0]):
                zp[(t, *at)] = term[:, 128 * t : 128 * (t + 1)]
        return carry

    lax.fori_loop(0, n // group, major, 0)

    def result(r, carry):
        total = dot3((high_ref[span(r), :], low_ref[span(r), :]), proj)
        minor = []
        for p in range(width // n):
            at = pl.ds(pl.multiple_of(r * width + p * n, 16), n)
            minor.append(dot(minor_ref[...], stacked(take(xp, at, batch))))
        total = total + jnp.concatenate(minor, axis=0) + take(zp, span(r), batch)
        if keep:
            target[r] = scale * total.T + keep * field[r]
        else:
            target[r] = scale * total.T
        return carry

    lax.fori_loop(0, blocks, result, 0)


def left_body(n, x_ref, *refs):
    *consts, out_ref, sent_ref, stage, xp, zp = refs
    for b in range(stage.shape[0]):
        stage[b] = unfold(x_ref.at[b], stage.shape[2])
    apply_operator(n, 0.0, 1.0, stage, out_ref, *consts, xp, zp)
    for b in range(stage.shape[0]):
        sent_ref[b] = fold(out_ref[b], sent_ref.shape[1:])


def left_again_body(n, spans, *refs):
    parts, (*consts, out_ref, stage, xp, zp) = refs[: len(spans)], refs[len(spans) :]
    for (start, stop), part in zip(spans, parts):
        stage[:, start:stop, :] = part[...]
    apply_operator(n, time_step, time_step * time_step / 2.0, stage, stage, *consts, xp, zp)
    for b in range(stage.shape[0]):
        out_ref[b] = fold(stage[b], out_ref.shape[1:])


def right_body(n, count, me_ref, *refs):
    ins, (*consts, out_ref, stage, xp, zp) = refs[:count], refs[count:]
    take_in(me_ref, ins, stage)
    apply_operator(
        n, time_step, time_step * time_step / 2.0, stage, out_ref, *consts, xp, zp
    )


def right_again_body(n, count, rows, spans, span, me_ref, base_ref, *refs):
    split = count * len(spans)
    ins, consts, outs = refs[:split], refs[split : split + 5], refs[split + 5 : split + 5 + count]
    stage, xp, zp, *arrived = refs[split + 5 + count :]
    for h, part in enumerate(arrived):
        take_in(me_ref, ins[h * count : (h + 1) * count], part)
    sizes = [stop - start for start, stop in spans]
    for b in range(count):
        parts = [
            part[b, span, r * size : (r + 1) * size]
            for r in range(rows)
            for part, size in zip(arrived, sizes)
        ]
        stage[b] = base_ref[b, span] + (time_step * time_step) * jnp.concatenate(parts, axis=1)
    apply_operator(n, 0.0, 1.0, stage, stage, *consts, xp, zp)
    hand_out(me_ref, stage, outs)


def tripled(matrix):
    high = lax.reduce_precision(matrix, 8, 7)
    low = matrix - high
    return jnp.concatenate([high, low, high], axis=1).astype(bf16)


def shift(parts, axis):
    n = len(parts)
    return [parts[0]] + [
        lax.ppermute(parts[s], axis, [(d, (d + s) % n) for d in range(n)]) for s in range(1, n)
    ]


def after(x, y):
    return lax.optimization_barrier((x, y))[0]


def exchange(x, axis):
    return lax.all_to_all(x, axis, split_axis=0, concat_axis=0, tiled=True)


def shards(rows, cols, pairs, one_body, aux, weights):
    n = one_body.shape[0]
    naux = aux.shape[2]
    local_rows, local_cols = pairs.shape
    size = local_rows * local_cols
    me = lax.axis_index("col").astype(jnp.int32).reshape(1)

    row_block = (rows, local_cols // rows, local_rows)
    col_block = (cols, local_rows // cols, local_cols)
    spans = halved(row_block[1])

    def row_wire(batch):
        return jax.ShapeDtypeStruct((rows, *wire(batch, local_rows)), f32)

    def col_wires(width):
        return [jax.ShapeDtypeStruct(wire(col_block[1], width), f32)] * cols

    row_stage, col_stage = pltpu.VMEM(row_block, f32), pltpu.VMEM(col_block, f32)

    crossed, *sent = call(
        functools.partial(cross_body, n, spans),
        [jax.ShapeDtypeStruct((local_cols, local_rows), f32)]
        + [row_wire(b - a) for a, b in spans],
        [pairs], moved=12 * size,
    )

    aux = after(aux, sent)
    whole = lax.all_gather(aux.reshape(-1, naux), "row", axis=0, tiled=True)
    mine = []
    for part in sent:
        mine.append(exchange(after(part, mine) if mine else part, "row"))
    turned = call(turn_body, col_wires(local_cols), [me, crossed], [col_stage], moved=8 * size)
    theirs = shift(turned, "col")
    whole = lax.all_gather(after(whole, theirs), "col", axis=0, tiled=False)
    group = 8 if n % 8 == 0 else n
    shape = jax.ShapeDtypeStruct((n * n, naux), bf16)
    high, low = pl.pallas_call(
        functools.partial(split_body, n),
        grid=(n // group,),
        in_specs=[pl.BlockSpec((cols, group * n // cols, naux), lambda s: (0, s, 0))],
        out_specs=[pl.BlockSpec((group * n, naux), lambda s: (s, 0))] * 2,
        out_shape=[shape, shape],
        compiler_params=pltpu.CompilerParams(vmem_limit_bytes=vmem_limit),
        cost_estimate=pl.CostEstimate(
            flops=2 * n * n * naux, bytes_accessed=8 * n * n * naux, transcendentals=0
        ),
    )(whole)

    left = tripled(one_body)
    right = tripled(-one_body.T)
    gain = weights.reshape(1, naux)

    def operator(body, arrays, consts, outs, block, scratch=()):
        batch = block[1]
        work = pltpu.VMEM((-(-batch // 128), n * n, 128), f32)
        return call(
            functools.partial(body, n),
            outs,
            [*arrays, high, low, *consts],
            [pltpu.VMEM(block, f32), work, work, *scratch],
            flops=12 * n * n * (naux + n) * batch,
            moved=4 * n * n * naux + 12 * size,
        )

    row_consts = [gain, left, right]
    col_consts = [-gain, right, left]

    first, parts = [], []
    for (start, stop), part in zip(spans, mine):
        block = (rows, stop - start, local_rows)
        outs = [jax.ShapeDtypeStruct(block, f32), row_wire(stop - start)]
        result, leaving = operator(
            left_body, [after(part, parts) if parts else part], row_consts, outs, block
        )
        first.append(result)
        parts.append(leaving)
    double = operator(
        lambda n, *refs: left_again_body(n, spans, *refs),
        first, row_consts, row_wire(row_block[1]), row_block,
    )
    base = operator(
        lambda n, *refs: right_body(n, cols, *refs),
        [me, *after(theirs, double)], col_consts, jax.ShapeDtypeStruct(col_block, f32), col_block,
    )
    arriving, part = [], double
    for h, (start, stop) in enumerate(spans):
        part = exchange(after(parts[h], (part, base)) if h else parts[h], "row")
        if h + 1 == len(spans):
            double = after(double, (part, arriving))
        if h:
            part = after(part, arriving)
        turned = call(
            turn_arriving_body, col_wires(rows * (stop - start)), [me, part],
            [
                pltpu.VMEM((rows, stop - start, local_rows), f32),
                pltpu.VMEM((*col_block[:2], rows * (stop - start)), f32),
            ],
            moved=8 * size // len(spans),
        )
        arriving += shift(turned, "col")
    double = exchange(double, "row")
    last, stages = [], []
    for start, stop in [(0, col_block[1])]:
        block = (cols, stop - start, local_cols)
        outs = operator(
            lambda n, *refs: right_again_body(n, cols, rows, spans, slice(start, stop), *refs),
            [me, base, *arriving], col_consts,
            [jax.ShapeDtypeStruct(wire(stop - start, local_cols), f32)] * cols, block,
            [pltpu.VMEM((*col_block[:2], rows * (b - a)), f32) for a, b in spans],
        )
        last += shift(outs, "col")
        stages.append(pltpu.VMEM(block, f32))

    return call(
        functools.partial(finish_body, n, len(stages)),
        jax.ShapeDtypeStruct(pairs.shape, f32),
        [me, pairs, double, *last],
        [*stages, row_stage, pltpu.VMEM((local_cols, local_rows), f32)],
        moved=16 * size,
    )


def solution(mesh):
    body = functools.partial(shards, mesh.shape["row"], mesh.shape["col"])
    in_specs = (P("row", "col"), P(), P("row", "col", None), P())
    return jax.shard_map(
        body, mesh=mesh, in_specs=in_specs, out_specs=P("row", "col"), check_vma=False
    )
```

```python
import functools

import jax
import jax.numpy as jnp
from jax import lax
from jax.experimental import pallas as pl
from jax.experimental.pallas import tpu as pltpu
from jax.sharding import PartitionSpec as P

time_step = 0.15
vmem_limit = 60 * 1024 * 1024
f32, bf16 = jnp.float32, jnp.bfloat16


def halves(x):
    high = x.astype(bf16)
    return high, (x - high.astype(f32)).astype(bf16)


def dot(a, b):
    return lax.dot_general(a, b, (((1,), (0,)), ((), ())), preferred_element_type=f32)


def dot3(a, b):
    return dot(a[0], b[0]) + dot(a[0], b[1]) + dot(a[1], b[0])


def stacked(x):
    high, low = halves(x)
    return jnp.concatenate([high, high, low], axis=0)


def call(body, out_shape, operands, scratch=(), flops=0, moved=0):
    vmem, smem = pl.BlockSpec(memory_space=pltpu.VMEM), pl.BlockSpec(memory_space=pltpu.SMEM)
    return pl.pallas_call(
        body,
        in_specs=[smem if x.dtype == jnp.int32 else vmem for x in operands],
        out_specs=jax.tree.map(lambda _: vmem, out_shape),
        out_shape=out_shape,
        scratch_shapes=list(scratch),
        compiler_params=pltpu.CompilerParams(vmem_limit_bytes=vmem_limit),
        cost_estimate=pl.CostEstimate(flops=flops, bytes_accessed=moved, transcendentals=0),
    )(*operands)


def tiles(total, size=128):
    return [slice(start, min(start + size, total)) for start in range(0, total, size)]


def folded(batch, width):
    def cost(g):
        return -(-batch // g // 8) * -(-g * width // 128)

    return min([g for g in range(1, batch + 1) if g == 1 or batch % (8 * g) == 0], key=cost)


def wire(batch, width):
    g = folded(batch, width)
    return (batch // g, g * width)


def fold(block, shape):
    rows, g = shape[0], shape[1] // block.shape[1]
    parts = [block[h * rows : (h + 1) * rows, :] for h in range(g)]
    return jnp.concatenate(parts, axis=1) if g > 1 else block


def unfold(in_ref, width):
    parts = [in_ref[:, h * width : (h + 1) * width] for h in range(in_ref.shape[1] // width)]
    return jnp.concatenate(parts, axis=0) if len(parts) > 1 else parts[0]


def halved(batch):
    cut = -(-batch * 16 // 25 // 8) * 8
    return [(0, cut), (cut, batch)] if cut < batch else [(0, batch)]


def hand_out(me_ref, stage, outs):
    for s, out_ref in enumerate(outs):
        out_ref[...] = fold(stage[lax.rem(me_ref[0] + s, len(outs))], out_ref.shape)


def take_in(me_ref, ins, stage):
    for s, in_ref in enumerate(ins):
        stage[lax.rem(me_ref[0] + len(ins) - s, len(ins))] = unfold(in_ref, stage.shape[2])


def rows_of(stage, span):
    batch = stage.shape[1]
    parts = []
    for b in range(span.start // batch, -(-span.stop // batch)):
        low, high = max(span.start - b * batch, 0), min(span.stop - b * batch, batch)
        parts.append(stage[b, low:high, :])
    return jnp.concatenate(parts, axis=0) if len(parts) > 1 else parts[0]


def cross_body(n, spans, x_ref, crossed_ref, *outs):
    rows = tiles(x_ref.shape[0], n)
    for k in tiles(x_ref.shape[1], n):
        crossed_ref[k, :] = jnp.concatenate([x_ref[i, k] for i in rows], axis=1)
    count = outs[0].shape[0]
    batch = crossed_ref.shape[0] // count
    for b in range(count):
        for (start, stop), out_ref in zip(spans, outs):
            block = crossed_ref[b * batch + start : b * batch + stop, :]
            out_ref[b] = fold(block, out_ref.shape[1:])


def turn_body(me_ref, x_ref, *refs):
    *outs, stage = refs
    turn_rows(lambda strip: x_ref[strip, :], x_ref.shape[0], stage)
    hand_out(me_ref, stage, outs)


def turn_rows(rows, total, stage):
    count, batch, _ = stage.shape
    for strip in tiles(total):
        turned = rows(strip).T
        for b in range(count):
            stage[b, :, strip] = turned[b * batch : (b + 1) * batch]


def turn_arriving_body(me_ref, x_ref, *refs):
    *outs, arrived, stage = refs
    for b in range(arrived.shape[0]):
        arrived[b] = unfold(x_ref.at[b], arrived.shape[2])
    turn_rows(lambda strip: rows_of(arrived, strip), arrived.shape[0] * arrived.shape[1], stage)
    hand_out(me_ref, stage, outs)


def finish_body(n, parts, me_ref, x_ref, crossed_ref, *refs):
    stages, (arrived, total) = refs[-2 - parts : -2], refs[-2:]
    *ins, out_ref = refs[: -2 - parts]
    for b in range(arrived.shape[0]):
        arrived[b] = unfold(crossed_ref.at[b], arrived.shape[2])
    count = len(ins) // parts
    for h, stage in enumerate(stages):
        take_in(me_ref, ins[h * count : (h + 1) * count], stage)
    for strip in tiles(total.shape[0]):
        turned = [stage[b, :, strip] for b in range(count) for stage in stages]
        total[strip, :] = rows_of(arrived, strip) + jnp.concatenate(turned, axis=0).T
    cols = tiles(x_ref.shape[1], n)
    for i in tiles(x_ref.shape[0], n):
        out_ref[i, :] = x_ref[i, :] + jnp.concatenate([total[k, i] for k in cols], axis=1)


def split_body(n, x_ref, high_ref, low_ref):
    wide = x_ref.shape[1] * x_ref.shape[0] // n
    each = n // x_ref.shape[0]
    for p in range(wide):
        parts = [x_ref[c, p * each : (p + 1) * each, :] for c in range(x_ref.shape[0])]
        rows = slice(p * n, (p + 1) * n)
        high_ref[rows, :], low_ref[rows, :] = halves(jnp.concatenate(parts, axis=0))


def take(ref, rows, batch):
    parts = [ref[t, rows, : min(128, batch - 128 * t)] for t in range(ref.shape[0])]
    return jnp.concatenate(parts, axis=1) if len(parts) > 1 else parts[0]


def put(ref, rows, value):
    for t in range(ref.shape[0]):
        part = value[:, 128 * t : 128 * (t + 1)]
        ref[t, rows, : part.shape[1]] = part


def apply_operator(
    n, keep, scale, field, target, high_ref, low_ref, weights_ref, major_ref, minor_ref, xp, zp
):
    blocks, batch, width = field.shape

    def span(r):
        return pl.ds(pl.multiple_of(r * width, 16), width)

    def project(r, total):
        x = field[r]
        put(xp, span(r), x.T)
        return total + dot3(halves(x), (high_ref[span(r), :], low_ref[span(r), :]))

    total = jnp.zeros((batch, high_ref.shape[1]), f32)
    total = lax.fori_loop(0, blocks, project, total)
    proj = halves((total * weights_ref[...]).T)

    group = 8 if n % 8 == 0 else 1

    def major(step, carry):
        for g in range(group):
            at = (pl.ds(step * group + g, n, stride=n), slice(None))
            parts = [xp[(t, *at)] for t in range(xp.shape[0])]
            x = jnp.concatenate(parts, axis=1) if len(parts) > 1 else parts[0]
            term = dot(major_ref[...], stacked(x))
            for t in range(xp.shape[0]):
                zp[(t, *at)] = term[:, 128 * t : 128 * (t + 1)]
        return carry

    lax.fori_loop(0, n // group, major, 0)

    def result(r, carry):
        total = dot3((high_ref[span(r), :], low_ref[span(r), :]), proj)
        minor = []
        for p in range(width // n):
            at = pl.ds(pl.multiple_of(r * width + p * n, 16), n)
            minor.append(dot(minor_ref[...], stacked(take(xp, at, batch))))
        total = total + jnp.concatenate(minor, axis=0) + take(zp, span(r), batch)
        if keep:
            target[r] = scale * total.T + keep * field[r]
        else:
            target[r] = scale * total.T
        return carry

    lax.fori_loop(0, blocks, result, 0)


def left_body(n, x_ref, *refs):
    *consts, out_ref, sent_ref, stage, xp, zp = refs
    for b in range(stage.shape[0]):
        stage[b] = unfold(x_ref.at[b], stage.shape[2])
    apply_operator(n, 0.0, 1.0, stage, out_ref, *consts, xp, zp)
    for b in range(stage.shape[0]):
        sent_ref[b] = fold(out_ref[b], sent_ref.shape[1:])


def left_again_body(n, spans, *refs):
    parts, (*consts, out_ref, stage, xp, zp) = refs[: len(spans)], refs[len(spans) :]
    for (start, stop), part in zip(spans, parts):
        stage[:, start:stop, :] = part[...]
    apply_operator(n, time_step, time_step * time_step / 2.0, stage, stage, *consts, xp, zp)
    for b in range(stage.shape[0]):
        out_ref[b] = fold(stage[b], out_ref.shape[1:])


def right_body(n, count, me_ref, *refs):
    ins, (*consts, out_ref, stage, xp, zp) = refs[:count], refs[count:]
    take_in(me_ref, ins, stage)
    apply_operator(
        n, time_step, time_step * time_step / 2.0, stage, out_ref, *consts, xp, zp
    )


def right_again_body(n, count, rows, spans, span, me_ref, base_ref, *refs):
    split = count * len(spans)
    ins, consts, outs = refs[:split], refs[split : split + 5], refs[split + 5 : split + 5 + count]
    stage, xp, zp, *arrived = refs[split + 5 + count :]
    for h, part in enumerate(arrived):
        take_in(me_ref, ins[h * count : (h + 1) * count], part)
    sizes = [stop - start for start, stop in spans]
    for b in range(count):
        parts = [
            part[b, span, r * size : (r + 1) * size]
            for r in range(rows)
            for part, size in zip(arrived, sizes)
        ]
        stage[b] = base_ref[b, span] + (time_step * time_step) * jnp.concatenate(parts, axis=1)
    apply_operator(n, 0.0, 1.0, stage, stage, *consts, xp, zp)
    hand_out(me_ref, stage, outs)


def tripled(matrix):
    high = lax.reduce_precision(matrix, 8, 7)
    low = matrix - high
    return jnp.concatenate([high, low, high], axis=1).astype(bf16)


def shift(parts, axis):
    n = len(parts)
    return [parts[0]] + [
        lax.ppermute(parts[s], axis, [(d, (d + s) % n) for d in range(n)]) for s in range(1, n)
    ]


def after(x, y):
    return lax.optimization_barrier((x, y))[0]


def exchange(x, axis):
    return lax.all_to_all(x, axis, split_axis=0, concat_axis=0, tiled=True)


def shards(rows, cols, pairs, one_body, aux, weights):
    n = one_body.shape[0]
    naux = aux.shape[2]
    local_rows, local_cols = pairs.shape
    size = local_rows * local_cols
    me = lax.axis_index("col").astype(jnp.int32).reshape(1)

    row_block = (rows, local_cols // rows, local_rows)
    col_block = (cols, local_rows // cols, local_cols)
    spans = halved(row_block[1])

    def row_wire(batch):
        return jax.ShapeDtypeStruct((rows, *wire(batch, local_rows)), f32)

    def col_wires(width):
        return [jax.ShapeDtypeStruct(wire(col_block[1], width), f32)] * cols

    row_stage, col_stage = pltpu.VMEM(row_block, f32), pltpu.VMEM(col_block, f32)

    crossed, *sent = call(
        functools.partial(cross_body, n, spans),
        [jax.ShapeDtypeStruct((local_cols, local_rows), f32)]
        + [row_wire(b - a) for a, b in spans],
        [pairs], moved=12 * size,
    )

    aux = after(aux, sent)
    whole = lax.all_gather(aux.reshape(-1, naux), "row", axis=0, tiled=True)
    mine = []
    for part in sent:
        mine.append(exchange(after(part, mine) if mine else part, "row"))
    turned = call(turn_body, col_wires(local_cols), [me, crossed], [col_stage], moved=8 * size)
    theirs = shift(turned, "col")
    whole = lax.all_gather(after(whole, theirs), "col", axis=0, tiled=False)
    group = 8 if n % 8 == 0 else n
    shape = jax.ShapeDtypeStruct((n * n, naux), bf16)
    high, low = pl.pallas_call(
        functools.partial(split_body, n),
        grid=(n // group,),
        in_specs=[pl.BlockSpec((cols, group * n // cols, naux), lambda s: (0, s, 0))],
        out_specs=[pl.BlockSpec((group * n, naux), lambda s: (s, 0))] * 2,
        out_shape=[shape, shape],
        compiler_params=pltpu.CompilerParams(vmem_limit_bytes=vmem_limit),
        cost_estimate=pl.CostEstimate(
            flops=2 * n * n * naux, bytes_accessed=8 * n * n * naux, transcendentals=0
        ),
    )(whole)

    left = tripled(one_body)
    right = tripled(-one_body.T)
    gain = weights.reshape(1, naux)

    def operator(body, arrays, consts, outs, block, scratch=()):
        batch = block[1]
        work = pltpu.VMEM((-(-batch // 128), n * n, 128), f32)
        return call(
            functools.partial(body, n),
            outs,
            [*arrays, high, low, *consts],
            [pltpu.VMEM(block, f32), work, work, *scratch],
            flops=12 * n * n * (naux + n) * batch,
            moved=4 * n * n * naux + 12 * size,
        )

    row_consts = [gain, left, right]
    col_consts = [-gain, right, left]

    first, parts = [], []
    for (start, stop), part in zip(spans, mine):
        block = (rows, stop - start, local_rows)
        outs = [jax.ShapeDtypeStruct(block, f32), row_wire(stop - start)]
        result, leaving = operator(
            left_body, [after(part, parts) if parts else part], row_consts, outs, block
        )
        first.append(result)
        parts.append(leaving)
    base = operator(
        lambda n, *refs: right_body(n, cols, *refs),
        [me, *after(theirs, parts)], col_consts, jax.ShapeDtypeStruct(col_block, f32), col_block,
    )
    arriving = []
    for h, (start, stop) in enumerate(spans):
        part = exchange(after(parts[h], (part, base)) if h else parts[h], "row")
        if h + 1 == len(spans):
            double = operator(
                lambda n, *refs: left_again_body(n, spans, *refs),
                after(first, turned) if h else first, row_consts, row_wire(row_block[1]), row_block,
            )
            part, double = after(part, (arriving, double)), after(double, (part, arriving))
        turned = call(
            turn_arriving_body, col_wires(rows * (stop - start)), [me, part],
            [
                pltpu.VMEM((rows, stop - start, local_rows), f32),
                pltpu.VMEM((*col_block[:2], rows * (stop - start)), f32),
            ],
            moved=8 * size // len(spans),
        )
        arriving += shift(turned, "col")
    double = exchange(double, "row")
    last, stages = [], []
    for start, stop in [(0, col_block[1])]:
        block = (cols, stop - start, local_cols)
        outs = operator(
            lambda n, *refs: right_again_body(n, cols, rows, spans, slice(start, stop), *refs),
            [me, base, *arriving], col_consts,
            [jax.ShapeDtypeStruct(wire(stop - start, local_cols), f32)] * cols, block,
            [pltpu.VMEM((*col_block[:2], rows * (b - a)), f32) for a, b in spans],
        )
        last += shift(outs, "col")
        stages.append(pltpu.VMEM(block, f32))

    return call(
        functools.partial(finish_body, n, len(stages)),
        jax.ShapeDtypeStruct(pairs.shape, f32),
        [me, pairs, double, *last],
        [*stages, row_stage, pltpu.VMEM((local_cols, local_rows), f32)],
        moved=16 * size,
    )


def solution(mesh):
    body = functools.partial(shards, mesh.shape["row"], mesh.shape["col"])
    in_specs = (P("row", "col"), P(), P("row", "col", None), P())
    return jax.shard_map(
        body, mesh=mesh, in_specs=in_specs, out_specs=P("row", "col"), check_vma=False
    )
```

```python
import functools

import jax
import jax.numpy as jnp
from jax import lax
from jax.experimental import pallas as pl
from jax.experimental.pallas import tpu as pltpu
from jax.sharding import PartitionSpec as P

time_step = 0.15
vmem_limit = 60 * 1024 * 1024
f32, bf16 = jnp.float32, jnp.bfloat16


def halves(x):
    high = x.astype(bf16)
    return high, (x - high.astype(f32)).astype(bf16)


def dot(a, b):
    return lax.dot_general(a, b, (((1,), (0,)), ((), ())), preferred_element_type=f32)


def dot3(a, b):
    return dot(a[0], b[0]) + dot(a[0], b[1]) + dot(a[1], b[0])


def stacked(x):
    high, low = halves(x)
    return jnp.concatenate([high, high, low], axis=0)


def call(body, out_shape, operands, scratch=(), flops=0, moved=0):
    vmem, smem = pl.BlockSpec(memory_space=pltpu.VMEM), pl.BlockSpec(memory_space=pltpu.SMEM)
    return pl.pallas_call(
        body,
        in_specs=[smem if x.dtype == jnp.int32 else vmem for x in operands],
        out_specs=jax.tree.map(lambda _: vmem, out_shape),
        out_shape=out_shape,
        scratch_shapes=list(scratch),
        compiler_params=pltpu.CompilerParams(vmem_limit_bytes=vmem_limit),
        cost_estimate=pl.CostEstimate(flops=flops, bytes_accessed=moved, transcendentals=0),
    )(*operands)


def tiles(total, size=128):
    return [slice(start, min(start + size, total)) for start in range(0, total, size)]


def folded(batch, width):
    def cost(g):
        return -(-batch // g // 8) * -(-g * width // 128)

    return min([g for g in range(1, batch + 1) if g == 1 or batch % (8 * g) == 0], key=cost)


def wire(batch, width):
    g = folded(batch, width)
    return (batch // g, g * width)


def fold(block, shape):
    rows, g = shape[0], shape[1] // block.shape[1]
    parts = [block[h * rows : (h + 1) * rows, :] for h in range(g)]
    return jnp.concatenate(parts, axis=1) if g > 1 else block


def unfold(in_ref, width):
    parts = [in_ref[:, h * width : (h + 1) * width] for h in range(in_ref.shape[1] // width)]
    return jnp.concatenate(parts, axis=0) if len(parts) > 1 else parts[0]


def halved(batch):
    cut = -(-batch * 16 // 25 // 8) * 8
    return [(0, cut), (cut, batch)] if cut < batch else [(0, batch)]


def hand_out(me_ref, stage, outs):
    for s, out_ref in enumerate(outs):
        out_ref[...] = fold(stage[lax.rem(me_ref[0] + s, len(outs))], out_ref.shape)


def take_in(me_ref, ins, stage):
    for s, in_ref in enumerate(ins):
        stage[lax.rem(me_ref[0] + len(ins) - s, len(ins))] = unfold(in_ref, stage.shape[2])


def rows_of(stage, span):
    batch = stage.shape[1]
    parts = []
    for b in range(span.start // batch, -(-span.stop // batch)):
        low, high = max(span.start - b * batch, 0), min(span.stop - b * batch, batch)
        parts.append(stage[b, low:high, :])
    return jnp.concatenate(parts, axis=0) if len(parts) > 1 else parts[0]


def cross_body(n, spans, x_ref, crossed_ref, *outs):
    rows = tiles(x_ref.shape[0], n)
    for k in tiles(x_ref.shape[1], n):
        crossed_ref[k, :] = jnp.concatenate([x_ref[i, k] for i in rows], axis=1)
    count = outs[0].shape[0]
    batch = crossed_ref.shape[0] // count
    for b in range(count):
        for (start, stop), out_ref in zip(spans, outs):
            block = crossed_ref[b * batch + start : b * batch + stop, :]
            out_ref[b] = fold(block, out_ref.shape[1:])


def turn_body(me_ref, x_ref, *refs):
    *outs, stage = refs
    turn_rows(lambda strip: x_ref[strip, :], x_ref.shape[0], stage)
    hand_out(me_ref, stage, outs)


def turn_rows(rows, total, stage):
    count, batch, _ = stage.shape
    for strip in tiles(total):
        turned = rows(strip).T
        for b in range(count):
            stage[b, :, strip] = turned[b * batch : (b + 1) * batch]


def turn_arriving_body(me_ref, x_ref, *refs):
    *outs, arrived, stage = refs
    for b in range(arrived.shape[0]):
        arrived[b] = unfold(x_ref.at[b], arrived.shape[2])
    turn_rows(lambda strip: rows_of(arrived, strip), arrived.shape[0] * arrived.shape[1], stage)
    hand_out(me_ref, stage, outs)


def finish_body(n, parts, me_ref, x_ref, crossed_ref, *refs):
    stages, (arrived, total) = refs[-2 - parts : -2], refs[-2:]
    *ins, out_ref = refs[: -2 - parts]
    for b in range(arrived.shape[0]):
        arrived[b] = unfold(crossed_ref.at[b], arrived.shape[2])
    count = len(ins) // parts
    for h, stage in enumerate(stages):
        take_in(me_ref, ins[h * count : (h + 1) * count], stage)
    for strip in tiles(total.shape[0]):
        turned = [stage[b, :, strip] for b in range(count) for stage in stages]
        total[strip, :] = rows_of(arrived, strip) + jnp.concatenate(turned, axis=0).T
    cols = tiles(x_ref.shape[1], n)
    for i in tiles(x_ref.shape[0], n):
        out_ref[i, :] = x_ref[i, :] + jnp.concatenate([total[k, i] for k in cols], axis=1)


def split_body(n, x_ref, high_ref, low_ref):
    wide = x_ref.shape[1] * x_ref.shape[0] // n
    each = n // x_ref.shape[0]
    for p in range(wide):
        parts = [x_ref[c, p * each : (p + 1) * each, :] for c in range(x_ref.shape[0])]
        rows = slice(p * n, (p + 1) * n)
        high_ref[rows, :], low_ref[rows, :] = halves(jnp.concatenate(parts, axis=0))


def take(ref, rows, batch):
    parts = [ref[t, rows, : min(128, batch - 128 * t)] for t in range(ref.shape[0])]
    return jnp.concatenate(parts, axis=1) if len(parts) > 1 else parts[0]


def put(ref, rows, value):
    for t in range(ref.shape[0]):
        part = value[:, 128 * t : 128 * (t + 1)]
        ref[t, rows, : part.shape[1]] = part


def apply_operator(
    n, keep, scale, field, target, high_ref, low_ref, weights_ref, major_ref, minor_ref, xp, zp
):
    blocks, batch, width = field.shape

    def span(r):
        return pl.ds(pl.multiple_of(r * width, 16), width)

    def project(r, total):
        x = field[r]
        put(xp, span(r), x.T)
        return total + dot3(halves(x), (high_ref[span(r), :], low_ref[span(r), :]))

    total = jnp.zeros((batch, high_ref.shape[1]), f32)
    total = lax.fori_loop(0, blocks, project, total)
    proj = halves((total * weights_ref[...]).T)

    group = 8 if n % 8 == 0 else 1

    def major(step, carry):
        for g in range(group):
            at = (pl.ds(step * group + g, n, stride=n), slice(None))
            parts = [xp[(t, *at)] for t in range(xp.shape[0])]
            x = jnp.concatenate(parts, axis=1) if len(parts) > 1 else parts[0]
            term = dot(major_ref[...], stacked(x))
            for t in range(xp.shape[0]):
                zp[(t, *at)] = term[:, 128 * t : 128 * (t + 1)]
        return carry

    lax.fori_loop(0, n // group, major, 0)

    def result(r, carry):
        total = dot3((high_ref[span(r), :], low_ref[span(r), :]), proj)
        minor = []
        for p in range(width // n):
            at = pl.ds(pl.multiple_of(r * width + p * n, 16), n)
            minor.append(dot(minor_ref[...], stacked(take(xp, at, batch))))
        total = total + jnp.concatenate(minor, axis=0) + take(zp, span(r), batch)
        if keep:
            target[r] = scale * total.T + keep * field[r]
        else:
            target[r] = scale * total.T
        return carry

    lax.fori_loop(0, blocks, result, 0)


def left_body(n, x_ref, *refs):
    *consts, out_ref, sent_ref, stage, xp, zp = refs
    for b in range(stage.shape[0]):
        stage[b] = unfold(x_ref.at[b], stage.shape[2])
    apply_operator(n, 0.0, 1.0, stage, out_ref, *consts, xp, zp)
    for b in range(stage.shape[0]):
        sent_ref[b] = fold(out_ref[b], sent_ref.shape[1:])


def left_again_body(n, spans, *refs):
    parts, (*consts, out_ref, stage, xp, zp) = refs[: len(spans)], refs[len(spans) :]
    for (start, stop), part in zip(spans, parts):
        stage[:, start:stop, :] = part[...]
    apply_operator(n, time_step, time_step * time_step / 2.0, stage, stage, *consts, xp, zp)
    for b in range(stage.shape[0]):
        out_ref[b] = fold(stage[b], out_ref.shape[1:])


def right_body(n, count, me_ref, *refs):
    ins, (*consts, out_ref, stage, xp, zp) = refs[:count], refs[count:]
    take_in(me_ref, ins, stage)
    apply_operator(
        n, time_step, time_step * time_step / 2.0, stage, out_ref, *consts, xp, zp
    )


def right_again_body(n, count, rows, spans, span, me_ref, base_ref, *refs):
    split = count * len(spans)
    ins, consts, outs = refs[:split], refs[split : split + 5], refs[split + 5 : split + 5 + count]
    stage, xp, zp, *arrived = refs[split + 5 + count :]
    for h, part in enumerate(arrived):
        take_in(me_ref, ins[h * count : (h + 1) * count], part)
    sizes = [stop - start for start, stop in spans]
    for b in range(count):
        parts = [
            part[b, span, r * size : (r + 1) * size]
            for r in range(rows)
            for part, size in zip(arrived, sizes)
        ]
        stage[b] = base_ref[b, span] + (time_step * time_step) * jnp.concatenate(parts, axis=1)
    apply_operator(n, 0.0, 1.0, stage, stage, *consts, xp, zp)
    hand_out(me_ref, stage, outs)


def tripled(matrix):
    high = lax.reduce_precision(matrix, 8, 7)
    low = matrix - high
    return jnp.concatenate([high, low, high], axis=1).astype(bf16)


def shift(parts, axis):
    n = len(parts)
    return [parts[0]] + [
        lax.ppermute(parts[s], axis, [(d, (d + s) % n) for d in range(n)]) for s in range(1, n)
    ]


def after(x, y):
    return lax.optimization_barrier((x, y))[0]


def exchange(x, axis):
    return lax.all_to_all(x, axis, split_axis=0, concat_axis=0, tiled=True)


def shards(rows, cols, pairs, one_body, aux, weights):
    n = one_body.shape[0]
    naux = aux.shape[2]
    local_rows, local_cols = pairs.shape
    size = local_rows * local_cols
    me = lax.axis_index("col").astype(jnp.int32).reshape(1)

    row_block = (rows, local_cols // rows, local_rows)
    col_block = (cols, local_rows // cols, local_cols)
    spans = halved(row_block[1])

    def row_wire(batch):
        return jax.ShapeDtypeStruct((rows, *wire(batch, local_rows)), f32)

    def col_wires(width):
        return [jax.ShapeDtypeStruct(wire(col_block[1], width), f32)] * cols

    row_stage, col_stage = pltpu.VMEM(row_block, f32), pltpu.VMEM(col_block, f32)

    crossed, *sent = call(
        functools.partial(cross_body, n, spans),
        [jax.ShapeDtypeStruct((local_cols, local_rows), f32)]
        + [row_wire(b - a) for a, b in spans],
        [pairs], moved=12 * size,
    )

    whole = lax.all_gather(aux.reshape(-1, naux), "row", axis=0, tiled=True)
    mine = []
    for part in sent:
        mine.append(exchange(after(part, mine) if mine else part, "row"))
    turned = call(turn_body, col_wires(local_cols), [me, crossed], [col_stage], moved=8 * size)
    theirs = shift(turned, "col")
    whole = lax.all_gather(after(whole, theirs[:-1]), "col", axis=0, tiled=False)
    group = 8 if n % 8 == 0 else n
    shape = jax.ShapeDtypeStruct((n * n, naux), bf16)
    high, low = pl.pallas_call(
        functools.partial(split_body, n),
        grid=(n // group,),
        in_specs=[pl.BlockSpec((cols, group * n // cols, naux), lambda s: (0, s, 0))],
        out_specs=[pl.BlockSpec((group * n, naux), lambda s: (s, 0))] * 2,
        out_shape=[shape, shape],
        compiler_params=pltpu.CompilerParams(vmem_limit_bytes=vmem_limit),
        cost_estimate=pl.CostEstimate(
            flops=2 * n * n * naux, bytes_accessed=8 * n * n * naux, transcendentals=0
        ),
    )(whole)

    left = tripled(one_body)
    right = tripled(-one_body.T)
    gain = weights.reshape(1, naux)

    def operator(body, arrays, consts, outs, block, scratch=()):
        batch = block[1]
        work = pltpu.VMEM((-(-batch // 128), n * n, 128), f32)
        return call(
            functools.partial(body, n),
            outs,
            [*arrays, high, low, *consts],
            [pltpu.VMEM(block, f32), work, work, *scratch],
            flops=12 * n * n * (naux + n) * batch,
            moved=4 * n * n * naux + 12 * size,
        )

    row_consts = [gain, left, right]
    col_consts = [-gain, right, left]

    first, parts = [], []
    for (start, stop), part in zip(spans, mine):
        block = (rows, stop - start, local_rows)
        outs = [jax.ShapeDtypeStruct(block, f32), row_wire(stop - start)]
        result, leaving = operator(
            left_body, [after(part, parts) if parts else part], row_consts, outs, block
        )
        first.append(result)
        parts.append(leaving)
    base = operator(
        lambda n, *refs: right_body(n, cols, *refs),
        [me, *after(theirs, parts)], col_consts, jax.ShapeDtypeStruct(col_block, f32), col_block,
    )
    arriving = []
    for h, (start, stop) in enumerate(spans):
        part = exchange(after(parts[h], (part, base)) if h else parts[h], "row")
        if h + 1 == len(spans):
            double = operator(
                lambda n, *refs: left_again_body(n, spans, *refs),
                after(first, turned) if h else first, row_consts, row_wire(row_block[1]), row_block,
            )
            part, double = after(part, (arriving, double)), after(double, (part, arriving))
        turned = call(
            turn_arriving_body, col_wires(rows * (stop - start)), [me, part],
            [
                pltpu.VMEM((rows, stop - start, local_rows), f32),
                pltpu.VMEM((*col_block[:2], rows * (stop - start)), f32),
            ],
            moved=8 * size // len(spans),
        )
        arriving += shift(turned, "col")
    double = exchange(double, "row")
    last, stages = [], []
    for start, stop in [(0, col_block[1])]:
        block = (cols, stop - start, local_cols)
        outs = operator(
            lambda n, *refs: right_again_body(n, cols, rows, spans, slice(start, stop), *refs),
            [me, base, *arriving], col_consts,
            [jax.ShapeDtypeStruct(wire(stop - start, local_cols), f32)] * cols, block,
            [pltpu.VMEM((*col_block[:2], rows * (b - a)), f32) for a, b in spans],
        )
        last += shift(outs, "col")
        stages.append(pltpu.VMEM(block, f32))

    return call(
        functools.partial(finish_body, n, len(stages)),
        jax.ShapeDtypeStruct(pairs.shape, f32),
        [me, pairs, double, *last],
        [*stages, row_stage, pltpu.VMEM((local_cols, local_rows), f32)],
        moved=16 * size,
    )


def solution(mesh):
    body = functools.partial(shards, mesh.shape["row"], mesh.shape["col"])
    in_specs = (P("row", "col"), P(), P("row", "col", None), P())
    return jax.shard_map(
        body, mesh=mesh, in_specs=in_specs, out_specs=P("row", "col"), check_vma=False
    )
```

```python
import functools

import jax
import jax.numpy as jnp
from jax import lax
from jax.experimental import pallas as pl
from jax.experimental.pallas import tpu as pltpu
from jax.sharding import PartitionSpec as P

time_step = 0.15
vmem_limit = 60 * 1024 * 1024
f32, bf16 = jnp.float32, jnp.bfloat16


def halves(x):
    high = x.astype(bf16)
    return high, (x - high.astype(f32)).astype(bf16)


def dot(a, b):
    return lax.dot_general(a, b, (((1,), (0,)), ((), ())), preferred_element_type=f32)


def dot3(a, b):
    return dot(a[0], b[0]) + dot(a[0], b[1]) + dot(a[1], b[0])


def stacked(x):
    high, low = halves(x)
    return jnp.concatenate([high, high, low], axis=0)


def call(body, out_shape, operands, scratch=(), flops=0, moved=0):
    vmem, smem = pl.BlockSpec(memory_space=pltpu.VMEM), pl.BlockSpec(memory_space=pltpu.SMEM)
    return pl.pallas_call(
        body,
        in_specs=[smem if x.dtype == jnp.int32 else vmem for x in operands],
        out_specs=jax.tree.map(lambda _: vmem, out_shape),
        out_shape=out_shape,
        scratch_shapes=list(scratch),
        compiler_params=pltpu.CompilerParams(vmem_limit_bytes=vmem_limit),
        cost_estimate=pl.CostEstimate(flops=flops, bytes_accessed=moved, transcendentals=0),
    )(*operands)


def tiles(total, size=128):
    return [slice(start, min(start + size, total)) for start in range(0, total, size)]


def folded(batch, width):
    def cost(g):
        return -(-batch // g // 8) * -(-g * width // 128)

    return min([g for g in range(1, batch + 1) if g == 1 or batch % (8 * g) == 0], key=cost)


def wire(batch, width):
    g = folded(batch, width)
    return (batch // g, g * width)


def fold(block, shape):
    rows, g = shape[0], shape[1] // block.shape[1]
    parts = [block[h * rows : (h + 1) * rows, :] for h in range(g)]
    return jnp.concatenate(parts, axis=1) if g > 1 else block


def unfold(in_ref, width):
    parts = [in_ref[:, h * width : (h + 1) * width] for h in range(in_ref.shape[1] // width)]
    return jnp.concatenate(parts, axis=0) if len(parts) > 1 else parts[0]


def halved(batch):
    cut = -(-batch * 16 // 25 // 8) * 8
    return [(0, cut), (cut, batch)] if cut < batch else [(0, batch)]


def hand_out(me_ref, stage, outs):
    for s, out_ref in enumerate(outs):
        out_ref[...] = fold(stage[lax.rem(me_ref[0] + s, len(outs))], out_ref.shape)


def take_in(me_ref, ins, stage):
    for s, in_ref in enumerate(ins):
        stage[lax.rem(me_ref[0] + len(ins) - s, len(ins))] = unfold(in_ref, stage.shape[2])


def rows_of(stage, span):
    batch = stage.shape[1]
    parts = []
    for b in range(span.start // batch, -(-span.stop // batch)):
        low, high = max(span.start - b * batch, 0), min(span.stop - b * batch, batch)
        parts.append(stage[b, low:high, :])
    return jnp.concatenate(parts, axis=0) if len(parts) > 1 else parts[0]


def cross_body(n, spans, x_ref, crossed_ref, *outs):
    rows = tiles(x_ref.shape[0], n)
    for k in tiles(x_ref.shape[1], n):
        crossed_ref[k, :] = jnp.concatenate([x_ref[i, k] for i in rows], axis=1)
    count = outs[0].shape[0]
    batch = crossed_ref.shape[0] // count
    for b in range(count):
        for (start, stop), out_ref in zip(spans, outs):
            block = crossed_ref[b * batch + start : b * batch + stop, :]
            out_ref[b] = fold(block, out_ref.shape[1:])


def turn_body(me_ref, x_ref, *refs):
    *outs, stage = refs
    turn_rows(lambda strip: x_ref[strip, :], x_ref.shape[0], stage)
    hand_out(me_ref, stage, outs)


def turn_rows(rows, total, stage):
    count, batch, _ = stage.shape
    for strip in tiles(total):
        turned = rows(strip).T
        for b in range(count):
            stage[b, :, strip] = turned[b * batch : (b + 1) * batch]


def turn_arriving_body(me_ref, x_ref, *refs):
    *outs, arrived, stage = refs
    for b in range(arrived.shape[0]):
        arrived[b] = unfold(x_ref.at[b], arrived.shape[2])
    turn_rows(lambda strip: rows_of(arrived, strip), arrived.shape[0] * arrived.shape[1], stage)
    hand_out(me_ref, stage, outs)


def finish_body(n, parts, me_ref, x_ref, crossed_ref, *refs):
    stages, (arrived, total) = refs[-2 - parts : -2], refs[-2:]
    *ins, out_ref = refs[: -2 - parts]
    for b in range(arrived.shape[0]):
        arrived[b] = unfold(crossed_ref.at[b], arrived.shape[2])
    count = len(ins) // parts
    for h, stage in enumerate(stages):
        take_in(me_ref, ins[h * count : (h + 1) * count], stage)
    for strip in tiles(total.shape[0]):
        turned = [stage[b, :, strip] for b in range(count) for stage in stages]
        total[strip, :] = rows_of(arrived, strip) + jnp.concatenate(turned, axis=0).T
    cols = tiles(x_ref.shape[1], n)
    for i in tiles(x_ref.shape[0], n):
        out_ref[i, :] = x_ref[i, :] + jnp.concatenate([total[k, i] for k in cols], axis=1)


def split_body(n, x_ref, high_ref, low_ref):
    wide = x_ref.shape[1] * x_ref.shape[0] // n
    each = n // x_ref.shape[0]
    for p in range(wide):
        parts = [x_ref[c, p * each : (p + 1) * each, :] for c in range(x_ref.shape[0])]
        rows = slice(p * n, (p + 1) * n)
        high_ref[rows, :], low_ref[rows, :] = halves(jnp.concatenate(parts, axis=0))


def take(ref, rows, batch):
    parts = [ref[t, rows, : min(128, batch - 128 * t)] for t in range(ref.shape[0])]
    return jnp.concatenate(parts, axis=1) if len(parts) > 1 else parts[0]


def put(ref, rows, value):
    for t in range(ref.shape[0]):
        part = value[:, 128 * t : 128 * (t + 1)]
        ref[t, rows, : part.shape[1]] = part


def apply_operator(
    n, keep, scale, field, target, high_ref, low_ref, weights_ref, major_ref, minor_ref, xp, zp
):
    blocks, batch, width = field.shape

    def span(r):
        return pl.ds(pl.multiple_of(r * width, 16), width)

    def project(r, total):
        x = field[r]
        put(xp, span(r), x.T)
        return total + dot3(halves(x), (high_ref[span(r), :], low_ref[span(r), :]))

    total = jnp.zeros((batch, high_ref.shape[1]), f32)
    total = lax.fori_loop(0, blocks, project, total)
    proj = halves((total * weights_ref[...]).T)

    group = 8 if n % 8 == 0 else 1

    def major(step, carry):
        for g in range(group):
            at = (pl.ds(step * group + g, n, stride=n), slice(None))
            parts = [xp[(t, *at)] for t in range(xp.shape[0])]
            x = jnp.concatenate(parts, axis=1) if len(parts) > 1 else parts[0]
            term = dot(major_ref[...], stacked(x))
            for t in range(xp.shape[0]):
                zp[(t, *at)] = term[:, 128 * t : 128 * (t + 1)]
        return carry

    lax.fori_loop(0, n // group, major, 0)

    def result(r, carry):
        total = dot3((high_ref[span(r), :], low_ref[span(r), :]), proj)
        minor = []
        for p in range(width // n):
            at = pl.ds(pl.multiple_of(r * width + p * n, 16), n)
            minor.append(dot(minor_ref[...], stacked(take(xp, at, batch))))
        total = total + jnp.concatenate(minor, axis=0) + take(zp, span(r), batch)
        if keep:
            target[r] = scale * total.T + keep * field[r]
        else:
            target[r] = scale * total.T
        return carry

    lax.fori_loop(0, blocks, result, 0)


def left_body(n, x_ref, *refs):
    *consts, out_ref, sent_ref, stage, xp, zp = refs
    for b in range(stage.shape[0]):
        stage[b] = unfold(x_ref.at[b], stage.shape[2])
    apply_operator(n, 0.0, 1.0, stage, out_ref, *consts, xp, zp)
    for b in range(stage.shape[0]):
        sent_ref[b] = fold(out_ref[b], sent_ref.shape[1:])


def left_again_body(n, spans, *refs):
    parts, (*consts, out_ref, stage, xp, zp) = refs[: len(spans)], refs[len(spans) :]
    for (start, stop), part in zip(spans, parts):
        stage[:, start:stop, :] = part[...]
    apply_operator(n, time_step, time_step * time_step / 2.0, stage, stage, *consts, xp, zp)
    for b in range(stage.shape[0]):
        out_ref[b] = fold(stage[b], out_ref.shape[1:])


def right_body(n, count, me_ref, *refs):
    ins, (*consts, out_ref, stage, xp, zp) = refs[:count], refs[count:]
    take_in(me_ref, ins, stage)
    apply_operator(
        n, time_step, time_step * time_step / 2.0, stage, out_ref, *consts, xp, zp
    )


def right_again_body(n, count, rows, spans, span, me_ref, base_ref, *refs):
    split = count * len(spans)
    ins, consts, outs = refs[:split], refs[split : split + 5], refs[split + 5 : split + 5 + count]
    stage, xp, zp, *arrived = refs[split + 5 + count :]
    for h, part in enumerate(arrived):
        take_in(me_ref, ins[h * count : (h + 1) * count], part)
    sizes = [stop - start for start, stop in spans]
    for b in range(count):
        parts = [
            part[b, span, r * size : (r + 1) * size]
            for r in range(rows)
            for part, size in zip(arrived, sizes)
        ]
        stage[b] = base_ref[b, span] + (time_step * time_step) * jnp.concatenate(parts, axis=1)
    apply_operator(n, 0.0, 1.0, stage, stage, *consts, xp, zp)
    hand_out(me_ref, stage, outs)


def tripled(matrix):
    high = lax.reduce_precision(matrix, 8, 7)
    low = matrix - high
    return jnp.concatenate([high, low, high], axis=1).astype(bf16)


def shift(parts, axis):
    n = len(parts)
    return [parts[0]] + [
        lax.ppermute(parts[s], axis, [(d, (d + s) % n) for d in range(n)]) for s in range(1, n)
    ]


def after(x, y):
    return lax.optimization_barrier((x, y))[0]


def exchange(x, axis):
    return lax.all_to_all(x, axis, split_axis=0, concat_axis=0, tiled=True)


def shards(rows, cols, pairs, one_body, aux, weights):
    n = one_body.shape[0]
    naux = aux.shape[2]
    local_rows, local_cols = pairs.shape
    size = local_rows * local_cols
    me = lax.axis_index("col").astype(jnp.int32).reshape(1)

    row_block = (rows, local_cols // rows, local_rows)
    col_block = (cols, local_rows // cols, local_cols)
    spans = halved(row_block[1])

    def row_wire(batch):
        return jax.ShapeDtypeStruct((rows, *wire(batch, local_rows)), f32)

    def col_wires(width):
        return [jax.ShapeDtypeStruct(wire(col_block[1], width), f32)] * cols

    row_stage, col_stage = pltpu.VMEM(row_block, f32), pltpu.VMEM(col_block, f32)

    crossed, *sent = call(
        functools.partial(cross_body, n, spans),
        [jax.ShapeDtypeStruct((local_cols, local_rows), f32)]
        + [row_wire(b - a) for a, b in spans],
        [pairs], moved=12 * size,
    )

    whole = lax.all_gather(aux.reshape(-1, naux), "row", axis=0, tiled=True)
    mine = []
    for part in sent:
        mine.append(exchange(after(part, mine) if mine else part, "row"))
    turned = call(turn_body, col_wires(local_cols), [me, crossed], [col_stage], moved=8 * size)
    theirs = shift(turned, "col")
    whole = lax.all_gather(after(whole, theirs[:-1]), "col", axis=0, tiled=False)
    group = 16 if n % 16 == 0 else n
    shape = jax.ShapeDtypeStruct((n * n, naux), bf16)
    high, low = pl.pallas_call(
        functools.partial(split_body, n),
        grid=(n // group,),
        in_specs=[pl.BlockSpec((cols, group * n // cols, naux), lambda s: (0, s, 0))],
        out_specs=[pl.BlockSpec((group * n, naux), lambda s: (s, 0))] * 2,
        out_shape=[shape, shape],
        compiler_params=pltpu.CompilerParams(vmem_limit_bytes=vmem_limit),
        cost_estimate=pl.CostEstimate(
            flops=2 * n * n * naux, bytes_accessed=8 * n * n * naux, transcendentals=0
        ),
    )(whole)

    left = tripled(one_body)
    right = tripled(-one_body.T)
    gain = weights.reshape(1, naux)

    def operator(body, arrays, consts, outs, block, scratch=()):
        batch = block[1]
        work = pltpu.VMEM((-(-batch // 128), n * n, 128), f32)
        return call(
            functools.partial(body, n),
            outs,
            [*arrays, high, low, *consts],
            [pltpu.VMEM(block, f32), work, work, *scratch],
            flops=12 * n * n * (naux + n) * batch,
            moved=4 * n * n * naux + 12 * size,
        )

    row_consts = [gain, left, right]
    col_consts = [-gain, right, left]

    first, parts = [], []
    for (start, stop), part in zip(spans, mine):
        block = (rows, stop - start, local_rows)
        outs = [jax.ShapeDtypeStruct(block, f32), row_wire(stop - start)]
        result, leaving = operator(
            left_body, [after(part, parts) if parts else part], row_consts, outs, block
        )
        first.append(result)
        parts.append(leaving)
    base = operator(
        lambda n, *refs: right_body(n, cols, *refs),
        [me, *after(theirs, parts)], col_consts, jax.ShapeDtypeStruct(col_block, f32), col_block,
    )
    arriving = []
    for h, (start, stop) in enumerate(spans):
        part = exchange(after(parts[h], (part, base)) if h else parts[h], "row")
        if h + 1 == len(spans):
            double = operator(
                lambda n, *refs: left_again_body(n, spans, *refs),
                after(first, turned) if h else first, row_consts, row_wire(row_block[1]), row_block,
            )
            part, double = after(part, (arriving, double)), after(double, (part, arriving))
        turned = call(
            turn_arriving_body, col_wires(rows * (stop - start)), [me, part],
            [
                pltpu.VMEM((rows, stop - start, local_rows), f32),
                pltpu.VMEM((*col_block[:2], rows * (stop - start)), f32),
            ],
            moved=8 * size // len(spans),
        )
        arriving += shift(turned, "col")
    double = exchange(double, "row")
    last, stages = [], []
    for start, stop in [(0, col_block[1])]:
        block = (cols, stop - start, local_cols)
        outs = operator(
            lambda n, *refs: right_again_body(n, cols, rows, spans, slice(start, stop), *refs),
            [me, base, *arriving], col_consts,
            [jax.ShapeDtypeStruct(wire(stop - start, local_cols), f32)] * cols, block,
            [pltpu.VMEM((*col_block[:2], rows * (b - a)), f32) for a, b in spans],
        )
        last += shift(outs, "col")
        stages.append(pltpu.VMEM(block, f32))

    return call(
        functools.partial(finish_body, n, len(stages)),
        jax.ShapeDtypeStruct(pairs.shape, f32),
        [me, pairs, double, *last],
        [*stages, row_stage, pltpu.VMEM((local_cols, local_rows), f32)],
        moved=16 * size,
    )


def solution(mesh):
    body = functools.partial(shards, mesh.shape["row"], mesh.shape["col"])
    in_specs = (P("row", "col"), P(), P("row", "col", None), P())
    return jax.shard_map(
        body, mesh=mesh, in_specs=in_specs, out_specs=P("row", "col"), check_vma=False
    )
```
